32 devices in a mesh: dp: 8 (over y, x, core), seq: 4 (over z).
Axes of the slice: x: 2, y: 2, z: 4, core: 2. Of those that a mesh axis runs over, the one named last changes fastest.
Arguments:
- hidden_in: bfloat16 [16, 1024, 384], P('dp', 'seq'), may hold values from -6 to 6
- norm1_gain: float32 [2, 384], replicated, may hold values from 0.25 to 1.75
- qkv_weight: bfloat16 [2, 384, 1152], replicated, may hold values from -0.3125 to 0.3125
- out_weight: bfloat16 [2, 384, 384], replicated, may hold values from -1.75 to 1.75
- norm2_gain: float32 [2, 384], replicated, may hold values from 0.25 to 1.75
- fc_weight: bfloat16 [2, 384, 1536], replicated, may hold values from -0.3125 to 0.3125
- proj_weight: bfloat16 [2, 1536, 384], replicated, may hold values from -0.15625 to 0.15625
- prefix_len: int32 [16], P('dp'), may hold values from 1 to 1024, as said below
- block_order: int32 [8], replicated, may hold values from 0 to 7, each once
- grad_out: bfloat16 [16, 1024, 384], P('dp', 'seq'), may hold values from -6 to 6
Outputs:
- hidden_out: bfloat16 [16, 1024, 384], P('dp', 'seq')
- grad_in: bfloat16 [16, 1024, 384], P('dp', 'seq')
- norm1_grad: float32 [2, 384], replicated
- qkv_grad: float32 [2, 384, 1152], replicated
- out_grad: float32 [2, 384, 384], replicated
- norm2_grad: float32 [2, 384], replicated
- fc_grad: float32 [2, 384, 1536], replicated
- proj_grad: float32 [2, 1536, 384], replicated
The draws below stay inside these ranges and needn't reach their ends.
Inputs may be any that keep to these rules, and one draw needn't show every extreme that they name: Among the 2 rows of each index of dp, one row has prefix_len 1024 and the other has prefix_len 1. `block_order`: A permutation of the stored blocks.
All inputs are finite; a program needn't handle non-finite values.
Results may differ from the reference program's by a relative error of at most 0.03.
Values may be sent and summed in bfloat16 or wider, within the bound.
No kernel may reach another device: no remote copies, remote signals or barrier semaphores. Data moves between devices by JAX's collectives and lax.ppermute only.
A program may use at most 192 MiB of HBM per device.

```python
import math
import jax
import jax.numpy as jnp
from jax import lax

D = 384
HEADS = 6
HEAD = 64
FF = 1536
LAYERS = 2
ROW_LEN = 1024
ROWS_DEV = 2
BLOCKS = 8
ROWS = 16


def draw_prefix_len(key, part):
    key = jax.random.fold_in(key, 7)
    first, second = jax.random.split(key)
    groups = ROWS // ROWS_DEV
    lengths = jax.random.randint(first, (groups, ROWS_DEV), 1, ROW_LEN + 1)
    chosen = jax.random.randint(second, (groups, 1), 0, ROWS_DEV)
    places = jnp.arange(ROWS_DEV, dtype=jnp.int32)[None, :]
    lengths = jnp.where(places == chosen, ROW_LEN, lengths)
    lengths = jnp.where(places == (chosen + 1) % ROWS_DEV, 1, lengths)
    return lengths.reshape(ROWS).astype(jnp.int32)


def block_scale(own_key, dims, shards, smallest, top_value):
    factor_of, own = 1.0, jax.random.fold_in(own_key, 6)
    for dim, shards_of in shards:
        draws = jnp.exp(jax.random.uniform(jax.random.fold_in(own, dim), (shards_of,), jnp.float32, smallest / len(shards), top_value / len(shards)))
        factor_of = factor_of * jnp.repeat(draws, dims[dim] // shards_of).reshape([-1 if axis == dim else 1 for axis in range(len(dims))])
    return factor_of


def noise(own_key, shape, scale, bound, cuts=(), kind=jnp.bfloat16):
    entries = jax.random.normal(own_key, shape, jnp.float32) * scale
    if len(cuts) > 0:
        entries = block_scale(own_key, shape, cuts, -0.22, 0.18) * entries
    return jnp.clip(entries, min=-bound, max=bound).astype(kind)


def setup_inputs(seed: int = 0) -> dict:
    arg_keys = jax.random.split(jax.random.key(seed), 11)
    return {
        "hidden_in": noise(arg_keys[0], (ROWS, ROW_LEN, D), 1.0, 6.0, ((0, 8), (1, 4))),
        "norm1_gain": jnp.clip(1.0 + 0.15 * jax.random.normal(arg_keys[1], (LAYERS, D), jnp.float32), 0.25, 1.75),
        "qkv_weight": noise(arg_keys[2], (LAYERS, D, 3 * D), D ** -0.5, 0.3125),
        "out_weight": noise(arg_keys[3], (LAYERS, D, D), (max(D // 32, 1)) ** -0.5, 1.75),
        "norm2_gain": jnp.clip(1.0 + 0.15 * jax.random.normal(arg_keys[4], (LAYERS, D), jnp.float32), 0.25, 1.75),
        "fc_weight": noise(arg_keys[5], (LAYERS, D, FF), D ** -0.5, 0.3125),
        "proj_weight": noise(arg_keys[6], (LAYERS, FF, D), FF ** -0.5, 0.15625),
        "prefix_len": draw_prefix_len(jax.random.fold_in(arg_keys[10], 71), 0),
        "block_order": jax.random.permutation(arg_keys[8], BLOCKS).astype(jnp.int32),
        "grad_out": noise(arg_keys[9], (ROWS, ROW_LEN, D), 1.0, 6.0, ((0, 8), (1, 4))),
    }


EPSILON = 1e-05
NEGATIVE = -1e+30

@jax.custom_vjp
def low(v):
    return lax.optimization_barrier(v.astype(jnp.bfloat16)).astype(jnp.float32)

@jax.custom_vjp
def low_back(v):
    return v

def low_keep(v):
    return (low(v), None)

def low_pass(kept, grad):
    return (grad,)

def back_keep(v):
    return (v, None)

def back_low(kept, grad):
    return (low(grad),)
low.defvjp(low_keep, low_pass)
low_back.defvjp(back_keep, back_low)

def matmul(left, right):
    return jnp.dot(left, right, precision=lax.Precision.HIGHEST)

def normalize(values, gain):
    centre = lax.optimization_barrier(jnp.mean(values, axis=-1, keepdims=True))
    centred = values - centre
    spread = lax.optimization_barrier(jnp.mean(centred * centred, axis=-1, keepdims=True))
    return centred * lax.rsqrt(spread + EPSILON) * gain

def one_layer(hidden, params, visible):
    gain_one, w_qkv, w_out, gain_two, w_fc, w_proj = params
    length = hidden.shape[0]
    scale = 1.0 / math.sqrt(HEAD)
    normed = low(normalize(hidden, gain_one))
    packed = low_back(low(matmul(normed, w_qkv)))
    queries = packed[:, :D].reshape(length, HEADS, HEAD)
    keys = packed[:, D:2 * D].reshape(length, HEADS, HEAD)
    values = packed[:, 2 * D:].reshape(length, HEADS, HEAD)
    scores = low_back(jnp.einsum('ihd,jhd->hij', queries, keys, precision=lax.Precision.HIGHEST) * scale)
    masked = jnp.where(visible[None], scores, NEGATIVE)
    highest = lax.optimization_barrier(jnp.max(masked, axis=-1, keepdims=True))
    raised = jnp.exp(masked - highest)
    soft = low(raised / lax.optimization_barrier(jnp.sum(raised, axis=-1, keepdims=True)))
    attended = jnp.einsum('hij,jhd->ihd', soft, values, precision=lax.Precision.HIGHEST).reshape(length, D)
    attended = low_back(low(attended))
    middle = hidden + low_back(matmul(attended, w_out))
    second = low(normalize(middle, gain_two))
    lifted = low_back(matmul(second, w_fc))
    activated = low(jax.nn.gelu(lifted, approximate=False))
    return middle + low_back(matmul(activated, w_proj))

def reference(hidden_in, norm1_gain, qkv_weight, out_weight, norm2_gain, fc_weight, proj_weight, prefix_len, block_order, grad_out):
    weights = tuple((item.astype(jnp.float32) for item in (norm1_gain, qkv_weight, out_weight, norm2_gain, fc_weight, proj_weight)))
    block_size = ROW_LEN // BLOCKS
    stored = jnp.arange(ROW_LEN, dtype=jnp.int32)
    real = block_order[stored // block_size] * block_size + stored % block_size
    earlier = real[None, :] <= real[:, None]

    def row_step(totals, row):
        hidden, prefix, cotangent = row
        visible = earlier | (real[None, :] < prefix)

        def forward(state, params):
            for index in range(LAYERS):
                state = one_layer(state, tuple((item[index] for item in params)), visible)
            return state
        output, pull = jax.vjp(forward, hidden.astype(jnp.float32), weights)
        hidden_grad, param_grads = pull(cotangent.astype(jnp.float32))
        totals = tuple((total + grad for total, grad in zip(totals, param_grads)))
        return (totals, (output.astype(jnp.bfloat16), hidden_grad.astype(jnp.bfloat16)))
    zeros = tuple((jnp.zeros(item.shape, jnp.float32) for item in weights))
    totals, outputs = lax.scan(row_step, zeros, (hidden_in, prefix_len, grad_out))
    return (outputs[0], outputs[1], totals[0], totals[1], totals[2], totals[3], totals[4], totals[5])
```

```python
import functools
import math

import jax
import jax.numpy as jnp
from jax import lax
from jax.experimental import pallas as pl
from jax.experimental.pallas import tpu as pltpu
from jax.sharding import PartitionSpec as P

HEADS = 6
EPSILON = 1e-05
NEGATIVE = -1e30
BF = jnp.bfloat16
F32 = jnp.float32
ALL = ("dp", "seq")
LANES = 128
MB = 1024 * 1024
VMEM = pltpu.VMEM
SMEM = pltpu.SMEM


def mm(a, b):
    return lax.dot_general(a, b, (((1,), (0,)), ((), ())), preferred_element_type=F32)


def mm_t(a, b):
    return lax.dot_general(a, b, (((1,), (1,)), ((), ())), preferred_element_type=F32)


def t_mm(a, b):
    return lax.dot_general(a, b, (((0,), (0,)), ((), ())), preferred_element_type=F32)


def call(body, name, ins, outs, scratch=(), limit=40, flops=0, transcendentals=0, grid=(1,), aliases=None):
    moved = sum(math.prod(o[0]) * jnp.dtype(o[1]).itemsize for o in outs)
    moved += sum(a.size * a.dtype.itemsize for a, _ in ins)
    return pl.pallas_call(
        body,
        out_shape=[jax.ShapeDtypeStruct(s, d) for s, d, _ in outs],
        grid=grid,
        in_specs=[s for _, s in ins],
        out_specs=[s for _, _, s in outs],
        scratch_shapes=list(scratch),
        input_output_aliases=aliases or {},
        compiler_params=pltpu.CompilerParams(vmem_limit_bytes=limit * MB),
        cost_estimate=pl.CostEstimate(flops=flops, bytes_accessed=moved, transcendentals=transcendentals),
        name=name,
    )(*[a for a, _ in ins])


def whole(*shape):
    return pl.BlockSpec(shape, lambda *_: (0,) * len(shape))


def layer_of(index, *shape):
    return pl.BlockSpec((None,) + shape, lambda *_: (index,) + (0,) * len(shape))


def scalars():
    return pl.BlockSpec(memory_space=SMEM)


def norm_parts(values):
    centre = jnp.mean(values, axis=-1, keepdims=True)
    centred = values - centre
    spread = jnp.mean(centred * centred, axis=-1, keepdims=True)
    inverse = lax.rsqrt(spread + EPSILON)
    return centred * inverse, inverse


def norm_back(grad, zhat, inverse, gain):
    e = grad * gain
    return inverse * (
        e
        - jnp.mean(e, axis=-1, keepdims=True)
        - zhat * jnp.mean(e * zhat, axis=-1, keepdims=True)
    )


def qkv_step(hidden, gain, weight, a_ref, q_ref, kv_ref, scale):
    zhat, _ = norm_parts(hidden)
    a = (zhat * gain).astype(BF)
    a_ref[...] = a
    packed = mm(a, weight).astype(BF)
    width = a.shape[1]
    q_ref[...] = packed[:, :width] * jnp.asarray(scale, BF)
    kv_ref[...] = packed[:, width:]


def first_body(scale, ha_ref, hb_ref, gain_ref, w_ref, h_ref, a_ref, q_ref, kv_ref):
    span = ha_ref.shape[0]
    h_ref[:span] = ha_ref[...].astype(F32)
    h_ref[span:] = hb_ref[...].astype(F32)
    qkv_step(h_ref[...], gain_ref[0:1], w_ref[...], a_ref, q_ref, kv_ref, scale)


def attend_body(block, info_ref, q_ref, ko_ref, vo_ref, kx_ref, vx_ref, bo_ref, bx_ref, hot_ref, p_ref, att_ref, inv_ref):
    tokens = q_ref.shape[0]
    half = tokens
    head = LANES // 2
    k_own = jnp.concatenate([ko_ref[...], bo_ref[...]], axis=1)
    k_oth = jnp.concatenate([kx_ref[...], bx_ref[...]], axis=1)
    ones = jnp.ones((half, LANES), BF)
    v_own = jnp.concatenate([vo_ref[...], ones], axis=1)
    v_oth = jnp.concatenate([vx_ref[...], ones], axis=1)
    lower = lax.broadcasted_iota(jnp.int32, (block, LANES), 1) < head
    at_q = lax.broadcasted_iota(jnp.int32, (block, block), 0)
    at_k = lax.broadcasted_iota(jnp.int32, (block, block), 1)
    prefix = info_ref[0]
    for t in range(tokens // block):
        rows = slice(t * block, (t + 1) * block)
        seen = (at_k <= at_q) | (info_ref[1 + t] * block + at_k < prefix)
        q = q_ref[rows]
        parts = []
        for n in range(2):
            qn = jnp.where(lower if n == 0 else ~lower, q, jnp.zeros_like(q))
            qn = jnp.concatenate([qn, hot_ref[rows]], axis=1)
            s_own = mm_t(qn, k_own)
            s_oth = mm_t(qn, k_oth)
            pieces = [s_own[:, i * block : (i + 1) * block] for i in range(half // block)]
            pieces[t] = jnp.where(seen, pieces[t], NEGATIVE)
            s_own = jnp.concatenate(pieces, axis=1)
            top = jnp.maximum(
                jnp.max(s_own, axis=1, keepdims=True), jnp.max(s_oth, axis=1, keepdims=True)
            )
            p_own = jnp.exp(s_own - top).astype(BF)
            p_oth = jnp.exp(s_oth - top).astype(BF)
            p_ref[n, rows, :half] = p_own
            p_ref[n, rows, half:] = p_oth
            parts.append(mm(p_own, v_own) + mm(p_oth, v_oth))
        inverse = 1.0 / jnp.where(lower, parts[0][:, LANES:], parts[1][:, LANES:])
        inv_ref[rows] = inverse
        att_ref[rows] = (
            jnp.where(lower, parts[0][:, :LANES], parts[1][:, :LANES]) * inverse
        ).astype(BF)


def feed(h_ref, att_ref, wout_ref, gain_ref, wfc_ref, wproj_ref, mid_ref, sec_ref, act_ref, gp_ref):
    middle = h_ref[...] + mm(att_ref[...], wout_ref[...])
    mid_ref[...] = middle
    zhat, _ = norm_parts(middle)
    second = (zhat * gain_ref).astype(BF)
    sec_ref[...] = second
    total = middle
    width = middle.shape[1]
    for j in range(wfc_ref.shape[1] // width):
        cols = slice(j * width, (j + 1) * width)
        lifted = mm(second, wfc_ref[:, cols])
        phi = 0.5 * (1.0 + lax.erf(lifted * (1.0 / math.sqrt(2.0))))
        slope = phi + lifted * jnp.exp(-0.5 * lifted * lifted) * (1.0 / math.sqrt(2.0 * math.pi))
        gp_ref[:, cols] = slope.astype(BF)
        act = (lifted * phi).astype(BF)
        act_ref[:, cols] = act
        total = total + mm(act, wproj_ref[cols, :])
    return total


def middle_body(scale, layer, h_ref, att_ref, wout_ref, g2_ref, wfc_ref, wproj_ref, g1_ref, wqkv_ref,
                mid_ref, sec_ref, act_ref, gp_ref, out_ref, a_ref, q_ref, kv_ref):
    out = feed(h_ref, att_ref, wout_ref, g2_ref[layer : layer + 1], wfc_ref, wproj_ref, mid_ref, sec_ref, act_ref, gp_ref)
    out_ref[...] = out
    qkv_step(out, g1_ref[layer + 1 : layer + 2], wqkv_ref[...], a_ref, q_ref, kv_ref, scale)


def last_body(layer, h_ref, att_ref, wout_ref, g2_ref, wfc_ref, wproj_ref, mid_ref, sec_ref, act_ref, gp_ref, oa_ref, ob_ref):
    out = feed(h_ref, att_ref, wout_ref, g2_ref[layer : layer + 1], wfc_ref, wproj_ref, mid_ref, sec_ref, act_ref, gp_ref)
    span = oa_ref.shape[0]
    oa_ref[...] = out[:span].astype(BF)
    ob_ref[...] = out[span:].astype(BF)


def hand_out(core_ref, g_ref, keep_ref, send_ref):
    core = core_ref[0]
    keep_ref[...] = g_ref[core]
    send_ref[...] = g_ref[1 - core]


def put_rows(g_ref, start, values):
    half = g_ref.shape[1]
    count = values.shape[0]
    if start < half < start + count:
        cut = half - start
        g_ref[0, start:half] = values[:cut]
        g_ref[1, : count - cut] = values[cut:]
    else:
        side, at = divmod(start, half)
        g_ref[side, at : at + count] = values


def back_feed_body(layer, split, *refs):
    if split:
        core_ref, ua_ref, ub_ref = refs[:3]
        upstream = jnp.concatenate([ua_ref[...], ub_ref[...]], axis=0).astype(F32)
        refs = refs[3:]
    else:
        core_ref, u_ref = refs[:2]
        upstream = u_ref[...]
        refs = refs[2:]
    (act_ref, gp_ref, sec_ref, mid_ref, att_ref, wproj_ref, wfc_ref, wout_ref, g2_ref,
     keep_ref, send_ref, mg_ref, ag_ref, g_ref) = refs
    down = upstream.astype(BF)
    width = down.shape[1]
    inner = act_ref.shape[1]
    second = sec_ref[...]
    second_grad = None
    for j in range(inner // width):
        cols = slice(j * width, (j + 1) * width)
        put_rows(g_ref, j * width, t_mm(act_ref[:, cols], down).astype(BF))
        lift = (mm_t(down, wproj_ref[cols, :]) * gp_ref[:, cols].astype(F32)).astype(BF)
        put_rows(g_ref, inner + j * width, t_mm(second, lift).astype(BF))
        term = mm_t(lift, wfc_ref[:, cols])
        second_grad = term if second_grad is None else second_grad + term
    zhat, inverse = norm_parts(mid_ref[...])
    gain_grad = jnp.sum(second_grad * zhat, axis=0, keepdims=True)
    mg = upstream + norm_back(second_grad, zhat, inverse, g2_ref[layer : layer + 1])
    mg_ref[...] = mg
    branch = mg.astype(BF)
    put_rows(g_ref, 2 * inner, t_mm(att_ref[...], branch).astype(BF))
    ag_ref[...] = mm_t(branch, wout_ref[...]).astype(BF)
    at = 2 * inner + width
    extra = 2 * g_ref.shape[1] - at
    put_rows(g_ref, at, jnp.broadcast_to(gain_grad, (extra, width)).astype(BF))
    hand_out(core_ref, g_ref, keep_ref, send_ref)


def back_attend_body(scale, q_ref, ko_ref, vo_ref, kx_ref, vx_ref, p_ref, att_ref, inv_ref, ag_ref,
                     dq_ref, dko_ref, dvo_ref, dkx_ref, dvx_ref):
    tokens = q_ref.shape[0]
    head = LANES // 2
    lower = lax.broadcasted_iota(jnp.int32, (tokens, LANES), 1) < head
    q = q_ref[...]
    ag = ag_ref[...].astype(F32)
    inv = inv_ref[...]
    scaled = ag * inv
    product = scaled * att_ref[...].astype(F32)
    dq = None
    sums = [None] * 4
    for n in range(2):
        mine = lower if n == 0 else ~lower
        qn = jnp.where(mine, q, jnp.zeros_like(q))
        gn = jnp.where(mine, scaled, 0.0).astype(BF)
        delta = jnp.sum(jnp.where(mine, product, 0.0), axis=1, keepdims=True)
        dqn = None
        for i, (k_ref, v_ref) in enumerate(((ko_ref, vo_ref), (kx_ref, vx_ref))):
            p = p_ref[n, :, i * tokens : (i + 1) * tokens]
            ds = (p.astype(F32) * (mm_t(gn, v_ref[...]) - delta)).astype(BF)
            term = mm(ds, k_ref[...])
            dqn = term if dqn is None else dqn + term
            dk = t_mm(ds, qn)
            dv = t_mm(p, gn)
            sums[2 * i] = dk if n == 0 else sums[2 * i] + dk
            sums[2 * i + 1] = dv if n == 0 else sums[2 * i + 1] + dv
        dq = dqn if n == 0 else jnp.where(lower, dq, dqn)
    dq_ref[...] = (dq * scale).astype(BF)
    dko_ref[...] = sums[0]
    dvo_ref[...] = sums[1]
    dkx_ref[...] = sums[2].astype(BF)
    dvx_ref[...] = sums[3].astype(BF)


def back_qkv_body(layer, split, core_ref, dq_ref, dko_ref, dvo_ref, rk_ref, rv_ref, a_ref, h_ref, g1_ref, w_ref, mg_ref,
                  keep_ref, send_ref, *rest):
    a = a_ref[...]
    width = a.shape[1]
    blocks = (
        dq_ref[...],
        (dko_ref[...] + rk_ref[...].astype(F32)).astype(BF),
        (dvo_ref[...] + rv_ref[...].astype(F32)).astype(BF),
    )
    g_ref = rest[-1]
    grad = None
    for j, block in enumerate(blocks):
        put_rows(g_ref, j * width, t_mm(a, block).astype(BF))
        term = mm_t(block, w_ref[:, j * width : (j + 1) * width])
        grad = term if grad is None else grad + term
    zhat, inverse = norm_parts(h_ref[...])
    gain_grad = jnp.sum(grad * zhat, axis=0, keepdims=True)
    up = mg_ref[...] + norm_back(grad, zhat, inverse, g1_ref[layer : layer + 1])
    if split:
        oa_ref, ob_ref = rest[:2]
        span = oa_ref.shape[0]
        oa_ref[...] = up[:span].astype(BF)
        ob_ref[...] = up[span:].astype(BF)
    else:
        rest[0][...] = up
    at = 3 * width
    extra = 2 * g_ref.shape[1] - at
    put_rows(g_ref, at, jnp.broadcast_to(gain_grad, (extra, width)).astype(BF))
    hand_out(core_ref, g_ref, keep_ref, send_ref)


def halve_body(bit_ref, a_ref, b_ref, keep_ref, send_ref):
    bit = bit_ref[0]
    keep_ref[...] = (a_ref[bit].astype(F32) + b_ref[bit].astype(F32)).astype(BF)
    send_ref[...] = (a_ref[1 - bit].astype(F32) + b_ref[1 - bit].astype(F32)).astype(BF)


def halve(bit, a, b):
    rows, width = a.shape
    half = rows // 2
    return call(
        halve_body, "halve",
        [(bit, scalars()), (a.reshape(2, half, width), whole(2, half, width)), (b.reshape(2, half, width), whole(2, half, width))],
        [((half, width), BF, whole(half, width))] * 2,
        limit=16,
    )


def add_body(a_ref, b_ref, o_ref):
    o_ref[...] = (a_ref[...].astype(F32) + b_ref[...].astype(F32)).astype(BF)


def add(a, b):
    spec = whole(*a.shape)
    return call(add_body, "add", [(a, spec), (b, spec)], [(a.shape, BF, spec)], limit=16)[0]


def join_body(bit_ref, a_ref, b_ref, o_ref):
    bit = bit_ref[0]
    o_ref[bit] = a_ref[...]
    o_ref[1 - bit] = b_ref[...]


def join(bit, a, b):
    rows, width = a.shape
    spec = whole(rows, width)
    out = call(
        join_body, "join", [(bit, scalars()), (a, spec), (b, spec)], [((2, rows, width), BF, whole(2, rows, width))], limit=16
    )[0]
    return out.reshape(2 * rows, width)


def unpack_body(core_ref, fa_ref, fb_ref, qa_ref, qb_ref, *refs):
    proj_ref, fc_ref, out_ref, qkv_ref, n1_ref, n2_ref, f_ref, g_ref = refs[-8:]
    core = core_ref[0]
    f_ref[core] = fa_ref[...]
    f_ref[1 - core] = fb_ref[...]
    g_ref[core] = qa_ref[...]
    g_ref[1 - core] = qb_ref[...]

    def rows(ref, start, count):
        half = ref.shape[1]
        if start < half < start + count:
            return jnp.concatenate([ref[0, start:half], ref[1, : start + count - half]], axis=0)
        side, at = divmod(start, half)
        return ref[side, at : at + count]

    inner, width = proj_ref.shape
    proj_ref[...] = rows(f_ref, 0, inner).astype(F32)
    for j in range(inner // width):
        fc_ref[:, j * width : (j + 1) * width] = rows(f_ref, inner + j * width, width).astype(F32)
    out_ref[...] = rows(f_ref, 2 * inner, width).astype(F32)
    n2_ref[...] = rows(f_ref, 2 * inner + width, 16)[0:1].astype(F32)
    for j in range(3):
        qkv_ref[:, j * width : (j + 1) * width] = rows(g_ref, j * width, width).astype(F32)
    n1_ref[...] = rows(g_ref, 3 * width, 16)[0:1].astype(F32)


def unpack(core, layer, layers, width, inner, feed_halves, qkv_halves, before):
    ins = [(core, scalars())]
    ins += [(x, whole(*x.shape)) for x in (*feed_halves, *qkv_halves)]
    aliases = {}
    shapes = [(inner, width), (width, inner), (width, width), (width, 3 * width)]
    if before is not None:
        for i, array in enumerate(before[:4]):
            aliases[len(ins)] = i
            ins.append((array, pl.BlockSpec(memory_space=pl.ANY)))
    outs = [((layers, *s), F32, layer_of(layer, *s)) for s in shapes]
    outs += [((1, width), F32, whole(1, width))] * 2
    f, q = feed_halves[0].shape, qkv_halves[0].shape
    return call(
        unpack_body, "unpack", ins, outs, scratch=[VMEM((2, *f), BF), VMEM((2, *q), BF)], limit=48, aliases=aliases
    )


def per_device(mesh_shape, hidden_in, norm1_gain, qkv_weight, out_weight, norm2_gain, fc_weight, proj_weight,
               prefix_len, block_order, grad_out):
    dp, seq = mesh_shape
    rows_here, span, width = hidden_in.shape
    layers = qkv_weight.shape[0]
    inner = fc_weight.shape[2]
    scale = 1.0 / math.sqrt(width // HEADS)
    row_length = span * seq
    block_count = block_order.shape[0]
    block = row_length // block_count
    per_span = span // block
    tokens = 2 * span
    pairs = width // LANES
    assert rows_here == 2 and seq == 4 and dp % 2 == 0
    di, si = lax.axis_index("dp"), lax.axis_index("seq")
    core = di & 1
    odd = si & 1
    core_arr = core.astype(jnp.int32).reshape(1)

    def spot(d, s):
        return d * seq + s

    perm_a = [(spot(d, s), spot((d & ~1) | (s >> 1), 2 * (d & 1) + (s & 1))) for d in range(dp) for s in range(seq)]
    perm_b = [(spot(d, s), spot((d & ~1) | (s >> 1), 2 * (d & 1) + 1 - (s & 1))) for d in range(dp) for s in range(seq)]
    back_a = [(b, a) for a, b in perm_a]
    back_b = [(b, a) for a, b in perm_b]
    pair_perm = [(spot(d, s), spot(d ^ 1, s)) for d in range(dp) for s in range(seq)]

    def pair(x):
        return lax.ppermute(x, ALL, pair_perm)

    def spread(x):
        first = lax.dynamic_index_in_dim(x, odd, 0, keepdims=False)
        other = lax.dynamic_index_in_dim(x, 1 - odd, 0, keepdims=False)
        return lax.ppermute(first, ALL, perm_a), lax.ppermute(other, ALL, perm_b)

    def collect(a, b):
        a, b = lax.ppermute(a, ALL, back_a), lax.ppermute(b, ALL, back_b)
        return jnp.where(odd == 0, jnp.stack([a, b]), jnp.stack([b, a]))

    ha, hb = spread(hidden_in)
    ua, ub = spread(grad_out)
    prefix_other = pair(prefix_len)
    prefix_both = jnp.where(core == 0, jnp.concatenate([prefix_len, prefix_other]), jnp.concatenate([prefix_other, prefix_len]))
    prefix = jnp.sum(jnp.where(jnp.arange(4) == si, prefix_both, 0))

    def spans_of(c):
        return [2 * c + odd, 2 * c + 1 - odd]

    stored = jnp.stack([sp * per_span + i for c in (core, 1 - core) for sp in spans_of(c) for i in range(per_span)])
    ranks = jnp.sum(jnp.where(stored[:, None] == jnp.arange(block_count)[None, :], block_order[None, :], 0), axis=1)
    own_blocks = tokens // block
    info = jnp.concatenate([prefix.reshape(1), ranks[:own_blocks]]).astype(jnp.int32)
    key_rank = jnp.repeat(ranks, block, total_repeat_length=2 * tokens)[:, None]
    key_place = jnp.arange(2 * tokens, dtype=jnp.int32)[:, None]
    key_real = key_rank * block + key_place % block
    lane = jnp.arange(LANES, dtype=jnp.int32)[None, :]
    lane_rank = jnp.concatenate([ranks[:own_blocks], jnp.zeros((LANES - own_blocks,), ranks.dtype)])[None, :]
    hidden_key = (lane < own_blocks) & (key_rank >= lane_rank) & (key_place // block != lane) & (key_real >= prefix)
    bias = jnp.where(hidden_key, NEGATIVE, 0.0).astype(BF)
    hot = (jnp.arange(tokens, dtype=jnp.int32)[:, None] // block == lane).astype(BF)

    t_w = (tokens, width)
    full = whole(*t_w)
    wide = whole(tokens, inner)
    gains = whole(layers, width)
    dense = 2 * tokens * width

    def qkv_out():
        return [(t_w, BF, full), (t_w, BF, full), ((tokens, 2 * width), BF, whole(tokens, 2 * width))]

    h, a, q, kv = call(
        functools.partial(first_body, scale), "first",
        [(ha, whole(span, width)), (hb, whole(span, width)), (norm1_gain, gains), (qkv_weight, layer_of(0, width, 3 * width))],
        [(t_w, F32, full)] + qkv_out(),
        flops=dense * 3 * width,
    )
    lane_block = pl.BlockSpec((tokens, LANES), lambda p: (0, p))
    lane_block_v = pl.BlockSpec((tokens, LANES), lambda p: (0, p + pairs))
    p_spec = pl.BlockSpec((2, tokens, 2 * tokens), lambda p: (p, 0, 0))
    saved = []
    for layer in range(layers):
        kv_other = pair(kv)
        p, att, inv = call(
            functools.partial(attend_body, block), "attend",
            [(info, scalars()), (q, lane_block), (kv, lane_block), (kv, lane_block_v), (kv_other, lane_block), (kv_other, lane_block_v),
             (bias, pl.BlockSpec((tokens, LANES), lambda p: (0, 0))), (bias, pl.BlockSpec((tokens, LANES), lambda p: (1, 0))),
             (hot, whole(tokens, LANES))],
            [((HEADS, tokens, 2 * tokens), BF, p_spec), (t_w, BF, lane_block), (t_w, F32, lane_block)],
            grid=(pairs,), flops=4 * tokens * 2 * tokens * 256 * HEADS, transcendentals=HEADS * tokens * 2 * tokens,
        )
        ins = [
            (h, full), (att, full), (out_weight, layer_of(layer, width, width)), (norm2_gain, gains),
            (fc_weight, layer_of(layer, width, inner)), (proj_weight, layer_of(layer, inner, width)),
        ]
        outs = [(t_w, F32, full), (t_w, BF, full), ((tokens, inner), BF, wide), ((tokens, inner), BF, wide)]
        flops = dense * (width + 2 * inner)
        if layer < layers - 1:
            mid, sec, act, gp, h_next, a_next, q_next, kv_next = call(
                functools.partial(middle_body, scale, layer), "middle",
                ins + [(norm1_gain, gains), (qkv_weight, layer_of(layer + 1, width, 3 * width))],
                outs + [(t_w, F32, full)] + qkv_out(),
                flops=flops + dense * 3 * width, transcendentals=2 * tokens * inner,
            )
            saved.append((h, a, q, kv, kv_other, p, att, inv, mid, sec, act, gp))
            h, a, q, kv = h_next, a_next, q_next, kv_next
        else:
            half_spec = whole(span, width)
            mid, sec, act, gp, oa, ob = call(
                functools.partial(last_body, layer), "last", ins, outs + [((span, width), BF, half_spec)] * 2,
                flops=flops, transcendentals=2 * tokens * inner,
            )
            saved.append((h, a, q, kv, kv_other, p, att, inv, mid, sec, act, gp))
    hidden_out = collect(oa, ob)

    dp_bits = [i for i in range(1, dp.bit_length() - 1)]
    seq_bits = [i for i in range(seq.bit_length() - 1)]
    orders = (dp_bits, dp_bits[::-1])
    z_orders = (seq_bits, seq_bits[::-1])

    def swap_dp(x, step):
        return lax.ppermute(x, ALL, [(spot(d, s), spot(d ^ (1 << orders[d & 1][step]), s)) for d in range(dp) for s in range(seq)])

    def swap_seq(x, step):
        return lax.ppermute(x, ALL, [(spot(d, s), spot(d, s ^ (1 << z_orders[d & 1][step]))) for d in range(dp) for s in range(seq)])

    def bit_of(step):
        bits = [(di >> orders[c][step]) & 1 for c in (0, 1)]
        return jnp.where(core == 0, bits[0], bits[1]).astype(jnp.int32).reshape(1)

    bit_arrays = [bit_of(i) for i in range(len(dp_bits))]

    def sum_bucket(keep, send):
        got = pair(send)
        for step in range(len(dp_bits)):
            keep, send = halve(bit_arrays[step], keep, got)
            got = swap_dp(send, step)
        keep = add(keep, got)
        for step in range(len(seq_bits)):
            keep = add(keep, swap_seq(keep, step))
        for step in reversed(range(len(dp_bits))):
            keep = join(bit_arrays[step], keep, swap_dp(keep, step))
        return keep, pair(keep)

    parts = 2 ** len(dp_bits) * 2 * 16

    def padded(rows):
        return -(-(rows + 1) // parts) * parts

    feed_half = padded(2 * inner + width) // 2
    qkv_half = padded(3 * width) // 2
    up = None
    results = None
    norms = [None] * layers
    for layer in reversed(range(layers)):
        h, a, q, kv, kv_other, p, att, inv, mid, sec, act, gp = saved[layer]
        split = layer == layers - 1
        ups = [(ua, whole(span, width)), (ub, whole(span, width))] if split else [(up, full)]
        keep, send, mg, ag = call(
            functools.partial(back_feed_body, layer, split), "back_feed",
            [(core_arr, scalars())] + ups + [
                (act, wide), (gp, wide), (sec, full), (mid, full), (att, full),
                (proj_weight, layer_of(layer, inner, width)), (fc_weight, layer_of(layer, width, inner)),
                (out_weight, layer_of(layer, width, width)), (norm2_gain, gains)],
            [((feed_half, width), BF, whole(feed_half, width))] * 2 + [(t_w, F32, full), (t_w, BF, full)],
            scratch=[VMEM((2, feed_half, width), BF)], flops=dense * (4 * inner + 2 * width),
        )
        feed_sum = sum_bucket(keep, send)
        dq, dko, dvo, dkx, dvx = call(
            functools.partial(back_attend_body, scale), "back_attend",
            [(q, lane_block), (kv, lane_block), (kv, lane_block_v), (kv_other, lane_block), (kv_other, lane_block_v),
             (p, p_spec), (att, lane_block), (inv, lane_block), (ag, lane_block)],
            [(t_w, BF, lane_block), (t_w, F32, lane_block), (t_w, F32, lane_block), (t_w, BF, lane_block), (t_w, BF, lane_block)],
            grid=(pairs,), flops=8 * tokens * 2 * tokens * 256 * HEADS,
        )
        rk, rv = pair(dkx), pair(dvx)
        outs = [((qkv_half, width), BF, whole(qkv_half, width))] * 2
        last = layer == 0
        outs += [((span, width), BF, whole(span, width))] * 2 if last else [(t_w, F32, full)]
        res = call(
            functools.partial(back_qkv_body, layer, last), "back_qkv",
            [(core_arr, scalars()), (dq, full), (dko, full), (dvo, full), (rk, full), (rv, full), (a, full), (h, full),
             (norm1_gain, gains), (qkv_weight, layer_of(layer, width, 3 * width)), (mg, full)],
            outs, scratch=[VMEM((2, qkv_half, width), BF)], flops=2 * dense * 3 * width,
        )
        qkv_sum = sum_bucket(res[0], res[1])
        if last:
            grad_in = collect(res[2], res[3])
        else:
            up = res[2]
        results = unpack(core_arr, layer, layers, width, inner, feed_sum, qkv_sum, results)
        norms[layer] = results[4:6]
    norm1_grad = jnp.concatenate([n[0] for n in norms], axis=0)
    norm2_grad = jnp.concatenate([n[1] for n in norms], axis=0)
    proj_grad, fc_grad, out_grad, qkv_grad = results[:4]
    return hidden_out, grad_in, norm1_grad, qkv_grad, out_grad, norm2_grad, fc_grad, proj_grad


def solution(mesh):
    block = P("dp", "seq", None)
    return jax.shard_map(
        functools.partial(per_device, (mesh.shape["dp"], mesh.shape["seq"])),
        mesh=mesh,
        in_specs=(block, P(), P(), P(), P(), P(), P(), P("dp"), P(), block),
        out_specs=(block, block, P(), P(), P(), P(), P(), P()),
        check_vma=False,
    )
```

```python
import functools
import math

import jax
import jax.numpy as jnp
from jax import lax
from jax.experimental import pallas as pl
from jax.experimental.pallas import tpu as pltpu
from jax.sharding import PartitionSpec as P

HEADS = 6
EPSILON = 1e-05
NEGATIVE = -1e30
BF = jnp.bfloat16
F32 = jnp.float32
ALL = ("dp", "seq")
LANES = 128
GAIN_ROWS = 16
SCHEDULE = """
SH A BA1a BA1b A BT BF A BA0a B BA0b A C BE B C PH A B D C A B PG D C A D B C D B A D C B D B C D C D
"""
MB = 1024 * 1024
VMEM = pltpu.VMEM
SMEM = pltpu.SMEM


def mm(a, b):
    return lax.dot_general(a, b, (((1,), (0,)), ((), ())), preferred_element_type=F32)


def mm_t(a, b):
    return lax.dot_general(a, b, (((1,), (1,)), ((), ())), preferred_element_type=F32)


def t_mm(a, b):
    return lax.dot_general(a, b, (((0,), (0,)), ((), ())), preferred_element_type=F32)


class Order:
    def __init__(self):
        self.last = []

    def after(self, x):
        x, *last = lax.optimization_barrier((x, *self.last))
        self.last = last[-1:]
        return x

    def add(self, *results):
        self.last = [min(results, key=lambda r: r.size * r.dtype.itemsize), *self.last]


def call(body, name, ins, outs, scratch=(), limit=16, flops=0, transcendentals=0, grid=(1,), aliases=None, order=None):
    moved = sum(math.prod(o[0]) * jnp.dtype(o[1]).itemsize for o in outs)
    moved += sum(a.size * a.dtype.itemsize for a, _ in ins)
    kernel = body
    if order is not None:
        count, more = len(ins), len(order.last)
        ins = [*ins, *((x, pl.BlockSpec(memory_space=pl.ANY)) for x in order.last)]
        order.last = []

        def kernel(*refs):
            body(*refs[:count], *refs[count + more :])

    results = pl.pallas_call(
        kernel,
        out_shape=[pltpu.HBM(o[0], o[1]) if len(o) > 3 else jax.ShapeDtypeStruct(o[0], o[1]) for o in outs],
        grid=grid,
        in_specs=[s for _, s in ins],
        out_specs=[o[2] for o in outs],
        scratch_shapes=list(scratch),
        input_output_aliases=aliases or {},
        compiler_params=pltpu.CompilerParams(vmem_limit_bytes=limit * MB),
        cost_estimate=pl.CostEstimate(flops=flops, bytes_accessed=moved, transcendentals=transcendentals),
        name=name,
    )(*[a for a, _ in ins])
    if order is not None:
        order.add(*results)
    return results


def whole(*shape):
    return pl.BlockSpec(shape, lambda *_: (0,) * len(shape))


def layer_of(index, *shape):
    return pl.BlockSpec((None,) + shape, lambda *_: (index,) + (0,) * len(shape))


def scalars():
    return pl.BlockSpec(memory_space=SMEM)


def norm_parts(values):
    centre = jnp.mean(values, axis=-1, keepdims=True)
    centred = values - centre
    spread = jnp.mean(centred * centred, axis=-1, keepdims=True)
    inverse = lax.rsqrt(spread + EPSILON)
    return centred * inverse, inverse


def norm_back(grad, zhat, inverse, gain):
    e = grad * gain
    return inverse * (
        e
        - jnp.mean(e, axis=-1, keepdims=True)
        - zhat * jnp.mean(e * zhat, axis=-1, keepdims=True)
    )


def qkv_step(hidden, gain, weight, a_ref, q_ref, kv_ref, scale):
    zhat, _ = norm_parts(hidden)
    a = (zhat * gain).astype(BF)
    a_ref[...] = a
    packed = mm(a, weight).astype(BF)
    width = a.shape[1]
    q_ref[...] = packed[:, :width] * jnp.asarray(scale, BF)
    kv_ref[...] = packed[:, width:]


def first_body(scale, ha_ref, hb_ref, gain_ref, w_ref, h_ref, a_ref, q_ref, kv_ref):
    span = ha_ref.shape[0]
    h_ref[:span] = ha_ref[...].astype(F32)
    h_ref[span:] = hb_ref[...].astype(F32)
    qkv_step(h_ref[...], gain_ref[0:1], w_ref[...], a_ref, q_ref, kv_ref, scale)


def attend_body(block, info_ref, q_ref, ko_ref, vo_ref, kx_ref, vx_ref, bo_ref, bx_ref, hot_ref, p_ref, att_ref, inv_ref):
    tokens = q_ref.shape[0]
    head = LANES // 2
    ones = jnp.ones((tokens, LANES), BF)

    def beside(a, b):
        return jnp.concatenate([a, b], axis=1)

    keys = jnp.concatenate([beside(ko_ref[...], bo_ref[...]), beside(kx_ref[...], bx_ref[...])], axis=0)
    values = jnp.concatenate([beside(vo_ref[...], ones), beside(vx_ref[...], ones)], axis=0)
    lower = lax.broadcasted_iota(jnp.int32, (tokens, LANES), 1) < head
    at_q = lax.broadcasted_iota(jnp.int32, (block, block), 0)
    at_k = lax.broadcasted_iota(jnp.int32, (block, block), 1)
    prefix = info_ref[0]
    q = q_ref[...]
    scores = []
    for n in range(2):
        qn = jnp.where(lower if n == 0 else ~lower, q, jnp.zeros_like(q))
        scores.append(mm_t(beside(qn, hot_ref[...]), keys))
    chances = []
    for n in range(2):
        rows = []
        for t in range(tokens // block):
            s = scores[n][t * block : (t + 1) * block]
            seen = (at_k <= at_q) | (info_ref[1 + t] * block + at_k < prefix)
            pieces = [s[:, : t * block], jnp.where(seen, s[:, t * block : (t + 1) * block], NEGATIVE), s[:, (t + 1) * block :]]
            s = jnp.concatenate([piece for piece in pieces if piece.shape[1]], axis=1)
            rows.append(jnp.exp(s - jnp.max(s, axis=1, keepdims=True)).astype(BF))
        p = jnp.concatenate(rows, axis=0)
        p_ref[n] = p
        chances.append(p)
    even, odd = [mm(p, values) for p in chances]
    inverse = 1.0 / jnp.where(lower, even[:, LANES:], odd[:, LANES:])
    inv_ref[...] = inverse
    att_ref[...] = (jnp.where(lower, even[:, :LANES], odd[:, :LANES]) * inverse).astype(BF)


def feed(h_ref, att_ref, wout_ref, gain, wfc_ref, wproj_ref, mid_ref, sec_ref, act_ref, gp_ref):
    middle = h_ref[...] + mm(att_ref[...], wout_ref[...])
    mid_ref[...] = middle
    zhat, _ = norm_parts(middle)
    second = (zhat * gain).astype(BF)
    sec_ref[...] = second
    total = middle
    width = middle.shape[1]
    for j in range(wfc_ref.shape[1] // width):
        cols = slice(j * width, (j + 1) * width)
        lifted = mm(second, wfc_ref[:, cols])
        phi = 0.5 * (1.0 + lax.erf(lifted * (1.0 / math.sqrt(2.0))))
        slope = phi + lifted * jnp.exp(-0.5 * lifted * lifted) * (1.0 / math.sqrt(2.0 * math.pi))
        gp_ref[:, cols] = slope.astype(BF)
        act = (lifted * phi).astype(BF)
        act_ref[:, cols] = act
        total = total + mm(act, wproj_ref[cols, :])
    return total


def middle_body(scale, layer, h_ref, att_ref, wout_ref, g2_ref, wfc_ref, wproj_ref, g1_ref, wqkv_ref,
                mid_ref, sec_ref, act_ref, gp_ref, out_ref, a_ref, q_ref, kv_ref):
    out = feed(h_ref, att_ref, wout_ref, g2_ref[layer : layer + 1], wfc_ref, wproj_ref, mid_ref, sec_ref, act_ref, gp_ref)
    out_ref[...] = out
    qkv_step(out, g1_ref[layer + 1 : layer + 2], wqkv_ref[...], a_ref, q_ref, kv_ref, scale)


def relative(bits, index, core):
    place = 0
    for mine, others in bits:
        place = 2 * place + (jnp.where(core == 0, index >> mine, index >> others) & 1)
    return place


def hand_out(bits, at_ref, g_ref, keep_ref, send_ref):
    index = at_ref[0]
    core = index & 1
    count = keep_ref.shape[0]
    for ref, side in ((keep_ref, core), (send_ref, 1 - core)):
        place = relative(bits, index, side)
        for i in range(count):
            ref[i] = g_ref[side * count + (place ^ i)]


def put_rows(g_ref, start, values):
    size = g_ref.shape[1]
    done = 0
    while done < values.shape[0]:
        block, at = divmod(start + done, size)
        count = min(size - at, values.shape[0] - done)
        g_ref[block, at : at + count] = values[done : done + count]
        done += count


def back_proj(upstream, act_ref, gp_ref, wproj_ref, g_ref, at, lift_ref):
    down = upstream.astype(BF)
    width = down.shape[1]
    for j in range(act_ref.shape[1] // width):
        cols = slice(j * width, (j + 1) * width)
        put_rows(g_ref, at + j * width, t_mm(act_ref[:, cols], down).astype(BF))
        lift_ref[:, cols] = (mm_t(down, wproj_ref[cols, :]) * gp_ref[:, cols].astype(F32)).astype(BF)


def back_fc(upstream, lift_ref, sec_ref, mid_ref, att_ref, wfc_ref, wout_ref, gain, g_ref, at, mg_ref, ag_ref, gain_ref):
    second = sec_ref[...]
    width = second.shape[1]
    inner = lift_ref.shape[1]
    second_grad = None
    for j in range(inner // width):
        cols = slice(j * width, (j + 1) * width)
        lift = lift_ref[:, cols]
        put_rows(g_ref, at + j * width, t_mm(second, lift).astype(BF))
        term = mm_t(lift, wfc_ref[:, cols])
        second_grad = term if second_grad is None else second_grad + term
    zhat, inverse = norm_parts(mid_ref[...])
    gain_ref[...] = jnp.broadcast_to(jnp.sum(second_grad * zhat, axis=0, keepdims=True), gain_ref.shape)
    mg = upstream + norm_back(second_grad, zhat, inverse, gain)
    mg_ref[...] = mg
    branch = mg.astype(BF)
    put_rows(g_ref, at + inner, t_mm(att_ref[...], branch).astype(BF))
    ag_ref[...] = mm_t(branch, wout_ref[...]).astype(BF)


def turn_body(layer, bits, core_ref, h_ref, att_ref, wout_ref, g2_ref, wfc_ref, wproj_ref, u_ref,
              oa_ref, ob_ref, keep_ref, send_ref, mg_ref, ag_ref, gain_ref,
              mid_ref, sec_ref, act_ref, gp_ref, lift_ref, g_ref):
    gain = g2_ref[layer : layer + 1]
    out = feed(h_ref, att_ref, wout_ref, gain, wfc_ref, wproj_ref, mid_ref, sec_ref, act_ref, gp_ref)
    span = oa_ref.shape[0]
    oa_ref[...] = out[:span].astype(BF)
    ob_ref[...] = out[span:].astype(BF)
    upstream = u_ref[...].astype(F32)
    back_proj(upstream, act_ref, gp_ref, wproj_ref, g_ref, 0, lift_ref)
    back_fc(upstream, lift_ref, sec_ref, mid_ref, att_ref, wfc_ref, wout_ref, gain, g_ref, act_ref.shape[1],
            mg_ref, ag_ref, gain_ref)
    hand_out(bits, core_ref, g_ref, keep_ref, send_ref)


def back_fc_body(layer, bits, core_ref, u_ref, lift_ref, sec_ref, mid_ref, att_ref, wfc_ref, wout_ref, g2_ref,
                 keep_ref, send_ref, mg_ref, ag_ref, gain_ref, g_ref):
    back_fc(u_ref[...], lift_ref, sec_ref, mid_ref, att_ref, wfc_ref, wout_ref, g2_ref[layer : layer + 1], g_ref, 0,
            mg_ref, ag_ref, gain_ref)
    hand_out(bits, core_ref, g_ref, keep_ref, send_ref)


def back_attend_body(scale, q_ref, ko_ref, vo_ref, kx_ref, vx_ref, p_ref, att_ref, inv_ref, ag_ref,
                     dq_ref, own_ref, oth_ref):
    tokens = q_ref.shape[0]
    head = LANES // 2
    lower = lax.broadcasted_iota(jnp.int32, (tokens, LANES), 1) < head
    q = q_ref[...]
    scaled = ag_ref[...].astype(F32) * inv_ref[...]
    product = scaled * att_ref[...].astype(F32)
    keys = jnp.concatenate([ko_ref[...], kx_ref[...]], axis=0)
    values = jnp.concatenate([vo_ref[...], vx_ref[...]], axis=0)
    dq = dk = dv = None
    for n in range(2):
        mine = lower if n == 0 else ~lower
        qn = jnp.where(mine, q, jnp.zeros_like(q))
        gn = jnp.where(mine, scaled, 0.0).astype(BF)
        delta = jnp.sum(jnp.where(mine, product, 0.0), axis=1, keepdims=True)
        p = p_ref[n]
        ds = (p.astype(F32) * (mm_t(gn, values) - delta)).astype(BF)
        dqn, dkn, dvn = mm(ds, keys), t_mm(qn, ds), t_mm(gn, p)
        if n == 0:
            dq, dk, dv = dqn, dkn, dvn
        else:
            dq, dk, dv = jnp.where(lower, dq, dqn), dk + dkn, dv + dvn
    dq_ref[...] = (dq * scale).astype(BF)
    for i, grad in enumerate((dk.T, dv.T)):
        own_ref[i] = grad[:tokens]
        oth_ref[i] = grad[tokens:].astype(BF)


def back_qkv(layer, parts, a_ref, h_ref, g1_ref, w_ref, mg_ref, g_ref):
    a = a_ref[...]
    width = a.shape[1]
    blocks = [jnp.concatenate([dq[...] for dq, _, _ in parts], axis=1)]
    for i in range(2):
        blocks.append(jnp.concatenate([(own[i] + got[i].astype(F32)).astype(BF) for _, own, got in parts], axis=1))
    grad = None
    for j, block in enumerate(blocks):
        put_rows(g_ref, j * width, t_mm(a, block).astype(BF))
        term = mm_t(block, w_ref[:, j * width : (j + 1) * width])
        grad = term if grad is None else grad + term
    zhat, inverse = norm_parts(h_ref[...])
    gain_grad = jnp.sum(grad * zhat, axis=0, keepdims=True)
    return mg_ref[...] + norm_back(grad, zhat, inverse, g1_ref[layer : layer + 1]), gain_grad


def back_turn_body(layer, bits, core_ref, *refs):
    parts, refs = (refs[:3], refs[3:6]), refs[6:]
    (a_ref, h_ref, g1_ref, w_ref, mg_ref, act_ref, gp_ref, wproj_ref,
     keep_ref, send_ref, up_ref, gain_ref, lift_ref, g_ref) = refs
    up, gain_grad = back_qkv(layer, parts, a_ref, h_ref, g1_ref, w_ref, mg_ref, g_ref)
    gain_ref[...] = jnp.broadcast_to(gain_grad, gain_ref.shape)
    up_ref[...] = up
    back_proj(up, act_ref, gp_ref, wproj_ref, g_ref, 3 * up.shape[1], lift_ref)
    hand_out(bits, core_ref, g_ref, keep_ref, send_ref)


def back_end_body(layer, bits, core_ref, *refs):
    parts, refs = (refs[:3], refs[3:6]), refs[6:]
    (a_ref, h_ref, g1_ref, w_ref, mg_ref, *gain_refs, keep_ref, send_ref, oa_ref, ob_ref, g_ref) = refs
    up, gain_grad = back_qkv(layer, parts, a_ref, h_ref, g1_ref, w_ref, mg_ref, g_ref)
    span = oa_ref.shape[0]
    width = up.shape[1]
    oa_ref[...] = up[:span].astype(BF)
    ob_ref[...] = up[span:].astype(BF)
    at = 3 * width
    for i, gain in enumerate([gain_grad] + [ref[0:1] for ref in gain_refs]):
        put_rows(g_ref, at + GAIN_ROWS * i, jnp.broadcast_to(gain, (GAIN_ROWS, width)).astype(BF))
    at += GAIN_ROWS * (1 + len(gain_refs))
    put_rows(g_ref, at, jnp.zeros((g_ref.shape[0] * g_ref.shape[1] - at, width), BF))
    hand_out(bits, core_ref, g_ref, keep_ref, send_ref)


def masks_body(per_span, block, ids_ref, order_ref, own_ref, other_ref, bias_ref, hot_ref, info_ref):
    core, place = ids_ref[0] & 1, ids_ref[1]
    odd = place & 1
    prefix = jnp.where((place >> 1) == core, own_ref[odd], other_ref[odd])
    info_ref[0] = prefix
    ranks = []
    for c in (core, 1 - core):
        for span in (2 * c + odd, 2 * c + 1 - odd):
            ranks += [order_ref[span * per_span + i] for i in range(per_span)]
    tokens = hot_ref.shape[0]
    own = tokens // block
    lane = lax.broadcasted_iota(jnp.int32, (block, LANES), 1)
    within = lax.broadcasted_iota(jnp.int32, (block, LANES), 0)
    lane_rank = jnp.full((block, LANES), -1, jnp.int32)
    for b in range(own):
        info_ref[1 + b] = ranks[b]
        lane_rank = jnp.where(lane == b, ranks[b], lane_rank)
        hot_ref[b * block : (b + 1) * block] = jnp.where(lane == b, 1.0, 0.0).astype(BF)
    for k, rank in enumerate(ranks):
        unseen = (lane < own) & (rank >= lane_rank) & (lane != k) & (rank * block + within >= prefix)
        bias_ref[k * block : (k + 1) * block] = jnp.where(unseen, NEGATIVE, 0.0).astype(BF)


def pick_body(odd_ref, x_ref, a_ref, b_ref):
    odd = odd_ref[1] & 1
    a_ref[...] = x_ref[odd]
    b_ref[...] = x_ref[1 - odd]


def place_body(odd_ref, a_ref, b_ref, o_ref):
    odd = odd_ref[1] & 1
    o_ref[odd] = a_ref[...]
    o_ref[1 - odd] = b_ref[...]


def stack_body(a_ref, b_ref, o_ref):
    span = a_ref.shape[0]
    o_ref[:span] = a_ref[...]
    o_ref[span:] = b_ref[...]


def add(a, b):
    return (a.astype(F32) + b.astype(F32)).astype(BF)


def take_rows(g_ref, start, count):
    size = g_ref.shape[1]
    pieces = []
    while count:
        block, at = divmod(start, size)
        here = min(size - at, count)
        pieces.append(g_ref[block, at : at + here])
        start, count = start + here, count - here
    return pieces[0] if len(pieces) == 1 else jnp.concatenate(pieces, axis=0)


def unpack_body(plan, gains, bits, at_ref, a_ref, b_ref, *refs):
    g_ref = refs[-1]
    out_refs = refs[len(refs) - 1 - len(plan) - len(gains) : -1]
    index = at_ref[0]
    core = index & 1
    count = a_ref.shape[0]
    for ref, side in ((a_ref, core), (b_ref, 1 - core)):
        place = relative(bits, index, side)
        for i in range(count):
            g_ref[side * count + (place ^ i)] = ref[i]
    width = a_ref.shape[2]
    for start, ref in zip(plan, out_refs):
        rows, cols = ref.shape
        for j in range(cols // width):
            ref[:, j * width : (j + 1) * width] = take_rows(g_ref, start + j * rows, rows).astype(F32)
    for i, ref in zip(gains, out_refs[len(plan) :]):
        ref[...] = take_rows(g_ref, i, GAIN_ROWS)[0:1].astype(F32)


def unpack(bits, at, halves, layers, parts, gains, order):
    ins = [(at, scalars())] + [(x, whole(*x.shape)) for x in halves]
    aliases = {}
    outs = []
    for i, (_, layer, shape, before) in enumerate(parts):
        if before is not None:
            aliases[len(ins)] = i
            ins.append((before, pl.BlockSpec(memory_space=pltpu.HBM)))
        outs.append(((layers, *shape), F32, layer_of(layer, *shape), True))
    count, rows, width = halves[0].shape
    outs += [((1, width), F32, whole(1, width))] * len(gains)
    return call(
        functools.partial(unpack_body, [p[0] for p in parts], gains, bits), "unpack", ins, outs,
        scratch=[VMEM((2 * count, rows, width), BF)], limit=32, aliases=aliases, order=order,
    )


def per_device(mesh_shape, hidden_in, norm1_gain, qkv_weight, out_weight, norm2_gain, fc_weight, proj_weight,
               prefix_len, block_order, grad_out):
    dp, seq = mesh_shape
    rows_here, span, width = hidden_in.shape
    layers = qkv_weight.shape[0]
    inner = fc_weight.shape[2]
    scale = 1.0 / math.sqrt(width // HEADS)
    row_length = span * seq
    block_count = block_order.shape[0]
    block = row_length // block_count
    per_span = span // block
    tokens = 2 * span
    pairs = width // LANES
    assert rows_here == 2 and seq == 4 and dp % 2 == 0 and layers == 2
    di, si = lax.axis_index("dp"), lax.axis_index("seq")
    at = jnp.stack([di, si]).astype(jnp.int32)
    order = Order()

    def spot(d, s):
        return d * seq + s

    perm_a = [(spot(d, s), spot((d & ~1) | (s >> 1), 2 * (d & 1) + (s & 1))) for d in range(dp) for s in range(seq)]
    perm_b = [(spot(d, s), spot((d & ~1) | (s >> 1), 2 * (d & 1) + 1 - (s & 1))) for d in range(dp) for s in range(seq)]
    back_a = [(b, a) for a, b in perm_a]
    back_b = [(b, a) for a, b in perm_b]
    pair_perm = [(spot(d, s), spot(d ^ 1, s)) for d in range(dp) for s in range(seq)]
    t_w = (tokens, width)
    full = whole(*t_w)
    half_spec = whole(span, width)
    both_spec = whole(2, span, width)

    def pair(x):
        return lax.ppermute(x, ALL, pair_perm)

    def spread(x, order):
        first, other = call(
            pick_body, "pick", [(at, scalars()), (x, both_spec)], [((span, width), BF, half_spec)] * 2, order=order
        )
        return lax.ppermute(first, ALL, perm_a), lax.ppermute(other, ALL, perm_b)

    class Collect:
        def __init__(self, a, b):
            self.a, self.b = lax.ppermute(a, ALL, back_a), lax.ppermute(b, ALL, back_b)

        def done(self, order):
            return call(
                place_body, "place", [(at, scalars()), (self.a, half_spec), (self.b, half_spec)],
                [((2, span, width), BF, both_spec, True)], limit=8, order=order,
            )[0]

    dp_bits = [i for i in range(1, dp.bit_length() - 1)]
    seq_bits = [i for i in range(seq.bit_length() - 1)]
    orders = (dp_bits, dp_bits[::-1])
    z_orders = (seq_bits, seq_bits[::-1])
    bits = list(zip(*orders))

    own_blocks = tokens // block
    ha, hb = spread(hidden_in, order)
    prefix_other = pair(prefix_len)
    bias, hot, info = call(
        functools.partial(masks_body, per_span, block), "masks",
        [(at, scalars()), (block_order, scalars()), (prefix_len, scalars()), (prefix_other, scalars())],
        [((2 * tokens, LANES), BF, whole(2 * tokens, LANES)), ((tokens, LANES), BF, whole(tokens, LANES)),
         ((1 + own_blocks,), jnp.int32, scalars())],
        order=order,
    )

    wide = whole(tokens, inner)
    gains = whole(layers, width)
    dense = 2 * tokens * width

    def qkv_out():
        return [(t_w, BF, full), (t_w, BF, full), ((tokens, 2 * width), BF, whole(tokens, 2 * width))]

    h, a, q, kv = call(
        functools.partial(first_body, scale), "first",
        [(ha, half_spec), (hb, half_spec), (norm1_gain, gains), (qkv_weight, layer_of(0, width, 3 * width))],
        [(t_w, F32, full)] + qkv_out(),
        flops=dense * 3 * width, order=order,
    )
    lane_block = pl.BlockSpec((tokens, LANES), lambda p: (0, p))
    lane_block_v = pl.BlockSpec((tokens, LANES), lambda p: (0, p + pairs))
    p_spec = pl.BlockSpec((2, tokens, 2 * tokens), lambda p: (p, 0, 0))

    def attend(q, kv, kv_other):
        return call(
            functools.partial(attend_body, block), "attend",
            [(info, scalars()), (q, lane_block), (kv, lane_block), (kv, lane_block_v), (kv_other, lane_block), (kv_other, lane_block_v),
             (bias, pl.BlockSpec((tokens, LANES), lambda p: (0, 0))), (bias, pl.BlockSpec((tokens, LANES), lambda p: (1, 0))),
             (hot, whole(tokens, LANES))],
            [((HEADS, tokens, 2 * tokens), BF, p_spec), (t_w, BF, lane_block), (t_w, F32, lane_block)],
            grid=(pairs,), flops=4 * tokens * 2 * tokens * 256 * HEADS, transcendentals=HEADS * tokens * 2 * tokens,
            limit=18, order=order,
        )

    def feed_ins(layer, h, att):
        return [
            (h, full), (att, full), (out_weight, layer_of(layer, width, width)), (norm2_gain, gains),
            (fc_weight, layer_of(layer, width, inner)), (proj_weight, layer_of(layer, inner, width)),
        ]

    def swap_dp(x, step):
        return lax.ppermute(x, ALL, [(spot(d, s), spot(d ^ (1 << orders[d & 1][step]), s)) for d in range(dp) for s in range(seq)])

    def swap_seq(x, step):
        return lax.ppermute(x, ALL, [(spot(d, s), spot(d, s ^ (1 << z_orders[d & 1][step]))) for d in range(dp) for s in range(seq)])

    class Bucket:
        def __init__(self, keep, send):
            self.halves = None
            self.steps = self.run(keep, send)
            next(self.steps)

        def run(self, keep, send):
            got = pair(send)
            for step in range(len(dp_bits)):
                yield
                total = add(keep, order.after(got))
                half = total.shape[0] // 2
                keep, send = total[:half], total[half:]
                order.add(keep)
                got = swap_dp(send, step)
            yield
            total = add(keep, order.after(got))
            order.add(total)
            for step in range(len(seq_bits)):
                got = swap_seq(total, step)
                yield
                total = add(total, order.after(got))
                order.add(total)
            for step in reversed(range(len(dp_bits))):
                got = swap_dp(total, step)
                yield
                total = jnp.concatenate([total, order.after(got)], axis=0)
                order.add(total)
            self.halves = (total, pair(total))
            yield

        def step(self):
            next(self.steps)

    def bucket_outs(rows):
        count = 2 ** len(dp_bits)
        size = rows // (2 * count)
        assert size * 2 * count == rows
        return [((count, size, width), BF, whole(count, size, width))] * 2, [VMEM((2 * count, size, width), BF)]

    gain_out = ((8, width), F32, whole(8, width))

    kv_other = pair(kv)
    ua, ub = spread(grad_out, order)
    p, att, inv = attend(q, kv, kv_other)
    u = call(stack_body, "stack", [(ua, half_spec), (ub, half_spec)], [(t_w, BF, full)], order=order)[0]
    mid, sec, act, gp, h_next, a_next, q_next, kv_next = call(
        functools.partial(middle_body, scale, 0), "middle",
        feed_ins(0, h, att) + [(norm1_gain, gains), (qkv_weight, layer_of(1, width, 3 * width))],
        [(t_w, F32, full), (t_w, BF, full), ((tokens, inner), BF, wide), ((tokens, inner), BF, wide), (t_w, F32, full)] + qkv_out(),
        flops=dense * (4 * width + 2 * inner), transcendentals=2 * tokens * inner, limit=24, order=order,
    )
    saved = (h, a, q, kv, kv_other, p, att, inv)
    h, a, q, kv = h_next, a_next, q_next, kv_next

    kv_other = pair(kv)
    p, att, inv = attend(q, kv, kv_other)
    outs, scratch = bucket_outs(2 * inner + width)
    oa, ob, keep, send, mg, ag, gain2_1 = call(
        functools.partial(turn_body, 1, bits), "turn",
        [(at, scalars())] + feed_ins(1, h, att) + [(u, full)],
        [((span, width), BF, half_spec)] * 2 + outs + [(t_w, F32, full), (t_w, BF, full), gain_out],
        scratch=[VMEM(t_w, F32), VMEM(t_w, BF)] + [VMEM((tokens, inner), BF)] * 3 + scratch,
        flops=dense * (3 * width + 6 * inner), transcendentals=2 * tokens * inner, limit=28, order=order,
    )
    feed_1 = Bucket(keep, send)

    def back_attend(first, count, q, kv, kv_other, p, att, inv, ag):
        spec = pl.BlockSpec((tokens, LANES), lambda p: (0, p + first))
        spec_v = pl.BlockSpec((tokens, LANES), lambda p: (0, p + first + pairs))
        out = (tokens, count * LANES)
        pair_out = pl.BlockSpec((2, tokens, LANES), lambda p: (0, 0, p))
        dq, own, oth = call(
            functools.partial(back_attend_body, scale), "back_attend",
            [(q, spec), (kv, spec), (kv, spec_v), (kv_other, spec), (kv_other, spec_v),
             (p, pl.BlockSpec((2, tokens, 2 * tokens), lambda p: (p + first, 0, 0))), (att, spec), (inv, spec), (ag, spec)],
            [(out, BF, lane_block), ((2, *out), F32, pair_out), ((2, *out), BF, pair_out)],
            grid=(count,), flops=8 * tokens * 2 * tokens * 256 * 2 * count, limit=18, order=order,
        )
        return dq, own, pair(oth)

    def part_ins(parts):
        return [(x, whole(*x.shape)) for part in parts for x in part]

    layer_1 = (q, kv, kv_other, p, att, inv)
    h_1, a_1, mg_1, ag_1 = h, a, mg, ag
    h_0, a_0, *layer_0 = saved
    v = {}
    buckets = {"A": feed_1}

    def back_turn():
        outs, scratch = bucket_outs(3 * width + inner)
        keep, send, v["up"], v["gain1_1"], v["lift"] = call(
            functools.partial(back_turn_body, 1, bits), "back_turn",
            [(at, scalars())] + part_ins((v["1a"], v["1b"])) + [
                (a_1, full), (h_1, full), (norm1_gain, gains), (qkv_weight, layer_of(1, width, 3 * width)), (mg_1, full),
                (act, wide), (gp, wide), (proj_weight, layer_of(0, inner, width))],
            outs + [(t_w, F32, full), gain_out, ((tokens, inner), BF, wide)],
            scratch=scratch, flops=dense * (6 * width + 2 * inner), limit=24, order=order,
        )
        buckets["B"] = Bucket(keep, send)

    def back_fc_0():
        outs, scratch = bucket_outs(inner + width)
        keep, send, v["mg"], v["ag"], v["gain2_0"] = call(
            functools.partial(back_fc_body, 0, bits), "back_fc",
            [(at, scalars()), (v["up"], full), (v["lift"], wide), (sec, full), (mid, full), (layer_0[4], full),
             (fc_weight, layer_of(0, width, inner)), (out_weight, layer_of(0, width, width)), (norm2_gain, gains)],
            outs + [(t_w, F32, full), (t_w, BF, full), gain_out],
            scratch=scratch, flops=dense * (2 * width + 2 * inner), limit=24, order=order,
        )
        buckets["C"] = Bucket(keep, send)

    def back_end():
        last_rows = -(-(3 * width + 4 * GAIN_ROWS) // 128) * 128
        outs, scratch = bucket_outs(last_rows)
        keep, send, ga, gb = call(
            functools.partial(back_end_body, 0, bits), "back_end",
            [(at, scalars())] + part_ins((v["0a"], v["0b"])) + [
                (a_0, full), (h_0, full), (norm1_gain, gains), (qkv_weight, layer_of(0, width, 3 * width)), (v["mg"], full)]
            + [(g, whole(8, width)) for g in (v["gain1_1"], v["gain2_0"], gain2_1)],
            outs + [((span, width), BF, half_spec)] * 2,
            scratch=scratch, flops=2 * dense * 3 * width, limit=16, order=order,
        )
        buckets["D"] = Bucket(keep, send)
        v["grad_in"] = Collect(ga, gb)

    def run_part(name, first, count, layer, ag):
        v[name] = back_attend(first, count, *layer, ag)

    def collected(name):
        v[name] = v[name].done(order)

    def unpacked(name):
        halves = buckets[name].halves
        if name == "A":
            parts = [(0, 1, (inner, width), "proj"), (inner, 1, (width, inner), "fc"), (2 * inner, 1, (width, width), "out")]
        elif name == "B":
            parts = [(0, 1, (width, 3 * width), "qkv"), (3 * width, 0, (inner, width), "proj")]
        elif name == "C":
            parts = [(0, 0, (width, inner), "fc"), (inner, 0, (width, width), "out")]
        else:
            parts = [(0, 0, (width, 3 * width), "qkv")]
        gain_rows = [3 * width + GAIN_ROWS * i for i in range(4)] if name == "D" else []
        got = unpack(bits, at, halves, layers, [(*part[:3], v.get(part[3])) for part in parts], gain_rows, order)
        for part, array in zip(parts, got):
            v[part[3]] = array
        if name == "D":
            v["gains"] = got[1:]

    def bucket_step(name):
        if name in buckets:
            if buckets[name].halves is None:
                buckets[name].step()
            else:
                unpacked(name)
                del buckets[name]

    kernels = {
        "BA1a": lambda: run_part("1a", 0, 1, layer_1, ag_1),
        "BA1b": lambda: run_part("1b", 1, pairs - 1, layer_1, ag_1),
        "BT": back_turn,
        "BF": back_fc_0,
        "BA0a": lambda: run_part("0a", 0, 1, layer_0, v["ag"]),
        "BA0b": lambda: run_part("0b", 1, pairs - 1, layer_0, v["ag"]),
        "BE": back_end,
        "SH": lambda: v.update(hidden_out=Collect(oa, ob)),
        "PH": lambda: collected("hidden_out"),
        "PG": lambda: collected("grad_in"),
    }
    for token in SCHEDULE.split():
        if token in kernels:
            kernels[token]()
        else:
            bucket_step(token)
    while buckets:
        for name in list(buckets):
            bucket_step(name)
    norm1_grad = jnp.concatenate([v["gains"][0], v["gains"][1]], axis=0)
    norm2_grad = jnp.concatenate([v["gains"][2], v["gains"][3]], axis=0)
    return v["hidden_out"], v["grad_in"], norm1_grad, v["qkv"], v["out"], norm2_grad, v["fc"], v["proj"]


def solution(mesh):
    block = P("dp", "seq", None)
    return jax.shard_map(
        functools.partial(per_device, (mesh.shape["dp"], mesh.shape["seq"])),
        mesh=mesh,
        in_specs=(block, P(), P(), P(), P(), P(), P(), P("dp"), P(), block),
        out_specs=(block, block, P(), P(), P(), P(), P(), P()),
        check_vma=False,
    )
```

```python
import functools
import math

import jax
import jax.numpy as jnp
from jax import lax
from jax.experimental import pallas as pl
from jax.experimental.pallas import tpu as pltpu
from jax.sharding import PartitionSpec as P

HEADS = 6
EPSILON = 1e-05
NEGATIVE = -1e30
BF = jnp.bfloat16
F32 = jnp.float32
ALL = ("dp", "seq")
LANES = 128
GAIN_ROWS = 16
SCHEDULE = """
BA1a BA1b A BT BF A B A C BA0a BA0b A B BE C B D A C B D A C D B C D SG B C D A B C D A PG D C B D
"""
MB = 1024 * 1024
VMEM = pltpu.VMEM
SMEM = pltpu.SMEM


def mm(a, b):
    return lax.dot_general(a, b, (((1,), (0,)), ((), ())), preferred_element_type=F32)


def mm_t(a, b):
    return lax.dot_general(a, b, (((1,), (1,)), ((), ())), preferred_element_type=F32)


def t_mm(a, b):
    return lax.dot_general(a, b, (((0,), (0,)), ((), ())), preferred_element_type=F32)


class Order:
    def __init__(self):
        self.last = []

    def after(self, x):
        x, *last = lax.optimization_barrier((x, *self.last))
        self.last = last[-1:]
        return x

    def add(self, result):
        self.last = [result, *self.last]


def call(body, name, ins, outs, scratch=(), limit=16, flops=0, transcendentals=0, grid=(1,), aliases=None, order=None):
    moved = sum(math.prod(o[0]) * jnp.dtype(o[1]).itemsize for o in outs)
    moved += sum(a.size * a.dtype.itemsize for a, _ in ins)
    kernel = body
    if order is not None:
        count, more = len(ins), len(order.last)
        ins = [*ins, *((x, pl.BlockSpec(memory_space=pl.ANY)) for x in order.last)]
        order.last = []
        results_at = count + more + len(outs)
        outs = [*outs, ((8, LANES), F32, whole(8, LANES))]

        def kernel(*refs):
            body(*refs[:count], *refs[count + more : results_at], *refs[results_at + 1 :])
            refs[results_at][...] = jnp.zeros((8, LANES), F32)

    results = pl.pallas_call(
        kernel,
        out_shape=[pltpu.HBM(o[0], o[1]) if len(o) > 3 else jax.ShapeDtypeStruct(o[0], o[1]) for o in outs],
        grid=grid,
        in_specs=[s for _, s in ins],
        out_specs=[o[2] for o in outs],
        scratch_shapes=list(scratch),
        input_output_aliases=aliases or {},
        compiler_params=pltpu.CompilerParams(vmem_limit_bytes=limit * MB),
        cost_estimate=pl.CostEstimate(flops=flops, bytes_accessed=moved, transcendentals=transcendentals),
        name=name,
    )(*[a for a, _ in ins])
    if order is not None:
        *results, token = results
        order.add(token)
    return results


def whole(*shape):
    return pl.BlockSpec(shape, lambda *_: (0,) * len(shape))


def layer_of(index, *shape):
    return pl.BlockSpec((None,) + shape, lambda *_: (index,) + (0,) * len(shape))


def in_hbm(x):
    return pltpu.with_memory_space_constraint(x, pltpu.HBM), pl.BlockSpec(memory_space=pltpu.HBM)


def scalars():
    return pl.BlockSpec(memory_space=SMEM)


def norm_parts(values):
    centre = jnp.mean(values, axis=-1, keepdims=True)
    centred = values - centre
    spread = jnp.mean(centred * centred, axis=-1, keepdims=True)
    inverse = lax.rsqrt(spread + EPSILON)
    return centred * inverse, inverse


def norm_back(grad, zhat, inverse, gain):
    e = grad * gain
    return inverse * (
        e
        - jnp.mean(e, axis=-1, keepdims=True)
        - zhat * jnp.mean(e * zhat, axis=-1, keepdims=True)
    )


def qkv_step(hidden, gain, weight, a_ref, q_ref, kv_ref, scale):
    zhat, _ = norm_parts(hidden)
    a = (zhat * gain).astype(BF)
    a_ref[...] = a
    packed = mm(a, weight).astype(BF)
    width = a.shape[1]
    q_ref[...] = packed[:, :width] * jnp.asarray(scale, BF)
    kv_ref[...] = packed[:, width:]


def first_body(scale, ha_ref, hb_ref, gain_ref, w_ref, h_ref, a_ref, q_ref, kv_ref):
    span = ha_ref.shape[0]
    h_ref[:span] = ha_ref[...].astype(F32)
    h_ref[span:] = hb_ref[...].astype(F32)
    qkv_step(h_ref[...], gain_ref[0:1], w_ref[...], a_ref, q_ref, kv_ref, scale)


def attend_body(block, info_ref, q_ref, ko_ref, vo_ref, kx_ref, vx_ref, bo_ref, bx_ref, hot_ref, p_ref, att_ref, inv_ref):
    tokens = q_ref.shape[0]
    head = LANES // 2
    ones = jnp.ones((tokens, LANES), BF)

    def beside(a, b):
        return jnp.concatenate([a, b], axis=1)

    keys = jnp.concatenate([beside(ko_ref[...], bo_ref[...]), beside(kx_ref[...], bx_ref[...])], axis=0)
    values = jnp.concatenate([beside(vo_ref[...], ones), beside(vx_ref[...], ones)], axis=0)
    lower = lax.broadcasted_iota(jnp.int32, (tokens, LANES), 1) < head
    at_q = lax.broadcasted_iota(jnp.int32, (block, block), 0)
    at_k = lax.broadcasted_iota(jnp.int32, (block, block), 1)
    prefix = info_ref[0]
    q = q_ref[...]
    scores = []
    for n in range(2):
        qn = jnp.where(lower if n == 0 else ~lower, q, jnp.zeros_like(q))
        scores.append(mm_t(beside(qn, hot_ref[...]), keys))
    chances = []
    for n in range(2):
        rows = []
        for t in range(tokens // block):
            s = scores[n][t * block : (t + 1) * block]
            seen = (at_k <= at_q) | (info_ref[1 + t] * block + at_k < prefix)
            pieces = [s[:, : t * block], jnp.where(seen, s[:, t * block : (t + 1) * block], NEGATIVE), s[:, (t + 1) * block :]]
            s = jnp.concatenate([piece for piece in pieces if piece.shape[1]], axis=1)
            rows.append(jnp.exp(s - jnp.max(s, axis=1, keepdims=True)).astype(BF))
        p = jnp.concatenate(rows, axis=0)
        p_ref[n] = p
        chances.append(p)
    even, odd = [mm(p, values) for p in chances]
    inverse = 1.0 / jnp.where(lower, even[:, LANES:], odd[:, LANES:])
    inv_ref[...] = inverse
    att_ref[...] = (jnp.where(lower, even[:, :LANES], odd[:, :LANES]) * inverse).astype(BF)


def feed(h_ref, att_ref, wout_ref, gain, wfc_ref, wproj_ref, mid_ref, sec_ref, act_ref, gp_ref):
    middle = h_ref[...] + mm(att_ref[...], wout_ref[...])
    mid_ref[...] = middle
    zhat, _ = norm_parts(middle)
    second = (zhat * gain).astype(BF)
    sec_ref[...] = second
    total = middle
    width = middle.shape[1]
    for j in range(wfc_ref.shape[1] // width):
        cols = slice(j * width, (j + 1) * width)
        lifted = mm(second, wfc_ref[:, cols])
        phi = 0.5 * (1.0 + lax.erf(lifted * (1.0 / math.sqrt(2.0))))
        slope = phi + lifted * jnp.exp(-0.5 * lifted * lifted) * (1.0 / math.sqrt(2.0 * math.pi))
        gp_ref[:, cols] = slope.astype(BF)
        act = (lifted * phi).astype(BF)
        act_ref[:, cols] = act
        total = total + mm(act, wproj_ref[cols, :])
    return total


def middle_body(scale, layer, h_ref, att_ref, wout_ref, g2_ref, wfc_ref, wproj_ref, g1_ref, wqkv_ref,
                mid_ref, sec_ref, act_ref, gp_ref, out_ref, a_ref, q_ref, kv_ref):
    out = feed(h_ref, att_ref, wout_ref, g2_ref[layer : layer + 1], wfc_ref, wproj_ref, mid_ref, sec_ref, act_ref, gp_ref)
    out_ref[...] = out
    qkv_step(out, g1_ref[layer + 1 : layer + 2], wqkv_ref[...], a_ref, q_ref, kv_ref, scale)


def relative(bits, index, core):
    place = 0
    for mine, others in bits:
        place = 2 * place + (jnp.where(core == 0, index >> mine, index >> others) & 1)
    return place


def hand_out(bits, at_ref, g_ref, keep_ref, send_ref):
    index = at_ref[0]
    core = index & 1
    count = keep_ref.shape[0]
    for ref, side in ((keep_ref, core), (send_ref, 1 - core)):
        place = relative(bits, index, side)
        for i in range(count):
            ref[i] = g_ref[side * count + (place ^ i)]


def put_rows(g_ref, at, values, first=0, total=None):
    share = (total or values.shape[0]) // g_ref.shape[0]
    done = 0
    while done < values.shape[0]:
        block, row = divmod(first + done, share)
        count = min(share - row, values.shape[0] - done)
        g_ref[block, at + row : at + row + count] = values[done : done + count]
        done += count


def back_proj(upstream, act_ref, gp_ref, wproj_ref, g_ref, at, lift_ref):
    down = upstream.astype(BF)
    width = down.shape[1]
    for j in range(act_ref.shape[1] // width):
        cols = slice(j * width, (j + 1) * width)
        put_rows(g_ref, at, t_mm(act_ref[:, cols], down).astype(BF), j * width, act_ref.shape[1])
        lift_ref[:, cols] = (mm_t(down, wproj_ref[cols, :]) * gp_ref[:, cols].astype(F32)).astype(BF)


def back_fc(upstream, lift_ref, sec_ref, mid_ref, att_ref, wfc_ref, wout_ref, gain, g_ref, at, mg_ref, ag_ref, gain_ref):
    second = sec_ref[...]
    width = second.shape[1]
    inner = lift_ref.shape[1]
    second_grad = None
    for j in range(inner // width):
        cols = slice(j * width, (j + 1) * width)
        lift = lift_ref[:, cols]
        put_rows(g_ref, at + j * width // g_ref.shape[0], t_mm(second, lift).astype(BF))
        term = mm_t(lift, wfc_ref[:, cols])
        second_grad = term if second_grad is None else second_grad + term
    zhat, inverse = norm_parts(mid_ref[...])
    gain_ref[...] = jnp.broadcast_to(jnp.sum(second_grad * zhat, axis=0, keepdims=True), gain_ref.shape)
    mg = upstream + norm_back(second_grad, zhat, inverse, gain)
    mg_ref[...] = mg
    branch = mg.astype(BF)
    put_rows(g_ref, at + inner // g_ref.shape[0], t_mm(att_ref[...], branch).astype(BF))
    ag_ref[...] = mm_t(branch, wout_ref[...]).astype(BF)


def turn_body(layer, bits, core_ref, h_ref, att_ref, wout_ref, g2_ref, wfc_ref, wproj_ref, ua_ref, ub_ref,
              oa_ref, ob_ref, keep_ref, send_ref, mg_ref, ag_ref, gain_ref,
              mid_ref, sec_ref, act_ref, gp_ref, lift_ref, g_ref):
    gain = g2_ref[layer : layer + 1]
    out = feed(h_ref, att_ref, wout_ref, gain, wfc_ref, wproj_ref, mid_ref, sec_ref, act_ref, gp_ref)
    span = oa_ref.shape[0]
    oa_ref[...] = out[:span].astype(BF)
    ob_ref[...] = out[span:].astype(BF)
    upstream = jnp.concatenate([ua_ref[...], ub_ref[...]], axis=0).astype(F32)
    back_proj(upstream, act_ref, gp_ref, wproj_ref, g_ref, 0, lift_ref)
    back_fc(upstream, lift_ref, sec_ref, mid_ref, att_ref, wfc_ref, wout_ref, gain, g_ref, act_ref.shape[1] // g_ref.shape[0],
            mg_ref, ag_ref, gain_ref)
    hand_out(bits, core_ref, g_ref, keep_ref, send_ref)


def back_fc_body(layer, bits, core_ref, u_ref, lift_ref, sec_ref, mid_ref, att_ref, wfc_ref, wout_ref, g2_ref,
                 keep_ref, send_ref, mg_ref, ag_ref, gain_ref, g_ref):
    back_fc(u_ref[...], lift_ref, sec_ref, mid_ref, att_ref, wfc_ref, wout_ref, g2_ref[layer : layer + 1], g_ref, 0,
            mg_ref, ag_ref, gain_ref)
    hand_out(bits, core_ref, g_ref, keep_ref, send_ref)


def back_attend_body(scale, q_ref, ko_ref, vo_ref, kx_ref, vx_ref, p_ref, att_ref, inv_ref, ag_ref,
                     dq_ref, own_ref, oth_ref):
    tokens = q_ref.shape[0]
    head = LANES // 2
    lower = lax.broadcasted_iota(jnp.int32, (tokens, LANES), 1) < head
    q = q_ref[...]
    scaled = ag_ref[...].astype(F32) * inv_ref[...]
    product = scaled * att_ref[...].astype(F32)
    keys = jnp.concatenate([ko_ref[...], kx_ref[...]], axis=0)
    values = jnp.concatenate([vo_ref[...], vx_ref[...]], axis=0)
    dq = dk = dv = None
    for n in range(2):
        mine = lower if n == 0 else ~lower
        qn = jnp.where(mine, q, jnp.zeros_like(q))
        gn = jnp.where(mine, scaled, 0.0).astype(BF)
        delta = jnp.sum(jnp.where(mine, product, 0.0), axis=1, keepdims=True)
        p = p_ref[n]
        ds = (p.astype(F32) * (mm_t(gn, values) - delta)).astype(BF)
        dqn, dkn, dvn = mm(ds, keys), t_mm(qn, ds), t_mm(gn, p)
        if n == 0:
            dq, dk, dv = dqn, dkn, dvn
        else:
            dq, dk, dv = jnp.where(lower, dq, dqn), dk + dkn, dv + dvn
    dq_ref[...] = (dq * scale).astype(BF)
    for i, grad in enumerate((dk.T, dv.T)):
        own_ref[i] = grad[:tokens]
        oth_ref[i] = grad[tokens:].astype(BF)


def back_qkv(layer, parts, a_ref, h_ref, g1_ref, w_ref, mg_ref, g_ref):
    a = a_ref[...]
    width = a.shape[1]
    blocks = [jnp.concatenate([dq[...] for dq, _, _ in parts], axis=1)]
    for i in range(2):
        blocks.append(jnp.concatenate([(own[i] + got[i].astype(F32)).astype(BF) for _, own, got in parts], axis=1))
    grad = None
    for j, block in enumerate(blocks):
        put_rows(g_ref, j * width // g_ref.shape[0], t_mm(a, block).astype(BF))
        term = mm_t(block, w_ref[:, j * width : (j + 1) * width])
        grad = term if grad is None else grad + term
    zhat, inverse = norm_parts(h_ref[...])
    gain_grad = jnp.sum(grad * zhat, axis=0, keepdims=True)
    return mg_ref[...] + norm_back(grad, zhat, inverse, g1_ref[layer : layer + 1]), gain_grad


def back_turn_body(layer, bits, core_ref, *refs):
    parts, refs = (refs[:3], refs[3:6]), refs[6:]
    (a_ref, h_ref, g1_ref, w_ref, mg_ref, act_ref, gp_ref, wproj_ref,
     keep_ref, send_ref, up_ref, gain_ref, lift_ref, g_ref) = refs
    up, gain_grad = back_qkv(layer, parts, a_ref, h_ref, g1_ref, w_ref, mg_ref, g_ref)
    gain_ref[...] = jnp.broadcast_to(gain_grad, gain_ref.shape)
    up_ref[...] = up
    back_proj(up, act_ref, gp_ref, wproj_ref, g_ref, 3 * up.shape[1] // g_ref.shape[0], lift_ref)
    hand_out(bits, core_ref, g_ref, keep_ref, send_ref)


def back_both_body(layer, bits, core_ref, *refs):
    parts, refs = (refs[:3], refs[3:6]), refs[6:]
    (a_ref, h_ref, g1_ref, w_ref, mg_ref, act_ref, gp_ref, wproj_ref, sec_ref, mid_ref, att_ref, wfc_ref, wout_ref, g2_ref,
     keep_ref, send_ref, mg_out, ag_ref, gain1_ref, gain2_ref, g_ref, up_ref, lift_ref) = refs
    up, gain_grad = back_qkv(layer, parts, a_ref, h_ref, g1_ref, w_ref, mg_ref, g_ref)
    gain1_ref[...] = jnp.broadcast_to(gain_grad, gain1_ref.shape)
    up_ref[...] = up
    at = 3 * up.shape[1]
    back_proj(up, act_ref, gp_ref, wproj_ref, g_ref, at // g_ref.shape[0], lift_ref)
    at += act_ref.shape[1]
    back_fc(up_ref[...], lift_ref, sec_ref, mid_ref, att_ref, wfc_ref, wout_ref, g2_ref[layer - 1 : layer], g_ref, at // g_ref.shape[0],
            mg_out, ag_ref, gain2_ref)
    hand_out(bits, core_ref, g_ref, keep_ref, send_ref)


def back_end_body(layer, bits, core_ref, *refs):
    parts, refs = (refs[:3], refs[3:6]), refs[6:]
    (a_ref, h_ref, g1_ref, w_ref, mg_ref, oa_ref, ob_ref, *gain_refs, keep_ref, send_ref, to_a_ref, to_b_ref, g_ref) = refs
    up, gain_grad = back_qkv(layer, parts, a_ref, h_ref, g1_ref, w_ref, mg_ref, g_ref)
    span = oa_ref.shape[0]
    width = up.shape[1]
    to_a_ref[0] = oa_ref[...]
    to_b_ref[0] = ob_ref[...]
    to_a_ref[1] = up[:span].astype(BF)
    to_b_ref[1] = up[span:].astype(BF)
    at = 3 * width // g_ref.shape[0]
    for i, gain in enumerate([gain_grad] + [ref[0:1] for ref in gain_refs]):
        put_rows(g_ref, at + i, jnp.broadcast_to(gain, (g_ref.shape[0], width)).astype(BF))
    at += 1 + len(gain_refs)
    for block in range(g_ref.shape[0]):
        g_ref[block, at:] = jnp.zeros((g_ref.shape[1] - at, width), BF)
    hand_out(bits, core_ref, g_ref, keep_ref, send_ref)


def masks_body(per_span, block, ids_ref, order_ref, own_ref, other_ref, w_in, g_in, bias_ref, hot_ref, info_ref, w_ref, g_ref, sem):
    copies = [pltpu.make_async_copy(w_in.at[0], w_ref, sem.at[0]), pltpu.make_async_copy(g_in, g_ref, sem.at[1])]
    for copy in copies:
        copy.start()
    core, place = ids_ref[0] & 1, ids_ref[1]
    odd = place & 1
    prefix = jnp.where((place >> 1) == core, own_ref[odd], other_ref[odd])
    info_ref[0] = prefix
    ranks = []
    for c in (core, 1 - core):
        for span in (2 * c + odd, 2 * c + 1 - odd):
            ranks += [order_ref[span * per_span + i] for i in range(per_span)]
    tokens = hot_ref.shape[0]
    own = tokens // block
    lane = lax.broadcasted_iota(jnp.int32, (block, LANES), 1)
    within = lax.broadcasted_iota(jnp.int32, (block, LANES), 0)
    lane_rank = jnp.full((block, LANES), -1, jnp.int32)
    for b in range(own):
        info_ref[1 + b] = ranks[b]
        lane_rank = jnp.where(lane == b, ranks[b], lane_rank)
        hot_ref[b * block : (b + 1) * block] = jnp.where(lane == b, 1.0, 0.0).astype(BF)
    for k, rank in enumerate(ranks):
        unseen = (lane < own) & (rank >= lane_rank) & (lane != k) & (rank * block + within >= prefix)
        bias_ref[k * block : (k + 1) * block] = jnp.where(unseen, NEGATIVE, 0.0).astype(BF)
    for copy in copies:
        copy.wait()


def pick_body(at_ref, x_ref, a_ref, b_ref):
    odd = at_ref[1] & 1
    a_ref[...] = x_ref[odd]
    b_ref[...] = x_ref[1 - odd]


def place_body(odd_ref, a_ref, b_ref, *out_refs):
    odd = odd_ref[1] & 1
    for i, ref in enumerate(out_refs):
        ref[odd] = a_ref[i]
        ref[1 - odd] = b_ref[i]


def add(a, b):
    return (a.astype(F32) + b.astype(F32)).astype(BF)


def unpack_body(plan, gains, bits, at_ref, a_ref, b_ref, *refs):
    *refs, sem = refs
    stage_refs = refs[len(refs) - len(plan) :]
    out_refs = refs[len(refs) - 2 * len(plan) - len(gains) : len(refs) - len(plan)]
    index = at_ref[0]
    core = index & 1
    count, _, width = a_ref.shape
    copies = []
    for ref, side in ((a_ref, core), (b_ref, 1 - core)):
        place = relative(bits, index, side)
        for i in range(count):
            block = side * count + (place ^ i)
            for (at, layer), out_ref, stage_ref in zip(plan, out_refs, stage_refs):
                _, rows, cols = stage_ref.shape
                for j in range(cols // width):
                    stage_ref[block, :, j * width : (j + 1) * width] = ref[i, at + j * rows : at + (j + 1) * rows].astype(F32)
                copies.append(pltpu.make_async_copy(stage_ref.at[block], out_ref.at[layer, block], sem.at[len(copies)]))
                copies[-1].start()
    for rows, ref in zip(gains, out_refs[len(plan) :]):
        ref[...] = jnp.concatenate([a_ref[0, row : row + 1] for row in rows], axis=0).astype(F32)
    for copy in copies:
        copy.wait()


def unpack(bits, at, halves, layers, parts, gains, order):
    ins = [(at, scalars())] + [(x, whole(*x.shape)) for x in halves]
    aliases = {}
    outs = []
    count, _, width = halves[0].shape
    blocks = 2 * count
    for i, (_, layer, shape, before) in enumerate(parts):
        if before is not None:
            aliases[len(ins)] = i
            ins.append((before, pl.BlockSpec(memory_space=pltpu.HBM)))
        outs.append(((layers, blocks, shape[0] // blocks, shape[1]), F32, pl.BlockSpec(memory_space=pltpu.HBM), True))
    outs += [((len(rows), width), F32, whole(len(rows), width)) for rows in gains]
    return call(
        functools.partial(unpack_body, [p[:2] for p in parts], gains, bits), "unpack", ins, outs,
        scratch=[VMEM((blocks, p[2][0] // blocks, p[2][1]), F32) for p in parts] + [pltpu.SemaphoreType.DMA((blocks * len(parts),))],
        limit=20, aliases=aliases, order=order,
    )


def per_device(mesh_shape, hidden_in, norm1_gain, qkv_weight, out_weight, norm2_gain, fc_weight, proj_weight,
               prefix_len, block_order, grad_out):
    dp, seq = mesh_shape
    rows_here, span, width = hidden_in.shape
    layers = qkv_weight.shape[0]
    inner = fc_weight.shape[2]
    scale = 1.0 / math.sqrt(width // HEADS)
    row_length = span * seq
    block_count = block_order.shape[0]
    block = row_length // block_count
    per_span = span // block
    tokens = 2 * span
    pairs = width // LANES
    assert rows_here == 2 and seq == 4 and dp % 2 == 0 and layers == 2
    di, si = lax.axis_index("dp"), lax.axis_index("seq")
    at = jnp.stack([di, si]).astype(jnp.int32)
    order = Order()

    def spot(d, s):
        return d * seq + s

    perm_a = [(spot(d, s), spot((d & ~1) | (s >> 1), 2 * (d & 1) + (s & 1))) for d in range(dp) for s in range(seq)]
    perm_b = [(spot(d, s), spot((d & ~1) | (s >> 1), 2 * (d & 1) + 1 - (s & 1))) for d in range(dp) for s in range(seq)]
    back_a = [(b, a) for a, b in perm_a]
    back_b = [(b, a) for a, b in perm_b]
    pair_perm = [(spot(d, s), spot(d ^ 1, s)) for d in range(dp) for s in range(seq)]
    t_w = (tokens, width)
    full = whole(*t_w)
    half_spec = whole(span, width)
    both_spec = whole(2, span, width)

    def pair(x):
        return lax.ppermute(x, ALL, pair_perm)

    def spread(x, order):
        first, other = call(
            pick_body, "pick", [(at, scalars()), (x, both_spec)], [((span, width), BF, half_spec)] * 2, limit=4, order=order
        )
        return lax.ppermute(first, ALL, perm_a), lax.ppermute(other, ALL, perm_b)

    class Collect:
        def __init__(self, a, b):
            self.a, self.b = lax.ppermute(a, ALL, back_a), lax.ppermute(b, ALL, back_b)

        def done(self, order):
            return call(
                place_body, "place", [(at, scalars()), (self.a, both_spec), (self.b, both_spec)],
                [((2, span, width), BF, both_spec, True)] * 2, limit=8, order=order,
            )

    dp_bits = [i for i in range(1, dp.bit_length() - 1)]
    seq_bits = [i for i in range(seq.bit_length() - 1)]
    orders = (dp_bits, dp_bits[::-1])
    z_orders = (seq_bits, seq_bits[::-1])
    bits = list(zip(*orders))
    blocks = 2 ** (len(dp_bits) + 1)

    own_blocks = tokens // block
    ha, hb = spread(hidden_in, order)
    prefix_other = pair(prefix_len)
    bias, hot, info, first_weight, first_gain = call(
        functools.partial(masks_body, per_span, block), "masks",
        [(at, scalars()), (block_order, scalars()), (prefix_len, scalars()), (prefix_other, scalars()),
         in_hbm(qkv_weight), in_hbm(norm1_gain)],
        [((2 * tokens, LANES), BF, whole(2 * tokens, LANES)), ((tokens, LANES), BF, whole(tokens, LANES)),
         ((1 + own_blocks,), jnp.int32, scalars()),
         ((width, 3 * width), BF, whole(width, 3 * width)), ((layers, width), F32, whole(layers, width))],
        scratch=[pltpu.SemaphoreType.DMA((2,))], order=order,
    )

    wide = whole(tokens, inner)
    gains = whole(layers, width)
    dense = 2 * tokens * width

    def qkv_out():
        return [(t_w, BF, full), (t_w, BF, full), ((tokens, 2 * width), BF, whole(tokens, 2 * width))]

    h, a, q, kv = call(
        functools.partial(first_body, scale), "first",
        [(ha, half_spec), (hb, half_spec), (first_gain, gains), (first_weight, whole(width, 3 * width))],
        [(t_w, F32, full)] + qkv_out(),
        flops=dense * 3 * width, order=order,
    )
    lane_block = pl.BlockSpec((tokens, LANES), lambda p: (0, p))
    lane_block_v = pl.BlockSpec((tokens, LANES), lambda p: (0, p + pairs))
    p_spec = pl.BlockSpec((2, tokens, 2 * tokens), lambda p: (p, 0, 0))

    def attend(q, kv, kv_other):
        return call(
            functools.partial(attend_body, block), "attend",
            [(info, scalars()), (q, lane_block), (kv, lane_block), (kv, lane_block_v), (kv_other, lane_block), (kv_other, lane_block_v),
             (bias, pl.BlockSpec((tokens, LANES), lambda p: (0, 0))), (bias, pl.BlockSpec((tokens, LANES), lambda p: (1, 0))),
             (hot, whole(tokens, LANES))],
            [((HEADS, tokens, 2 * tokens), BF, p_spec), (t_w, BF, lane_block), (t_w, F32, lane_block)],
            grid=(pairs,), flops=4 * tokens * 2 * tokens * 256 * HEADS, transcendentals=HEADS * tokens * 2 * tokens,
            limit=14, order=order,
        )

    def feed_ins(layer, h, att):
        return [
            (h, full), (att, full), (out_weight, layer_of(layer, width, width)), (norm2_gain, gains),
            (fc_weight, layer_of(layer, width, inner)), (proj_weight, layer_of(layer, inner, width)),
        ]

    def swap_dp(x, step):
        return lax.ppermute(x, ALL, [(spot(d, s), spot(d ^ (1 << orders[d & 1][step]), s)) for d in range(dp) for s in range(seq)])

    def swap_seq(x, step):
        return lax.ppermute(x, ALL, [(spot(d, s), spot(d, s ^ (1 << z_orders[d & 1][step]))) for d in range(dp) for s in range(seq)])

    class Bucket:
        def __init__(self, keep, send):
            self.halves = None
            self.parts = None
            self.steps = self.run(keep, send)
            next(self.steps)

        def run(self, keep, send):
            got = pair(send)
            for step in range(len(dp_bits)):
                yield
                total = add(keep, order.after(got))
                half = total.shape[0] // 2
                keep, send = total[:half], total[half:]
                order.add(keep)
                got = swap_dp(send, step)
            self.parts = [(keep, got)]
            yield
            yield from self.rest()

        def rest(self):
            total = jnp.concatenate([add(keep, order.after(got)) for keep, got in self.parts], axis=1)
            order.add(total)
            for step in range(len(seq_bits)):
                got = swap_seq(total, step)
                yield
                total = add(total, order.after(got))
                order.add(total)
            for step in reversed(range(len(dp_bits))):
                got = swap_dp(total, step)
                yield
                total = jnp.concatenate([total, order.after(got)], axis=0)
                order.add(total)
            self.halves = (total, pair(total))
            yield

        def step(self):
            next(self.steps)

    class Joined(Bucket):
        def __init__(self, *buckets):
            self.halves = None
            self.parts = [part for bucket in buckets for part in bucket.parts]
            self.steps = self.rest()

    def bucket_outs(rows):
        count = 2 ** len(dp_bits)
        size = rows // (2 * count)
        assert size * 2 * count == rows
        return [((count, size, width), BF, whole(count, size, width))] * 2, [VMEM((2 * count, size, width), BF)]

    gain_out = ((8, width), F32, whole(8, width))

    kv_other = pair(kv)
    ua, ub = spread(grad_out, order)
    p, att, inv = attend(q, kv, kv_other)
    order.last += [ua, ub]
    mid, sec, act, gp, h_next, a_next, q_next, kv_next = call(
        functools.partial(middle_body, scale, 0), "middle",
        feed_ins(0, h, att) + [(norm1_gain, gains), (qkv_weight, layer_of(1, width, 3 * width))],
        [(t_w, F32, full), (t_w, BF, full), ((tokens, inner), BF, wide), ((tokens, inner), BF, wide), (t_w, F32, full)] + qkv_out(),
        flops=dense * (4 * width + 2 * inner), transcendentals=2 * tokens * inner, limit=18, order=order,
    )
    saved = (h, a, q, kv, kv_other, p, att, inv)
    h, a, q, kv = h_next, a_next, q_next, kv_next

    kv_other = pair(kv)
    p, att, inv = attend(q, kv, kv_other)
    outs, scratch = bucket_outs(2 * inner + width)
    oa, ob, keep, send, mg, ag, gain2_1 = call(
        functools.partial(turn_body, 1, bits), "turn",
        [(at, scalars())] + feed_ins(1, h, att) + [(ua, half_spec), (ub, half_spec)],
        [((span, width), BF, half_spec)] * 2 + outs + [(t_w, F32, full), (t_w, BF, full), gain_out],
        scratch=[VMEM(t_w, F32), VMEM(t_w, BF)] + [VMEM((tokens, inner), BF)] * 3 + scratch,
        flops=dense * (3 * width + 6 * inner), transcendentals=2 * tokens * inner, limit=24, order=order,
    )
    feed_1 = Bucket(keep, send)

    def back_attend(first, count, q, kv, kv_other, p, att, inv, ag):
        spec = pl.BlockSpec((tokens, LANES), lambda p: (0, p + first))
        spec_v = pl.BlockSpec((tokens, LANES), lambda p: (0, p + first + pairs))
        out = (tokens, count * LANES)
        pair_out = pl.BlockSpec((2, tokens, LANES), lambda p: (0, 0, p))
        dq, own, oth = call(
            functools.partial(back_attend_body, scale), "back_attend",
            [(q, spec), (kv, spec), (kv, spec_v), (kv_other, spec), (kv_other, spec_v),
             (p, pl.BlockSpec((2, tokens, 2 * tokens), lambda p: (p + first, 0, 0))), (att, spec), (inv, spec), (ag, spec)],
            [(out, BF, lane_block), ((2, *out), F32, pair_out), ((2, *out), BF, pair_out)],
            grid=(count,), flops=8 * tokens * 2 * tokens * 256 * 2 * count, limit=14, order=order,
        )
        return dq, own, pair(oth)

    def part_ins(parts):
        return [(x, whole(*x.shape)) for part in parts for x in part]

    layer_1 = (q, kv, kv_other, p, att, inv)
    h_1, a_1, mg_1, ag_1 = h, a, mg, ag
    h_0, a_0, *layer_0 = saved
    v = {}
    buckets = {"A": feed_1}

    def back_turn():
        outs, scratch = bucket_outs(3 * width + inner)
        keep, send, v["up"], v["gain1_1"], v["lift"] = call(
            functools.partial(back_turn_body, 1, bits), "back_turn",
            [(at, scalars())] + part_ins((v["1a"], v["1b"])) + [
                (a_1, full), (h_1, full), (norm1_gain, gains), (qkv_weight, layer_of(1, width, 3 * width)), (mg_1, full),
                (act, wide), (gp, wide), (proj_weight, layer_of(0, inner, width))],
            outs + [(t_w, F32, full), gain_out, ((tokens, inner), BF, wide)],
            scratch=scratch, flops=dense * (6 * width + 2 * inner), limit=18, order=order,
        )
        buckets["B"] = Bucket(keep, send)

    def back_fc_0():
        outs, scratch = bucket_outs(inner + width)
        keep, send, v["mg"], v["ag"], v["gain2_0"] = call(
            functools.partial(back_fc_body, 0, bits), "back_fc",
            [(at, scalars()), (v["up"], full), (v["lift"], wide), (sec, full), (mid, full), (layer_0[4], full),
             (fc_weight, layer_of(0, width, inner)), (out_weight, layer_of(0, width, width)), (norm2_gain, gains)],
            outs + [(t_w, F32, full), (t_w, BF, full), gain_out],
            scratch=scratch, flops=dense * (2 * width + 2 * inner), limit=16, order=order,
        )
        buckets["C"] = Bucket(keep, send)

    def back_both():
        outs, scratch = bucket_outs(4 * width + 2 * inner)
        keep, send, v["mg"], v["ag"], v["gain1_1"], v["gain2_0"] = call(
            functools.partial(back_both_body, 1, bits), "back_both",
            [(at, scalars())] + part_ins((v["1a"], v["1b"])) + [
                (a_1, full), (h_1, full), (norm1_gain, gains), (qkv_weight, layer_of(1, width, 3 * width)), (mg_1, full),
                (act, wide), (gp, wide), (proj_weight, layer_of(0, inner, width)), (sec, full), (mid, full), (layer_0[4], full),
                (fc_weight, layer_of(0, width, inner)), (out_weight, layer_of(0, width, width)), (norm2_gain, gains)],
            outs + [(t_w, F32, full), (t_w, BF, full), gain_out, gain_out],
            scratch=scratch + [VMEM(t_w, F32), VMEM((tokens, inner), BF)], flops=dense * (8 * width + 4 * inner), limit=24, order=order,
        )
        v["both"] = True
        buckets["B"] = Bucket(keep, send)

    def back_end():
        outs, scratch = bucket_outs(3 * width + GAIN_ROWS * blocks)
        keep, send, ga, gb = call(
            functools.partial(back_end_body, 0, bits), "back_end",
            [(at, scalars())] + part_ins((v["0a"], v["0b"])) + [
                (a_0, full), (h_0, full), (norm1_gain, gains), (qkv_weight, layer_of(0, width, 3 * width)), (v["mg"], full),
                (oa, half_spec), (ob, half_spec)]
            + [(g, whole(8, width)) for g in (v["gain1_1"], v["gain2_0"], gain2_1)],
            outs + [((2, span, width), BF, both_spec)] * 2,
            scratch=scratch, flops=2 * dense * 3 * width, limit=12, order=order,
        )
        buckets["D"] = Bucket(keep, send)
        v["ga"], v["gb"] = ga, gb

    def run_part(name, first, count, layer, ag):
        v[name] = back_attend(first, count, *layer, ag)

    def unpacked(name):
        bucket = buckets[name]
        if name == "A":
            parts = [(0, 1, (inner, width), "proj"), (inner, 1, (width, inner), "fc"), (2 * inner, 1, (width, width), "out")]
        elif name == "B":
            parts = [(0, 1, (width, 3 * width), "qkv"), (3 * width, 0, (inner, width), "proj")]
            if "both" in v:
                at_fc = 3 * width + inner
                parts += [(at_fc, 0, (width, inner), "fc"), (at_fc + inner, 0, (width, width), "out")]
        else:
            parts = [(0, 0, (width, inner), "fc"), (inner, 0, (width, width), "out")] if name != "D" else []
            if name != "C":
                parts.append(((inner + width) * len(parts) // 2, 0, (width, 3 * width), "qkv"))
        gain_row = (sum(part[2][0] * part[2][1] for part in parts) // width) // blocks
        gain_rows = [[gain_row + i for i in pair] for pair in ((0, 1), (2, 3))] if name in "DE" else []
        got = unpack(bits, at, bucket.halves, layers, [(part[0] // blocks, *part[1:3], v.get(part[3])) for part in parts], gain_rows, order)
        for part, array in zip(parts, got):
            v[part[3]] = array
        if gain_rows:
            v["gains"] = got[len(parts) : len(parts) + 2]

    def bucket_step(name):
        if name == "E" and name not in buckets and "C" in buckets and "D" in buckets:
            for part in "CD":
                while buckets[part].parts is None:
                    buckets[part].step()
            buckets["E"] = Joined(buckets.pop("C"), buckets.pop("D"))
        if name in buckets:
            if buckets[name].halves is None:
                buckets[name].step()
            else:
                unpacked(name)
                del buckets[name]

    kernels = {
        "BA1a": lambda: run_part("1a", 0, 1, layer_1, ag_1),
        "BA1b": lambda: run_part("1b", 1, pairs - 1, layer_1, ag_1),
        "BT": back_turn,
        "BF": back_fc_0,
        "BTF": back_both,
        "BA0a": lambda: run_part("0a", 0, 1, layer_0, v["ag"]),
        "BA0b": lambda: run_part("0b", 1, pairs - 1, layer_0, v["ag"]),
        "BE": back_end,
        "SG": lambda: v.update(home=Collect(order.after(v["ga"]), order.after(v["gb"]))),
        "PG": lambda: v.update(home=v["home"].done(order)),
    }
    for token in SCHEDULE.split():
        if token in kernels:
            kernels[token]()
        else:
            bucket_step(token)
    while buckets:
        for name in "ABCDE":
            if name in buckets:
                bucket_step(name)
    norm1_grad, norm2_grad = v["gains"]
    qkv_grad, out_grad, fc_grad, proj_grad = (
        v[name].reshape(layers, -1, v[name].shape[-1]) for name in ("qkv", "out", "fc", "proj")
    )
    return *v["home"], norm1_grad, qkv_grad, out_grad, norm2_grad, fc_grad, proj_grad


def solution(mesh):
    block = P("dp", "seq", None)
    return jax.shard_map(
        functools.partial(per_device, (mesh.shape["dp"], mesh.shape["seq"])),
        mesh=mesh,
        in_specs=(block, P(), P(), P(), P(), P(), P(), P("dp"), P(), block),
        out_specs=(block, block, P(), P(), P(), P(), P(), P()),
        check_vma=False,
    )
```

```python
import functools
import math

import jax
import jax.numpy as jnp
from jax import lax
from jax.experimental import pallas as pl
from jax.experimental.pallas import tpu as pltpu
from jax.sharding import PartitionSpec as P

HEADS = 6
EPSILON = 1e-05
NEGATIVE = -1e30
BF = jnp.bfloat16
F32 = jnp.float32
ALL = ("dp", "seq")
LANES = 128
GAIN_ROWS = 16
SCHEDULE = """
BA1a BA1b A BT BF A B A C BA0a BA0b A B BE C B D A C B D A C D B C D SG B C D A B C D A PG D B D
"""
MB = 1024 * 1024
VMEM = pltpu.VMEM
SMEM = pltpu.SMEM


def mm(a, b):
    return lax.dot_general(a, b, (((1,), (0,)), ((), ())), preferred_element_type=F32)


def mm_t(a, b):
    return lax.dot_general(a, b, (((1,), (1,)), ((), ())), preferred_element_type=F32)


def t_mm(a, b):
    return lax.dot_general(a, b, (((0,), (0,)), ((), ())), preferred_element_type=F32)


class Order:
    def __init__(self):
        self.last = []

    def after(self, x):
        x, *last = lax.optimization_barrier((x, *self.last))
        self.last = last[-1:]
        return x

    def add(self, result):
        self.last = [result, *self.last]


def call(body, name, ins, outs, scratch=(), limit=16, flops=0, transcendentals=0, grid=(1,), aliases=None, order=None):
    moved = sum(math.prod(o[0]) * jnp.dtype(o[1]).itemsize for o in outs)
    moved += sum(a.size * a.dtype.itemsize for a, _ in ins)
    kernel = body
    if order is not None:
        count, more = len(ins), len(order.last)
        ins = [*ins, *((x, pl.BlockSpec(memory_space=pl.ANY)) for x in order.last)]
        order.last = []
        results_at = count + more + len(outs)
        outs = [*outs, ((8, LANES), F32, whole(8, LANES))]

        def kernel(*refs):
            body(*refs[:count], *refs[count + more : results_at], *refs[results_at + 1 :])
            refs[results_at][...] = jnp.zeros((8, LANES), F32)

    results = pl.pallas_call(
        kernel,
        out_shape=[pltpu.HBM(o[0], o[1]) if len(o) > 3 else jax.ShapeDtypeStruct(o[0], o[1]) for o in outs],
        grid=grid,
        in_specs=[s for _, s in ins],
        out_specs=[o[2] for o in outs],
        scratch_shapes=list(scratch),
        input_output_aliases=aliases or {},
        compiler_params=pltpu.CompilerParams(vmem_limit_bytes=limit * MB),
        cost_estimate=pl.CostEstimate(flops=flops, bytes_accessed=moved, transcendentals=transcendentals),
        name=name,
    )(*[a for a, _ in ins])
    if order is not None:
        *results, token = results
        order.add(token)
    return results


def whole(*shape):
    return pl.BlockSpec(shape, lambda *_: (0,) * len(shape))


def layer_of(index, *shape):
    return pl.BlockSpec((None,) + shape, lambda *_: (index,) + (0,) * len(shape))


def in_hbm(x):
    return pltpu.with_memory_space_constraint(x, pltpu.HBM), pl.BlockSpec(memory_space=pltpu.HBM)


def scalars():
    return pl.BlockSpec(memory_space=SMEM)


def norm_parts(values):
    centre = jnp.mean(values, axis=-1, keepdims=True)
    centred = values - centre
    spread = jnp.mean(centred * centred, axis=-1, keepdims=True)
    inverse = lax.rsqrt(spread + EPSILON)
    return centred * inverse, inverse


def norm_back(grad, zhat, inverse, gain):
    e = grad * gain
    return inverse * (
        e
        - jnp.mean(e, axis=-1, keepdims=True)
        - zhat * jnp.mean(e * zhat, axis=-1, keepdims=True)
    )


def qkv_step(hidden, gain, weight, a_ref, q_ref, kv_ref, scale):
    zhat, _ = norm_parts(hidden)
    a = (zhat * gain).astype(BF)
    a_ref[...] = a
    packed = mm(a, weight).astype(BF)
    width = a.shape[1]
    q_ref[...] = packed[:, :width] * jnp.asarray(scale, BF)
    kv_ref[...] = packed[:, width:]


def first_body(scale, ha_ref, hb_ref, gain_ref, w_ref, h_ref, a_ref, q_ref, kv_ref):
    span = ha_ref.shape[0]
    h_ref[:span] = ha_ref[...].astype(F32)
    h_ref[span:] = hb_ref[...].astype(F32)
    qkv_step(h_ref[...], gain_ref[0:1], w_ref[...], a_ref, q_ref, kv_ref, scale)


def attend_body(block, info_ref, q_ref, ko_ref, vo_ref, kx_ref, vx_ref, bo_ref, bx_ref, hot_ref, p_ref, att_ref, inv_ref):
    tokens = q_ref.shape[0]
    head = LANES // 2
    ones = jnp.ones((tokens, LANES), BF)

    def beside(a, b):
        return jnp.concatenate([a, b], axis=1)

    keys = jnp.concatenate([beside(ko_ref[...], bo_ref[...]), beside(kx_ref[...], bx_ref[...])], axis=0)
    values = jnp.concatenate([beside(vo_ref[...], ones), beside(vx_ref[...], ones)], axis=0)
    lower = lax.broadcasted_iota(jnp.int32, (tokens, LANES), 1) < head
    at_q = lax.broadcasted_iota(jnp.int32, (block, block), 0)
    at_k = lax.broadcasted_iota(jnp.int32, (block, block), 1)
    prefix = info_ref[0]
    q = q_ref[...]
    scores = []
    for n in range(2):
        qn = jnp.where(lower if n == 0 else ~lower, q, jnp.zeros_like(q))
        scores.append(mm_t(beside(qn, hot_ref[...]), keys))
    chances = []
    for n in range(2):
        rows = []
        for t in range(tokens // block):
            s = scores[n][t * block : (t + 1) * block]
            seen = (at_k <= at_q) | (info_ref[1 + t] * block + at_k < prefix)
            pieces = [s[:, : t * block], jnp.where(seen, s[:, t * block : (t + 1) * block], NEGATIVE), s[:, (t + 1) * block :]]
            s = jnp.concatenate([piece for piece in pieces if piece.shape[1]], axis=1)
            rows.append(jnp.exp(s - jnp.max(s, axis=1, keepdims=True)).astype(BF))
        p = jnp.concatenate(rows, axis=0)
        p_ref[n] = p
        chances.append(p)
    even, odd = [mm(p, values) for p in chances]
    inverse = 1.0 / jnp.where(lower, even[:, LANES:], odd[:, LANES:])
    inv_ref[...] = inverse
    att_ref[...] = (jnp.where(lower, even[:, :LANES], odd[:, :LANES]) * inverse).astype(BF)


def feed(h_ref, att_ref, wout_ref, gain, wfc_ref, wproj_ref, mid_ref, sec_ref, act_ref, gp_ref):
    middle = h_ref[...] + mm(att_ref[...], wout_ref[...])
    mid_ref[...] = middle
    zhat, _ = norm_parts(middle)
    second = (zhat * gain).astype(BF)
    sec_ref[...] = second
    total = middle
    width = middle.shape[1]
    for j in range(wfc_ref.shape[1] // width):
        cols = slice(j * width, (j + 1) * width)
        lifted = mm(second, wfc_ref[:, cols])
        phi = 0.5 * (1.0 + lax.erf(lifted * (1.0 / math.sqrt(2.0))))
        slope = phi + lifted * jnp.exp(-0.5 * lifted * lifted) * (1.0 / math.sqrt(2.0 * math.pi))
        gp_ref[:, cols] = slope.astype(BF)
        act = (lifted * phi).astype(BF)
        act_ref[:, cols] = act
        total = total + mm(act, wproj_ref[cols, :])
    return total


def middle_body(scale, layer, h_ref, att_ref, wout_ref, g2_ref, wfc_ref, wproj_ref, g1_ref, wqkv_ref,
                mid_ref, sec_ref, act_ref, gp_ref, out_ref, a_ref, q_ref, kv_ref):
    out = feed(h_ref, att_ref, wout_ref, g2_ref[layer : layer + 1], wfc_ref, wproj_ref, mid_ref, sec_ref, act_ref, gp_ref)
    out_ref[...] = out
    qkv_step(out, g1_ref[layer + 1 : layer + 2], wqkv_ref[...], a_ref, q_ref, kv_ref, scale)


def relative(bits, index, core):
    place = 0
    for mine, others in bits:
        place = 2 * place + (jnp.where(core == 0, index >> mine, index >> others) & 1)
    return place


def hand_out(bits, at_ref, g_ref, keep_ref, send_ref):
    index = at_ref[0]
    core = index & 1
    count = keep_ref.shape[0]
    for ref, side in ((keep_ref, core), (send_ref, 1 - core)):
        place = relative(bits, index, side)
        for i in range(count):
            ref[i] = g_ref[side * count + (place ^ i)]


def put_rows(g_ref, at, values, first=0, total=None):
    share = (total or values.shape[0]) // g_ref.shape[0]
    done = 0
    while done < values.shape[0]:
        block, row = divmod(first + done, share)
        count = min(share - row, values.shape[0] - done)
        g_ref[block, at + row : at + row + count] = values[done : done + count]
        done += count


def back_proj(upstream, act_ref, gp_ref, wproj_ref, g_ref, at, lift_ref):
    down = upstream.astype(BF)
    width = down.shape[1]
    for j in range(act_ref.shape[1] // width):
        cols = slice(j * width, (j + 1) * width)
        put_rows(g_ref, at, t_mm(act_ref[:, cols], down).astype(BF), j * width, act_ref.shape[1])
        lift_ref[:, cols] = (mm_t(down, wproj_ref[cols, :]) * gp_ref[:, cols].astype(F32)).astype(BF)


def back_fc(upstream, lift_ref, sec_ref, mid_ref, att_ref, wfc_ref, wout_ref, gain, g_ref, at, mg_ref, ag_ref, gain_ref):
    second = sec_ref[...]
    width = second.shape[1]
    inner = lift_ref.shape[1]
    second_grad = None
    for j in range(inner // width):
        cols = slice(j * width, (j + 1) * width)
        lift = lift_ref[:, cols]
        put_rows(g_ref, at + j * width // g_ref.shape[0], t_mm(second, lift).astype(BF))
        term = mm_t(lift, wfc_ref[:, cols])
        second_grad = term if second_grad is None else second_grad + term
    zhat, inverse = norm_parts(mid_ref[...])
    gain_ref[...] = jnp.broadcast_to(jnp.sum(second_grad * zhat, axis=0, keepdims=True), gain_ref.shape)
    mg = upstream + norm_back(second_grad, zhat, inverse, gain)
    mg_ref[...] = mg
    branch = mg.astype(BF)
    put_rows(g_ref, at + inner // g_ref.shape[0], t_mm(att_ref[...], branch).astype(BF))
    ag_ref[...] = mm_t(branch, wout_ref[...]).astype(BF)


def turn_body(layer, bits, core_ref, h_ref, att_ref, wout_ref, g2_ref, wfc_ref, wproj_ref, ua_ref, ub_ref,
              oa_ref, ob_ref, keep_ref, send_ref, mg_ref, ag_ref, gain_ref,
              mid_ref, sec_ref, act_ref, gp_ref, lift_ref, g_ref):
    gain = g2_ref[layer : layer + 1]
    out = feed(h_ref, att_ref, wout_ref, gain, wfc_ref, wproj_ref, mid_ref, sec_ref, act_ref, gp_ref)
    span = oa_ref.shape[0]
    oa_ref[...] = out[:span].astype(BF)
    ob_ref[...] = out[span:].astype(BF)
    upstream = jnp.concatenate([ua_ref[...], ub_ref[...]], axis=0).astype(F32)
    back_proj(upstream, act_ref, gp_ref, wproj_ref, g_ref, 0, lift_ref)
    back_fc(upstream, lift_ref, sec_ref, mid_ref, att_ref, wfc_ref, wout_ref, gain, g_ref, act_ref.shape[1] // g_ref.shape[0],
            mg_ref, ag_ref, gain_ref)
    hand_out(bits, core_ref, g_ref, keep_ref, send_ref)


def back_fc_body(layer, bits, core_ref, u_ref, lift_ref, sec_ref, mid_ref, att_ref, wfc_ref, wout_ref, g2_ref,
                 keep_ref, send_ref, mg_ref, ag_ref, gain_ref, g_ref):
    back_fc(u_ref[...], lift_ref, sec_ref, mid_ref, att_ref, wfc_ref, wout_ref, g2_ref[layer : layer + 1], g_ref, 0,
            mg_ref, ag_ref, gain_ref)
    hand_out(bits, core_ref, g_ref, keep_ref, send_ref)


def back_attend_body(scale, q_ref, ko_ref, vo_ref, kx_ref, vx_ref, p_ref, att_ref, inv_ref, ag_ref,
                     dq_ref, own_ref, oth_ref):
    tokens = q_ref.shape[0]
    head = LANES // 2
    lower = lax.broadcasted_iota(jnp.int32, (tokens, LANES), 1) < head
    q = q_ref[...]
    scaled = ag_ref[...].astype(F32) * inv_ref[...]
    product = scaled * att_ref[...].astype(F32)
    keys = jnp.concatenate([ko_ref[...], kx_ref[...]], axis=0)
    values = jnp.concatenate([vo_ref[...], vx_ref[...]], axis=0)
    dq = dk = dv = None
    for n in range(2):
        mine = lower if n == 0 else ~lower
        qn = jnp.where(mine, q, jnp.zeros_like(q))
        gn = jnp.where(mine, scaled, 0.0).astype(BF)
        delta = jnp.sum(jnp.where(mine, product, 0.0), axis=1, keepdims=True)
        p = p_ref[n]
        ds = (p.astype(F32) * (mm_t(gn, values) - delta)).astype(BF)
        dqn, dkn, dvn = mm(ds, keys), t_mm(qn, ds), t_mm(gn, p)
        if n == 0:
            dq, dk, dv = dqn, dkn, dvn
        else:
            dq, dk, dv = jnp.where(lower, dq, dqn), dk + dkn, dv + dvn
    dq_ref[...] = (dq * scale).astype(BF)
    for i, grad in enumerate((dk.T, dv.T)):
        own_ref[i] = grad[:tokens]
        oth_ref[i] = grad[tokens:].astype(BF)


def back_qkv(layer, parts, a_ref, h_ref, g1_ref, w_ref, mg_ref, g_ref):
    a = a_ref[...]
    width = a.shape[1]
    blocks = [jnp.concatenate([dq[...] for dq, _, _ in parts], axis=1)]
    for i in range(2):
        blocks.append(jnp.concatenate([(own[i] + got[i].astype(F32)).astype(BF) for _, own, got in parts], axis=1))
    grad = None
    for j, block in enumerate(blocks):
        put_rows(g_ref, j * width // g_ref.shape[0], t_mm(a, block).astype(BF))
        term = mm_t(block, w_ref[:, j * width : (j + 1) * width])
        grad = term if grad is None else grad + term
    zhat, inverse = norm_parts(h_ref[...])
    gain_grad = jnp.sum(grad * zhat, axis=0, keepdims=True)
    return mg_ref[...] + norm_back(grad, zhat, inverse, g1_ref[layer : layer + 1]), gain_grad


def back_turn_body(layer, bits, core_ref, *refs):
    parts, refs = (refs[:3], refs[3:6]), refs[6:]
    (a_ref, h_ref, g1_ref, w_ref, mg_ref, act_ref, gp_ref, wproj_ref,
     keep_ref, send_ref, up_ref, gain_ref, lift_ref, g_ref) = refs
    up, gain_grad = back_qkv(layer, parts, a_ref, h_ref, g1_ref, w_ref, mg_ref, g_ref)
    gain_ref[...] = jnp.broadcast_to(gain_grad, gain_ref.shape)
    up_ref[...] = up
    back_proj(up, act_ref, gp_ref, wproj_ref, g_ref, 3 * up.shape[1] // g_ref.shape[0], lift_ref)
    hand_out(bits, core_ref, g_ref, keep_ref, send_ref)


def back_both_body(layer, bits, core_ref, *refs):
    parts, refs = (refs[:3], refs[3:6]), refs[6:]
    (a_ref, h_ref, g1_ref, w_ref, mg_ref, act_ref, gp_ref, wproj_ref, sec_ref, mid_ref, att_ref, wfc_ref, wout_ref, g2_ref,
     keep_ref, send_ref, mg_out, ag_ref, gain1_ref, gain2_ref, g_ref, up_ref, lift_ref) = refs
    up, gain_grad = back_qkv(layer, parts, a_ref, h_ref, g1_ref, w_ref, mg_ref, g_ref)
    gain1_ref[...] = jnp.broadcast_to(gain_grad, gain1_ref.shape)
    up_ref[...] = up
    at = 3 * up.shape[1]
    back_proj(up, act_ref, gp_ref, wproj_ref, g_ref, at // g_ref.shape[0], lift_ref)
    at += act_ref.shape[1]
    back_fc(up_ref[...], lift_ref, sec_ref, mid_ref, att_ref, wfc_ref, wout_ref, g2_ref[layer - 1 : layer], g_ref, at // g_ref.shape[0],
            mg_out, ag_ref, gain2_ref)
    hand_out(bits, core_ref, g_ref, keep_ref, send_ref)


def back_end_body(layer, bits, core_ref, *refs):
    parts, refs = (refs[:3], refs[3:6]), refs[6:]
    (a_ref, h_ref, g1_ref, w_ref, mg_ref, oa_ref, ob_ref, *gain_refs, keep_ref, send_ref, to_a_ref, to_b_ref, g_ref) = refs
    up, gain_grad = back_qkv(layer, parts, a_ref, h_ref, g1_ref, w_ref, mg_ref, g_ref)
    span = oa_ref.shape[0]
    width = up.shape[1]
    to_a_ref[0] = oa_ref[...]
    to_b_ref[0] = ob_ref[...]
    to_a_ref[1] = up[:span].astype(BF)
    to_b_ref[1] = up[span:].astype(BF)
    at = 3 * width // g_ref.shape[0]
    for i, gain in enumerate([gain_grad] + [ref[0:1] for ref in gain_refs]):
        put_rows(g_ref, at + i, jnp.broadcast_to(gain, (g_ref.shape[0], width)).astype(BF))
    at += 1 + len(gain_refs)
    for block in range(g_ref.shape[0]):
        g_ref[block, at:] = jnp.zeros((g_ref.shape[1] - at, width), BF)
    hand_out(bits, core_ref, g_ref, keep_ref, send_ref)


def masks_body(per_span, block, ids_ref, order_ref, own_ref, other_ref, w_in, g_in, bias_ref, hot_ref, info_ref, w_ref, g_ref, sem):
    copies = [pltpu.make_async_copy(w_in.at[0], w_ref, sem.at[0]), pltpu.make_async_copy(g_in, g_ref, sem.at[1])]
    for copy in copies:
        copy.start()
    core, place = ids_ref[0] & 1, ids_ref[1]
    odd = place & 1
    prefix = jnp.where((place >> 1) == core, own_ref[odd], other_ref[odd])
    info_ref[0] = prefix
    ranks = []
    for c in (core, 1 - core):
        for span in (2 * c + odd, 2 * c + 1 - odd):
            ranks += [order_ref[span * per_span + i] for i in range(per_span)]
    tokens = hot_ref.shape[0]
    own = tokens // block
    lane = lax.broadcasted_iota(jnp.int32, (block, LANES), 1)
    within = lax.broadcasted_iota(jnp.int32, (block, LANES), 0)
    lane_rank = jnp.full((block, LANES), -1, jnp.int32)
    for b in range(own):
        info_ref[1 + b] = ranks[b]
        lane_rank = jnp.where(lane == b, ranks[b], lane_rank)
        hot_ref[b * block : (b + 1) * block] = jnp.where(lane == b, 1.0, 0.0).astype(BF)
    for k, rank in enumerate(ranks):
        unseen = (lane < own) & (rank >= lane_rank) & (lane != k) & (rank * block + within >= prefix)
        bias_ref[k * block : (k + 1) * block] = jnp.where(unseen, NEGATIVE, 0.0).astype(BF)
    for copy in copies:
        copy.wait()


def pick_body(at_ref, x_ref, a_ref, b_ref):
    odd = at_ref[1] & 1
    a_ref[...] = x_ref[odd]
    b_ref[...] = x_ref[1 - odd]


def place_body(odd_ref, a_ref, b_ref, *out_refs):
    odd = odd_ref[1] & 1
    for i, ref in enumerate(out_refs):
        ref[odd] = a_ref[i]
        ref[1 - odd] = b_ref[i]


def add(a, b):
    return (a.astype(F32) + b.astype(F32)).astype(BF)


def unpack_body(plan, gains, bits, groups, befores, at_ref, *refs):
    halves, refs = refs[: 2 * groups], refs[2 * groups + befores :]
    out_refs, refs = refs[: len(plan)], refs[len(plan) :]
    gain_refs, refs = refs[: len(gains)], refs[len(gains) :]
    *stage_refs, sem = refs
    index = at_ref[0]
    core = index & 1
    copies = []
    for group in range(groups):
        a_ref, b_ref = halves[2 * group : 2 * group + 2]
        count, _, width = a_ref.shape
        mine = [(at, layer, out, stage) for (g, at, layer), out, stage in zip(plan, out_refs, stage_refs) if g == group]
        for ref, side in ((a_ref, core), (b_ref, 1 - core)):
            place = relative(bits, index, side)
            for i in range(count):
                block = side * count + (place ^ i)
                for at, layer, out_ref, stage_ref in mine:
                    _, rows, cols = stage_ref.shape
                    for j in range(cols // width):
                        stage_ref[block, :, j * width : (j + 1) * width] = ref[i, at + j * rows : at + (j + 1) * rows].astype(F32)
                    copies.append(pltpu.make_async_copy(stage_ref.at[block], out_ref.at[layer, block], sem.at[len(copies)]))
                    copies[-1].start()
    for rows, ref in zip(gains, gain_refs):
        ref[...] = jnp.concatenate([halves[-2][0, row : row + 1] for row in rows], axis=0).astype(F32)
    for copy in copies:
        copy.wait()


def unpack(bits, at, groups, layers, gains, order):
    ins = [(at, scalars())] + [(x, whole(*x.shape)) for halves, _ in groups for x in halves]
    aliases = {}
    outs, plan = [], []
    count, _, width = groups[0][0][0].shape
    blocks = 2 * count
    scratch = []
    for group, (_, parts) in enumerate(groups):
        for row, layer, shape, before in parts:
            if before is not None:
                aliases[len(ins)] = len(outs)
                ins.append((before, pl.BlockSpec(memory_space=pltpu.HBM)))
            outs.append(((layers, blocks, shape[0] // blocks, shape[1]), F32, pl.BlockSpec(memory_space=pltpu.HBM), True))
            plan.append((group, row, layer))
            scratch.append(VMEM((blocks, shape[0] // blocks, shape[1]), F32))
    outs += [((len(rows), width), F32, whole(len(rows), width)) for rows in gains]
    return call(
        functools.partial(unpack_body, plan, gains, bits, len(groups), len(aliases)), "unpack", ins, outs,
        scratch=[*scratch, pltpu.SemaphoreType.DMA((blocks * len(plan),))], limit=24, aliases=aliases, order=order,
    )


def per_device(mesh_shape, hidden_in, norm1_gain, qkv_weight, out_weight, norm2_gain, fc_weight, proj_weight,
               prefix_len, block_order, grad_out):
    dp, seq = mesh_shape
    rows_here, span, width = hidden_in.shape
    layers = qkv_weight.shape[0]
    inner = fc_weight.shape[2]
    scale = 1.0 / math.sqrt(width // HEADS)
    row_length = span * seq
    block_count = block_order.shape[0]
    block = row_length // block_count
    per_span = span // block
    tokens = 2 * span
    pairs = width // LANES
    assert rows_here == 2 and seq == 4 and dp % 2 == 0 and layers == 2
    di, si = lax.axis_index("dp"), lax.axis_index("seq")
    at = jnp.stack([di, si]).astype(jnp.int32)
    order = Order()

    def spot(d, s):
        return d * seq + s

    perm_a = [(spot(d, s), spot((d & ~1) | (s >> 1), 2 * (d & 1) + (s & 1))) for d in range(dp) for s in range(seq)]
    perm_b = [(spot(d, s), spot((d & ~1) | (s >> 1), 2 * (d & 1) + 1 - (s & 1))) for d in range(dp) for s in range(seq)]
    back_a = [(b, a) for a, b in perm_a]
    back_b = [(b, a) for a, b in perm_b]
    pair_perm = [(spot(d, s), spot(d ^ 1, s)) for d in range(dp) for s in range(seq)]
    t_w = (tokens, width)
    full = whole(*t_w)
    half_spec = whole(span, width)
    both_spec = whole(2, span, width)

    def pair(x):
        return lax.ppermute(x, ALL, pair_perm)

    def pick(x):
        return call(
            pick_body, "pick", [(at, scalars()), (x, both_spec)], [((span, width), BF, half_spec)] * 2, limit=4, order=order
        )

    def spread(first, other):
        return lax.ppermute(first, ALL, perm_a), lax.ppermute(other, ALL, perm_b)

    class Collect:
        def __init__(self, a, b):
            self.a, self.b = lax.ppermute(a, ALL, back_a), lax.ppermute(b, ALL, back_b)

        def done(self, order):
            return call(
                place_body, "place", [(at, scalars()), (self.a, both_spec), (self.b, both_spec)],
                [((2, span, width), BF, both_spec, True)] * 2, limit=8, order=order,
            )

    dp_bits = [i for i in range(1, dp.bit_length() - 1)]
    seq_bits = [i for i in range(seq.bit_length() - 1)]
    orders = (dp_bits, dp_bits[::-1])
    z_orders = (seq_bits, seq_bits[::-1])
    bits = list(zip(*orders))
    blocks = 2 ** (len(dp_bits) + 1)

    own_blocks = tokens // block
    ha, hb = spread(*pick(hidden_in))
    grad_pieces = pick(grad_out)
    prefix_other = pair(prefix_len)
    bias, hot, info, first_weight, first_gain = call(
        functools.partial(masks_body, per_span, block), "masks",
        [(at, scalars()), (block_order, scalars()), (prefix_len, scalars()), (prefix_other, scalars()),
         in_hbm(qkv_weight), in_hbm(norm1_gain)],
        [((2 * tokens, LANES), BF, whole(2 * tokens, LANES)), ((tokens, LANES), BF, whole(tokens, LANES)),
         ((1 + own_blocks,), jnp.int32, scalars()),
         ((width, 3 * width), BF, whole(width, 3 * width)), ((layers, width), F32, whole(layers, width))],
        scratch=[pltpu.SemaphoreType.DMA((2,))], order=order,
    )

    wide = whole(tokens, inner)
    gains = whole(layers, width)
    dense = 2 * tokens * width

    def qkv_out():
        return [(t_w, BF, full), (t_w, BF, full), ((tokens, 2 * width), BF, whole(tokens, 2 * width))]

    h, a, q, kv = call(
        functools.partial(first_body, scale), "first",
        [(ha, half_spec), (hb, half_spec), (first_gain, gains), (first_weight, whole(width, 3 * width))],
        [(t_w, F32, full)] + qkv_out(),
        flops=dense * 3 * width, order=order,
    )
    lane_block = pl.BlockSpec((tokens, LANES), lambda p: (0, p))
    lane_block_v = pl.BlockSpec((tokens, LANES), lambda p: (0, p + pairs))
    p_spec = pl.BlockSpec((2, tokens, 2 * tokens), lambda p: (p, 0, 0))

    def attend(q, kv, kv_other):
        return call(
            functools.partial(attend_body, block), "attend",
            [(info, scalars()), (q, lane_block), (kv, lane_block), (kv, lane_block_v), (kv_other, lane_block), (kv_other, lane_block_v),
             (bias, pl.BlockSpec((tokens, LANES), lambda p: (0, 0))), (bias, pl.BlockSpec((tokens, LANES), lambda p: (1, 0))),
             (hot, whole(tokens, LANES))],
            [((HEADS, tokens, 2 * tokens), BF, p_spec), (t_w, BF, lane_block), (t_w, F32, lane_block)],
            grid=(pairs,), flops=4 * tokens * 2 * tokens * 256 * HEADS, transcendentals=HEADS * tokens * 2 * tokens,
            limit=14, order=order,
        )

    def feed_ins(layer, h, att):
        return [
            (h, full), (att, full), (out_weight, layer_of(layer, width, width)), (norm2_gain, gains),
            (fc_weight, layer_of(layer, width, inner)), (proj_weight, layer_of(layer, inner, width)),
        ]

    def swap_dp(x, step):
        return lax.ppermute(x, ALL, [(spot(d, s), spot(d ^ (1 << orders[d & 1][step]), s)) for d in range(dp) for s in range(seq)])

    def swap_seq(x, step):
        return lax.ppermute(x, ALL, [(spot(d, s), spot(d, s ^ (1 << z_orders[d & 1][step]))) for d in range(dp) for s in range(seq)])

    class Bucket:
        def __init__(self, keep, send):
            self.halves = None
            self.parts = None
            self.steps = self.run(keep, send)
            next(self.steps)

        def run(self, keep, send):
            got = pair(send)
            for step in range(len(dp_bits)):
                yield
                total = add(keep, order.after(got))
                half = total.shape[0] // 2
                keep, send = total[:half], total[half:]
                order.add(keep)
                got = swap_dp(send, step)
            self.parts = [(keep, got)]
            yield
            yield from self.rest()

        def rest(self):
            total = jnp.concatenate([add(keep, order.after(got)) for keep, got in self.parts], axis=1)
            order.add(total)
            for step in range(len(seq_bits)):
                got = swap_seq(total, step)
                yield
                total = add(total, order.after(got))
                order.add(total)
            for step in reversed(range(len(dp_bits))):
                got = swap_dp(total, step)
                yield
                total = jnp.concatenate([total, order.after(got)], axis=0)
                order.add(total)
            self.halves = (total, pair(total))
            yield

        def step(self):
            next(self.steps)

    def bucket_outs(rows):
        count = 2 ** len(dp_bits)
        size = rows // (2 * count)
        assert size * 2 * count == rows
        return [((count, size, width), BF, whole(count, size, width))] * 2, [VMEM((2 * count, size, width), BF)]

    gain_out = ((8, width), F32, whole(8, width))

    kv_other = pair(kv)
    ua, ub = spread(*[order.after(x) for x in grad_pieces])
    p, att, inv = attend(q, kv, kv_other)
    order.last += [ua, ub]
    mid, sec, act, gp, h_next, a_next, q_next, kv_next = call(
        functools.partial(middle_body, scale, 0), "middle",
        feed_ins(0, h, att) + [(norm1_gain, gains), (qkv_weight, layer_of(1, width, 3 * width))],
        [(t_w, F32, full), (t_w, BF, full), ((tokens, inner), BF, wide), ((tokens, inner), BF, wide), (t_w, F32, full)] + qkv_out(),
        flops=dense * (4 * width + 2 * inner), transcendentals=2 * tokens * inner, limit=18, order=order,
    )
    saved = (h, a, q, kv, kv_other, p, att, inv)
    h, a, q, kv = h_next, a_next, q_next, kv_next

    kv_other = pair(kv)
    p, att, inv = attend(q, kv, kv_other)
    outs, scratch = bucket_outs(2 * inner + width)
    oa, ob, keep, send, mg, ag, gain2_1 = call(
        functools.partial(turn_body, 1, bits), "turn",
        [(at, scalars())] + feed_ins(1, h, att) + [(ua, half_spec), (ub, half_spec)],
        [((span, width), BF, half_spec)] * 2 + outs + [(t_w, F32, full), (t_w, BF, full), gain_out],
        scratch=[VMEM(t_w, F32), VMEM(t_w, BF)] + [VMEM((tokens, inner), BF)] * 3 + scratch,
        flops=dense * (3 * width + 6 * inner), transcendentals=2 * tokens * inner, limit=24, order=order,
    )
    feed_1 = Bucket(keep, send)

    def back_attend(first, count, q, kv, kv_other, p, att, inv, ag):
        spec = pl.BlockSpec((tokens, LANES), lambda p: (0, p + first))
        spec_v = pl.BlockSpec((tokens, LANES), lambda p: (0, p + first + pairs))
        out = (tokens, count * LANES)
        pair_out = pl.BlockSpec((2, tokens, LANES), lambda p: (0, 0, p))
        dq, own, oth = call(
            functools.partial(back_attend_body, scale), "back_attend",
            [(q, spec), (kv, spec), (kv, spec_v), (kv_other, spec), (kv_other, spec_v),
             (p, pl.BlockSpec((2, tokens, 2 * tokens), lambda p: (p + first, 0, 0))), (att, spec), (inv, spec), (ag, spec)],
            [(out, BF, lane_block), ((2, *out), F32, pair_out), ((2, *out), BF, pair_out)],
            grid=(count,), flops=8 * tokens * 2 * tokens * 256 * 2 * count, limit=14, order=order,
        )
        return dq, own, pair(oth)

    def part_ins(parts):
        return [(x, whole(*x.shape)) for part in parts for x in part]

    layer_1 = (q, kv, kv_other, p, att, inv)
    h_1, a_1, mg_1, ag_1 = h, a, mg, ag
    h_0, a_0, *layer_0 = saved
    v = {}
    buckets = {"A": feed_1}

    def back_turn():
        outs, scratch = bucket_outs(3 * width + inner)
        keep, send, v["up"], v["gain1_1"], v["lift"] = call(
            functools.partial(back_turn_body, 1, bits), "back_turn",
            [(at, scalars())] + part_ins((v["1a"], v["1b"])) + [
                (a_1, full), (h_1, full), (norm1_gain, gains), (qkv_weight, layer_of(1, width, 3 * width)), (mg_1, full),
                (act, wide), (gp, wide), (proj_weight, layer_of(0, inner, width))],
            outs + [(t_w, F32, full), gain_out, ((tokens, inner), BF, wide)],
            scratch=scratch, flops=dense * (6 * width + 2 * inner), limit=18, order=order,
        )
        buckets["B"] = Bucket(keep, send)

    def back_fc_0():
        outs, scratch = bucket_outs(inner + width)
        keep, send, v["mg"], v["ag"], v["gain2_0"] = call(
            functools.partial(back_fc_body, 0, bits), "back_fc",
            [(at, scalars()), (v["up"], full), (v["lift"], wide), (sec, full), (mid, full), (layer_0[4], full),
             (fc_weight, layer_of(0, width, inner)), (out_weight, layer_of(0, width, width)), (norm2_gain, gains)],
            outs + [(t_w, F32, full), (t_w, BF, full), gain_out],
            scratch=scratch, flops=dense * (2 * width + 2 * inner), limit=16, order=order,
        )
        buckets["C"] = Bucket(keep, send)

    def back_both():
        outs, scratch = bucket_outs(4 * width + 2 * inner)
        keep, send, v["mg"], v["ag"], v["gain1_1"], v["gain2_0"] = call(
            functools.partial(back_both_body, 1, bits), "back_both",
            [(at, scalars())] + part_ins((v["1a"], v["1b"])) + [
                (a_1, full), (h_1, full), (norm1_gain, gains), (qkv_weight, layer_of(1, width, 3 * width)), (mg_1, full),
                (act, wide), (gp, wide), (proj_weight, layer_of(0, inner, width)), (sec, full), (mid, full), (layer_0[4], full),
                (fc_weight, layer_of(0, width, inner)), (out_weight, layer_of(0, width, width)), (norm2_gain, gains)],
            outs + [(t_w, F32, full), (t_w, BF, full), gain_out, gain_out],
            scratch=scratch + [VMEM(t_w, F32), VMEM((tokens, inner), BF)], flops=dense * (8 * width + 4 * inner), limit=24, order=order,
        )
        v["both"] = True
        buckets["B"] = Bucket(keep, send)

    def back_end():
        outs, scratch = bucket_outs(3 * width + GAIN_ROWS * blocks)
        keep, send, ga, gb = call(
            functools.partial(back_end_body, 0, bits), "back_end",
            [(at, scalars())] + part_ins((v["0a"], v["0b"])) + [
                (a_0, full), (h_0, full), (norm1_gain, gains), (qkv_weight, layer_of(0, width, 3 * width)), (v["mg"], full),
                (oa, half_spec), (ob, half_spec)]
            + [(g, whole(8, width)) for g in (v["gain1_1"], v["gain2_0"], gain2_1)],
            outs + [((2, span, width), BF, both_spec)] * 2,
            scratch=scratch, flops=2 * dense * 3 * width, limit=12, order=order,
        )
        buckets["D"] = Bucket(keep, send)
        v["ga"], v["gb"] = ga, gb

    def run_part(name, first, count, layer, ag):
        v[name] = back_attend(first, count, *layer, ag)

    parts_of = {
        "A": [(0, 1, (inner, width), "proj"), (inner, 1, (width, inner), "fc"), (2 * inner, 1, (width, width), "out")],
        "B": [(0, 1, (width, 3 * width), "qkv"), (3 * width, 0, (inner, width), "proj")],
        "C": [(0, 0, (width, inner), "fc"), (inner, 0, (width, width), "out")],
        "D": [(0, 0, (width, 3 * width), "qkv")],
    }

    def unpacked(names):
        last = "D" in names
        groups = [
            (buckets.pop(name).halves, [(row // blocks, layer, shape, v.get(key)) for row, layer, shape, key in parts_of[name]])
            for name in names
        ]
        gain_rows = [[3 * width // blocks + i for i in pair] for pair in ((0, 1), (2, 3))] if last else []
        got = unpack(bits, at, groups, layers, gain_rows, order)
        keys = [part[3] for name in names for part in parts_of[name]]
        v.update(zip(keys, got))
        if last:
            v["gains"] = got[len(keys) : len(keys) + 2]

    def bucket_step(name):
        if name not in buckets:
            return
        if buckets[name].halves is None:
            buckets[name].step()
        elif name == "D":
            while "C" in buckets and buckets["C"].halves is None:
                buckets["C"].step()
            unpacked([n for n in "CD" if n in buckets])
        elif name != "C":
            unpacked([name])

    kernels = {
        "BA1a": lambda: run_part("1a", 0, 1, layer_1, ag_1),
        "BA1b": lambda: run_part("1b", 1, pairs - 1, layer_1, ag_1),
        "BT": back_turn,
        "BF": back_fc_0,
        "BTF": back_both,
        "BA0a": lambda: run_part("0a", 0, 1, layer_0, v["ag"]),
        "BA0b": lambda: run_part("0b", 1, pairs - 1, layer_0, v["ag"]),
        "BE": back_end,
        "PG": lambda: v.update(home=v["home"].done(order)),
        "SG": lambda: v.update(home=Collect(order.after(v["ga"]), order.after(v["gb"]))),
    }
    for token in SCHEDULE.split():
        if token in kernels:
            kernels[token]()
        else:
            bucket_step(token)
    while buckets:
        for name in "ABCD":
            bucket_step(name)
    norm1_grad, norm2_grad = v["gains"]
    qkv_grad, out_grad, fc_grad, proj_grad = (
        v[name].reshape(layers, -1, v[name].shape[-1]) for name in ("qkv", "out", "fc", "proj")
    )
    return *v["home"], norm1_grad, qkv_grad, out_grad, norm2_grad, fc_grad, proj_grad


def solution(mesh):
    block = P("dp", "seq", None)
    return jax.shard_map(
        functools.partial(per_device, (mesh.shape["dp"], mesh.shape["seq"])),
        mesh=mesh,
        in_specs=(block, P(), P(), P(), P(), P(), P(), P("dp"), P(), block),
        out_specs=(block, block, P(), P(), P(), P(), P(), P()),
        check_vma=False,
    )
```

```python
import functools
import math

import jax
import jax.numpy as jnp
from jax import lax
from jax.experimental import pallas as pl
from jax.experimental.pallas import tpu as pltpu
from jax.sharding import PartitionSpec as P

HEADS = 6
EPSILON = 1e-05
NEGATIVE = -1e30
BF = jnp.bfloat16
F32 = jnp.float32
ALL = ("dp", "seq")
LANES = 128
GAIN_ROWS = 16
SCHEDULE = """
BA1a A BA1b BT A BF B A BA0a BA0b C A B BE C B D A C B D A C D B C D SG B C D A B C D A PG D B D
"""
MB = 1024 * 1024
VMEM = pltpu.VMEM
SMEM = pltpu.SMEM


def mm(a, b):
    return lax.dot_general(a, b, (((1,), (0,)), ((), ())), preferred_element_type=F32)


def mm_t(a, b):
    return lax.dot_general(a, b, (((1,), (1,)), ((), ())), preferred_element_type=F32)


def t_mm(a, b):
    return lax.dot_general(a, b, (((0,), (0,)), ((), ())), preferred_element_type=F32)


class Order:
    def __init__(self):
        self.last = []

    def after(self, x):
        x, *last = lax.optimization_barrier((x, *self.last))
        self.last = last[-1:]
        return x

    def add(self, result):
        self.last = [result, *self.last]


def call(body, name, ins, outs, scratch=(), limit=16, flops=0, transcendentals=0, grid=(1,), aliases=None, order=None):
    moved = sum(math.prod(o[0]) * jnp.dtype(o[1]).itemsize for o in outs)
    moved += sum(a.size * a.dtype.itemsize for a, _ in ins)
    kernel = body
    if order is not None:
        count, more = len(ins), len(order.last)
        ins = [*ins, *((x, pl.BlockSpec(memory_space=pl.ANY)) for x in order.last)]
        order.last = []
        results_at = count + more + len(outs)
        outs = [*outs, ((8, LANES), F32, whole(8, LANES))]

        def kernel(*refs):
            body(*refs[:count], *refs[count + more : results_at], *refs[results_at + 1 :])
            refs[results_at][...] = jnp.zeros((8, LANES), F32)

    results = pl.pallas_call(
        kernel,
        out_shape=[pltpu.HBM(o[0], o[1]) if len(o) > 3 else jax.ShapeDtypeStruct(o[0], o[1]) for o in outs],
        grid=grid,
        in_specs=[s for _, s in ins],
        out_specs=[o[2] for o in outs],
        scratch_shapes=list(scratch),
        input_output_aliases=aliases or {},
        compiler_params=pltpu.CompilerParams(vmem_limit_bytes=limit * MB),
        cost_estimate=pl.CostEstimate(flops=flops, bytes_accessed=moved, transcendentals=transcendentals),
        name=name,
    )(*[a for a, _ in ins])
    if order is not None:
        *results, token = results
        order.add(token)
    return results


def whole(*shape):
    return pl.BlockSpec(shape, lambda *_: (0,) * len(shape))


def layer_of(index, *shape):
    return pl.BlockSpec((None,) + shape, lambda *_: (index,) + (0,) * len(shape))


def in_hbm(x):
    return pltpu.with_memory_space_constraint(x, pltpu.HBM), pl.BlockSpec(memory_space=pltpu.HBM)


def scalars():
    return pl.BlockSpec(memory_space=SMEM)


def norm_parts(values):
    centre = jnp.mean(values, axis=-1, keepdims=True)
    centred = values - centre
    spread = jnp.mean(centred * centred, axis=-1, keepdims=True)
    inverse = lax.rsqrt(spread + EPSILON)
    return centred * inverse, inverse


def norm_back(grad, zhat, inverse, gain):
    e = grad * gain
    return inverse * (
        e
        - jnp.mean(e, axis=-1, keepdims=True)
        - zhat * jnp.mean(e * zhat, axis=-1, keepdims=True)
    )


def qkv_step(hidden, gain, weight, a_ref, q_ref, kv_ref, scale):
    zhat, _ = norm_parts(hidden)
    a = (zhat * gain).astype(BF)
    a_ref[...] = a
    packed = mm(a, weight).astype(BF)
    width = a.shape[1]
    q_ref[...] = packed[:, :width] * jnp.asarray(scale, BF)
    kv_ref[...] = packed[:, width:]


def first_body(scale, ha_ref, hb_ref, gain_ref, w_ref, h_ref, a_ref, q_ref, kv_ref):
    span = ha_ref.shape[0]
    h_ref[:span] = ha_ref[...].astype(F32)
    h_ref[span:] = hb_ref[...].astype(F32)
    qkv_step(h_ref[...], gain_ref[0:1], w_ref[...], a_ref, q_ref, kv_ref, scale)


def attend_body(block, info_ref, q_ref, kv_ref, kx_ref, bias_ref, hot_ref, p_ref, att_ref, inv_ref):
    tokens, width = q_ref.shape
    head = LANES // 2
    ones = jnp.ones((tokens, LANES), BF)

    def beside(a, b):
        return jnp.concatenate([a, b], axis=1)

    lower = lax.broadcasted_iota(jnp.int32, (tokens, LANES), 1) < head
    at_q = lax.broadcasted_iota(jnp.int32, (block, block), 0)
    at_k = lax.broadcasted_iota(jnp.int32, (block, block), 1)
    prefix = info_ref[0]
    for pair in range(width // LANES):
        cols = slice(pair * LANES, (pair + 1) * LANES)
        vcols = slice(width + pair * LANES, width + (pair + 1) * LANES)
        keys = jnp.concatenate([beside(kv_ref[:, cols], bias_ref[:tokens]), beside(kx_ref[:, cols], bias_ref[tokens:])], axis=0)
        values = jnp.concatenate([beside(kv_ref[:, vcols], ones), beside(kx_ref[:, vcols], ones)], axis=0)
        q = q_ref[:, cols]
        scores = []
        for n in range(2):
            qn = jnp.where(lower if n == 0 else ~lower, q, jnp.zeros_like(q))
            scores.append(mm_t(beside(qn, hot_ref[...]), keys))
        chances = []
        for n in range(2):
            rows = []
            for t in range(tokens // block):
                s = scores[n][t * block : (t + 1) * block]
                seen = (at_k <= at_q) | (info_ref[1 + t] * block + at_k < prefix)
                pieces = [s[:, : t * block], jnp.where(seen, s[:, t * block : (t + 1) * block], NEGATIVE), s[:, (t + 1) * block :]]
                s = jnp.concatenate([piece for piece in pieces if piece.shape[1]], axis=1)
                rows.append(jnp.exp(s - jnp.max(s, axis=1, keepdims=True)).astype(BF))
            p = jnp.concatenate(rows, axis=0)
            p_ref[2 * pair + n] = p
            chances.append(p)
        even, odd = [mm(p, values) for p in chances]
        inverse = 1.0 / jnp.where(lower, even[:, LANES:], odd[:, LANES:])
        inv_ref[:, cols] = inverse
        att_ref[:, cols] = (jnp.where(lower, even[:, :LANES], odd[:, :LANES]) * inverse).astype(BF)


def feed(h_ref, att_ref, wout_ref, gain, wfc_ref, wproj_ref, mid_ref, sec_ref, act_ref, gp_ref):
    middle = h_ref[...] + mm(att_ref[...], wout_ref[...])
    mid_ref[...] = middle
    zhat, _ = norm_parts(middle)
    second = (zhat * gain).astype(BF)
    sec_ref[...] = second
    total = middle
    width = middle.shape[1]
    for j in range(wfc_ref.shape[1] // width):
        cols = slice(j * width, (j + 1) * width)
        lifted = mm(second, wfc_ref[:, cols])
        phi = 0.5 * (1.0 + lax.erf(lifted * (1.0 / math.sqrt(2.0))))
        slope = phi + lifted * jnp.exp(-0.5 * lifted * lifted) * (1.0 / math.sqrt(2.0 * math.pi))
        gp_ref[:, cols] = slope.astype(BF)
        act = (lifted * phi).astype(BF)
        act_ref[:, cols] = act
        total = total + mm(act, wproj_ref[cols, :])
    return total


def middle_body(scale, layer, h_ref, att_ref, wout_ref, g2_ref, wfc_ref, wproj_ref, g1_ref, wqkv_ref,
                mid_ref, sec_ref, act_ref, gp_ref, out_ref, a_ref, q_ref, kv_ref):
    out = feed(h_ref, att_ref, wout_ref, g2_ref[layer : layer + 1], wfc_ref, wproj_ref, mid_ref, sec_ref, act_ref, gp_ref)
    out_ref[...] = out
    qkv_step(out, g1_ref[layer + 1 : layer + 2], wqkv_ref[...], a_ref, q_ref, kv_ref, scale)


def relative(bits, index, core):
    place = 0
    for mine, others in bits:
        place = 2 * place + (jnp.where(core == 0, index >> mine, index >> others) & 1)
    return place


def hand_out(bits, at_ref, g_ref, keep_ref, send_ref):
    index = at_ref[0]
    core = index & 1
    count = keep_ref.shape[0]
    for ref, side in ((keep_ref, core), (send_ref, 1 - core)):
        place = relative(bits, index, side)
        for i in range(count):
            ref[i] = g_ref[side * count + (place ^ i)]


def put_rows(g_ref, at, values, first=0, total=None):
    share = (total or values.shape[0]) // g_ref.shape[0]
    done = 0
    while done < values.shape[0]:
        block, row = divmod(first + done, share)
        count = min(share - row, values.shape[0] - done)
        g_ref[block, at + row : at + row + count] = values[done : done + count]
        done += count


def back_proj(upstream, act_ref, gp_ref, wproj_ref, g_ref, at, lift_ref):
    down = upstream.astype(BF)
    width = down.shape[1]
    for j in range(act_ref.shape[1] // width):
        cols = slice(j * width, (j + 1) * width)
        put_rows(g_ref, at, t_mm(act_ref[:, cols], down).astype(BF), j * width, act_ref.shape[1])
        lift_ref[:, cols] = (mm_t(down, wproj_ref[cols, :]) * gp_ref[:, cols].astype(F32)).astype(BF)


def back_fc(upstream, lift_ref, sec_ref, mid_ref, att_ref, wfc_ref, wout_ref, gain, g_ref, at, mg_ref, ag_ref, gain_ref):
    second = sec_ref[...]
    width = second.shape[1]
    inner = lift_ref.shape[1]
    second_grad = None
    for j in range(inner // width):
        cols = slice(j * width, (j + 1) * width)
        lift = lift_ref[:, cols]
        put_rows(g_ref, at + j * width // g_ref.shape[0], t_mm(second, lift).astype(BF))
        term = mm_t(lift, wfc_ref[:, cols])
        second_grad = term if second_grad is None else second_grad + term
    zhat, inverse = norm_parts(mid_ref[...])
    gain_ref[...] = jnp.broadcast_to(jnp.sum(second_grad * zhat, axis=0, keepdims=True), gain_ref.shape)
    mg = upstream + norm_back(second_grad, zhat, inverse, gain)
    mg_ref[...] = mg
    branch = mg.astype(BF)
    put_rows(g_ref, at + inner // g_ref.shape[0], t_mm(att_ref[...], branch).astype(BF))
    ag_ref[...] = mm_t(branch, wout_ref[...]).astype(BF)


def turn_body(layer, bits, core_ref, h_ref, att_ref, wout_ref, g2_ref, wfc_ref, wproj_ref, ua_ref, ub_ref,
              oa_ref, ob_ref, keep_ref, send_ref, mg_ref, ag_ref, gain_ref,
              mid_ref, sec_ref, act_ref, gp_ref, lift_ref, g_ref):
    gain = g2_ref[layer : layer + 1]
    out = feed(h_ref, att_ref, wout_ref, gain, wfc_ref, wproj_ref, mid_ref, sec_ref, act_ref, gp_ref)
    span = oa_ref.shape[0]
    oa_ref[...] = out[:span].astype(BF)
    ob_ref[...] = out[span:].astype(BF)
    upstream = jnp.concatenate([ua_ref[...], ub_ref[...]], axis=0).astype(F32)
    back_proj(upstream, act_ref, gp_ref, wproj_ref, g_ref, 0, lift_ref)
    back_fc(upstream, lift_ref, sec_ref, mid_ref, att_ref, wfc_ref, wout_ref, gain, g_ref, act_ref.shape[1] // g_ref.shape[0],
            mg_ref, ag_ref, gain_ref)
    hand_out(bits, core_ref, g_ref, keep_ref, send_ref)


def back_fc_body(layer, bits, core_ref, u_ref, lift_ref, sec_ref, mid_ref, att_ref, wfc_ref, wout_ref, g2_ref,
                 keep_ref, send_ref, mg_ref, ag_ref, gain_ref, g_ref):
    back_fc(u_ref[...], lift_ref, sec_ref, mid_ref, att_ref, wfc_ref, wout_ref, g2_ref[layer : layer + 1], g_ref, 0,
            mg_ref, ag_ref, gain_ref)
    hand_out(bits, core_ref, g_ref, keep_ref, send_ref)


def back_attend_body(scale, first, q_ref, kv_ref, kx_ref, p_ref, att_ref, inv_ref, ag_ref, dq_ref, own_ref, oth_ref):
    tokens, width = q_ref.shape
    head = LANES // 2
    lower = lax.broadcasted_iota(jnp.int32, (tokens, LANES), 1) < head
    for pair in range(dq_ref.shape[1] // LANES):
        out = slice(pair * LANES, (pair + 1) * LANES)
        cols = slice((first + pair) * LANES, (first + pair + 1) * LANES)
        vcols = slice(width + (first + pair) * LANES, width + (first + pair + 1) * LANES)
        q = q_ref[:, cols]
        scaled = ag_ref[:, cols].astype(F32) * inv_ref[:, cols]
        product = scaled * att_ref[:, cols].astype(F32)
        keys = jnp.concatenate([kv_ref[:, cols], kx_ref[:, cols]], axis=0)
        values = jnp.concatenate([kv_ref[:, vcols], kx_ref[:, vcols]], axis=0)
        dq = dk = dv = None
        for n in range(2):
            mine = lower if n == 0 else ~lower
            qn = jnp.where(mine, q, jnp.zeros_like(q))
            gn = jnp.where(mine, scaled, 0.0).astype(BF)
            delta = jnp.sum(jnp.where(mine, product, 0.0), axis=1, keepdims=True)
            p = p_ref[2 * (first + pair) + n]
            ds = (p.astype(F32) * (mm_t(gn, values) - delta)).astype(BF)
            dqn, dkn, dvn = mm(ds, keys), t_mm(qn, ds), t_mm(gn, p)
            if n == 0:
                dq, dk, dv = dqn, dkn, dvn
            else:
                dq, dk, dv = jnp.where(lower, dq, dqn), dk + dkn, dv + dvn
        dq_ref[:, out] = (dq * scale).astype(BF)
        for i, grad in enumerate((dk.T, dv.T)):
            own_ref[i, :, out] = grad[:tokens]
            oth_ref[i, :, out] = grad[tokens:].astype(BF)


def back_qkv(layer, parts, a_ref, h_ref, g1_ref, w_ref, mg_ref, g_ref):
    a = a_ref[...]
    width = a.shape[1]
    blocks = [jnp.concatenate([dq[...] for dq, _, _ in parts], axis=1)]
    for i in range(2):
        blocks.append(jnp.concatenate([(own[i] + got[i].astype(F32)).astype(BF) for _, own, got in parts], axis=1))
    grad = None
    for j, block in enumerate(blocks):
        put_rows(g_ref, j * width // g_ref.shape[0], t_mm(a, block).astype(BF))
        term = mm_t(block, w_ref[:, j * width : (j + 1) * width])
        grad = term if grad is None else grad + term
    zhat, inverse = norm_parts(h_ref[...])
    gain_grad = jnp.sum(grad * zhat, axis=0, keepdims=True)
    return mg_ref[...] + norm_back(grad, zhat, inverse, g1_ref[layer : layer + 1]), gain_grad


def back_turn_body(layer, bits, core_ref, *refs):
    parts, refs = (refs[:3], refs[3:6]), refs[6:]
    (a_ref, h_ref, g1_ref, w_ref, mg_ref, act_ref, gp_ref, wproj_ref,
     keep_ref, send_ref, up_ref, gain_ref, lift_ref, g_ref) = refs
    up, gain_grad = back_qkv(layer, parts, a_ref, h_ref, g1_ref, w_ref, mg_ref, g_ref)
    gain_ref[...] = jnp.broadcast_to(gain_grad, gain_ref.shape)
    up_ref[...] = up
    back_proj(up, act_ref, gp_ref, wproj_ref, g_ref, 3 * up.shape[1] // g_ref.shape[0], lift_ref)
    hand_out(bits, core_ref, g_ref, keep_ref, send_ref)


def back_both_body(layer, bits, core_ref, *refs):
    parts, refs = (refs[:3], refs[3:6]), refs[6:]
    (a_ref, h_ref, g1_ref, w_ref, mg_ref, act_ref, gp_ref, wproj_ref, sec_ref, mid_ref, att_ref, wfc_ref, wout_ref, g2_ref,
     keep_ref, send_ref, mg_out, ag_ref, gain1_ref, gain2_ref, g_ref, up_ref, lift_ref) = refs
    up, gain_grad = back_qkv(layer, parts, a_ref, h_ref, g1_ref, w_ref, mg_ref, g_ref)
    gain1_ref[...] = jnp.broadcast_to(gain_grad, gain1_ref.shape)
    up_ref[...] = up
    at = 3 * up.shape[1]
    back_proj(up, act_ref, gp_ref, wproj_ref, g_ref, at // g_ref.shape[0], lift_ref)
    at += act_ref.shape[1]
    back_fc(up_ref[...], lift_ref, sec_ref, mid_ref, att_ref, wfc_ref, wout_ref, g2_ref[layer - 1 : layer], g_ref, at // g_ref.shape[0],
            mg_out, ag_ref, gain2_ref)
    hand_out(bits, core_ref, g_ref, keep_ref, send_ref)


def back_end_body(layer, bits, core_ref, *refs):
    parts, refs = (refs[:3], refs[3:6]), refs[6:]
    (a_ref, h_ref, g1_ref, w_ref, mg_ref, oa_ref, ob_ref, *gain_refs, keep_ref, send_ref, to_a_ref, to_b_ref, g_ref) = refs
    up, gain_grad = back_qkv(layer, parts, a_ref, h_ref, g1_ref, w_ref, mg_ref, g_ref)
    span = oa_ref.shape[0]
    width = up.shape[1]
    to_a_ref[0] = oa_ref[...]
    to_b_ref[0] = ob_ref[...]
    to_a_ref[1] = up[:span].astype(BF)
    to_b_ref[1] = up[span:].astype(BF)
    at = 3 * width // g_ref.shape[0]
    for i, gain in enumerate([gain_grad] + [ref[0:1] for ref in gain_refs]):
        put_rows(g_ref, at + i, jnp.broadcast_to(gain, (g_ref.shape[0], width)).astype(BF))
    at += 1 + len(gain_refs)
    for block in range(g_ref.shape[0]):
        g_ref[block, at:] = jnp.zeros((g_ref.shape[1] - at, width), BF)
    hand_out(bits, core_ref, g_ref, keep_ref, send_ref)


def masks_body(per_span, block, ids_ref, order_ref, own_ref, other_ref, w_in, g_in, bias_ref, hot_ref, info_ref, w_ref, g_ref, sem):
    copies = [pltpu.make_async_copy(w_in.at[0], w_ref, sem.at[0]), pltpu.make_async_copy(g_in, g_ref, sem.at[1])]
    for copy in copies:
        copy.start()
    core, place = ids_ref[0] & 1, ids_ref[1]
    odd = place & 1
    prefix = jnp.where((place >> 1) == core, own_ref[odd], other_ref[odd])
    info_ref[0] = prefix
    ranks = []
    for c in (core, 1 - core):
        for span in (2 * c + odd, 2 * c + 1 - odd):
            ranks += [order_ref[span * per_span + i] for i in range(per_span)]
    tokens = hot_ref.shape[0]
    own = tokens // block
    lane = lax.broadcasted_iota(jnp.int32, (block, LANES), 1)
    within = lax.broadcasted_iota(jnp.int32, (block, LANES), 0)
    lane_rank = jnp.full((block, LANES), -1, jnp.int32)
    for b in range(own):
        info_ref[1 + b] = ranks[b]
        lane_rank = jnp.where(lane == b, ranks[b], lane_rank)
        hot_ref[b * block : (b + 1) * block] = jnp.where(lane == b, 1.0, 0.0).astype(BF)
    for k, rank in enumerate(ranks):
        unseen = (lane < own) & (rank >= lane_rank) & (lane != k) & (rank * block + within >= prefix)
        bias_ref[k * block : (k + 1) * block] = jnp.where(unseen, NEGATIVE, 0.0).astype(BF)
    for copy in copies:
        copy.wait()


def pick_body(at_ref, x_ref, a_ref, b_ref):
    odd = at_ref[1] & 1
    a_ref[...] = x_ref[odd]
    b_ref[...] = x_ref[1 - odd]


def place_body(odd_ref, a_ref, b_ref, *out_refs):
    odd = odd_ref[1] & 1
    for i, ref in enumerate(out_refs):
        ref[odd] = a_ref[i]
        ref[1 - odd] = b_ref[i]


def add(a, b):
    return (a.astype(F32) + b.astype(F32)).astype(BF)


def unpack_body(plan, gains, bits, groups, befores, at_ref, *refs):
    halves, refs = refs[: 2 * groups], refs[2 * groups + befores :]
    out_refs, refs = refs[: len(plan)], refs[len(plan) :]
    gain_refs, refs = refs[: len(gains)], refs[len(gains) :]
    *stage_refs, sem = refs
    index = at_ref[0]
    core = index & 1
    copies = []
    for group in range(groups):
        a_ref, b_ref = halves[2 * group : 2 * group + 2]
        count, _, width = a_ref.shape
        mine = [(at, layer, out, stage) for (g, at, layer), out, stage in zip(plan, out_refs, stage_refs) if g == group]
        for ref, side in ((a_ref, core), (b_ref, 1 - core)):
            place = relative(bits, index, side)
            for i in range(count):
                block = side * count + (place ^ i)
                for at, layer, out_ref, stage_ref in mine:
                    _, rows, cols = stage_ref.shape
                    for j in range(cols // width):
                        stage_ref[block, :, j * width : (j + 1) * width] = ref[i, at + j * rows : at + (j + 1) * rows].astype(F32)
                    copies.append(pltpu.make_async_copy(stage_ref.at[block], out_ref.at[layer, block], sem.at[len(copies)]))
                    copies[-1].start()
    for rows, ref in zip(gains, gain_refs):
        ref[...] = jnp.concatenate([halves[-2][0, row : row + 1] for row in rows], axis=0).astype(F32)
    for copy in copies:
        copy.wait()


def unpack(bits, at, groups, layers, gains, order):
    ins = [(at, scalars())] + [(x, whole(*x.shape)) for halves, _ in groups for x in halves]
    aliases = {}
    outs, plan = [], []
    count, _, width = groups[0][0][0].shape
    blocks = 2 * count
    scratch = []
    for group, (_, parts) in enumerate(groups):
        for row, layer, shape, before in parts:
            if before is not None:
                aliases[len(ins)] = len(outs)
                ins.append((before, pl.BlockSpec(memory_space=pltpu.HBM)))
            outs.append(((layers, blocks, shape[0] // blocks, shape[1]), F32, pl.BlockSpec(memory_space=pltpu.HBM), True))
            plan.append((group, row, layer))
            scratch.append(VMEM((blocks, shape[0] // blocks, shape[1]), F32))
    outs += [((len(rows), width), F32, whole(len(rows), width)) for rows in gains]
    return call(
        functools.partial(unpack_body, plan, gains, bits, len(groups), len(aliases)), "unpack", ins, outs,
        scratch=[*scratch, pltpu.SemaphoreType.DMA((blocks * len(plan),))], limit=24, aliases=aliases, order=order,
    )


def per_device(mesh_shape, hidden_in, norm1_gain, qkv_weight, out_weight, norm2_gain, fc_weight, proj_weight,
               prefix_len, block_order, grad_out):
    dp, seq = mesh_shape
    rows_here, span, width = hidden_in.shape
    layers = qkv_weight.shape[0]
    inner = fc_weight.shape[2]
    scale = 1.0 / math.sqrt(width // HEADS)
    row_length = span * seq
    block_count = block_order.shape[0]
    block = row_length // block_count
    per_span = span // block
    tokens = 2 * span
    pairs = width // LANES
    assert rows_here == 2 and seq == 4 and dp % 2 == 0 and layers == 2
    di, si = lax.axis_index("dp"), lax.axis_index("seq")
    at = jnp.stack([di, si]).astype(jnp.int32)
    order = Order()

    def spot(d, s):
        return d * seq + s

    perm_a = [(spot(d, s), spot((d & ~1) | (s >> 1), 2 * (d & 1) + (s & 1))) for d in range(dp) for s in range(seq)]
    perm_b = [(spot(d, s), spot((d & ~1) | (s >> 1), 2 * (d & 1) + 1 - (s & 1))) for d in range(dp) for s in range(seq)]
    back_a = [(b, a) for a, b in perm_a]
    back_b = [(b, a) for a, b in perm_b]
    pair_perm = [(spot(d, s), spot(d ^ 1, s)) for d in range(dp) for s in range(seq)]
    t_w = (tokens, width)
    full = whole(*t_w)
    half_spec = whole(span, width)
    both_spec = whole(2, span, width)

    def pair(x):
        return lax.ppermute(x, ALL, pair_perm)

    def pick(x):
        return call(
            pick_body, "pick", [(at, scalars()), (x, both_spec)], [((span, width), BF, half_spec)] * 2, limit=4, order=order
        )

    def spread(first, other):
        return lax.ppermute(first, ALL, perm_a), lax.ppermute(other, ALL, perm_b)

    class Collect:
        def __init__(self, a, b):
            self.a, self.b = lax.ppermute(a, ALL, back_a), lax.ppermute(b, ALL, back_b)

        def done(self, order):
            return call(
                place_body, "place", [(at, scalars()), (self.a, both_spec), (self.b, both_spec)],
                [((2, span, width), BF, both_spec, True)] * 2, limit=8, order=order,
            )

    dp_bits = [i for i in range(1, dp.bit_length() - 1)]
    seq_bits = [i for i in range(seq.bit_length() - 1)]
    orders = (dp_bits, dp_bits[::-1])
    z_orders = (seq_bits, seq_bits[::-1])
    bits = list(zip(*orders))
    blocks = 2 ** (len(dp_bits) + 1)

    own_blocks = tokens // block
    ha, hb = spread(*pick(hidden_in))
    grad_pieces = pick(grad_out)
    prefix_other = pair(prefix_len)
    bias, hot, info, first_weight, first_gain = call(
        functools.partial(masks_body, per_span, block), "masks",
        [(at, scalars()), (block_order, scalars()), (prefix_len, scalars()), (prefix_other, scalars()),
         in_hbm(qkv_weight), in_hbm(norm1_gain)],
        [((2 * tokens, LANES), BF, whole(2 * tokens, LANES)), ((tokens, LANES), BF, whole(tokens, LANES)),
         ((1 + own_blocks,), jnp.int32, scalars()),
         ((width, 3 * width), BF, whole(width, 3 * width)), ((layers, width), F32, whole(layers, width))],
        scratch=[pltpu.SemaphoreType.DMA((2,))], order=order,
    )

    wide = whole(tokens, inner)
    gains = whole(layers, width)
    dense = 2 * tokens * width

    def qkv_out():
        return [(t_w, BF, full), (t_w, BF, full), ((tokens, 2 * width), BF, whole(tokens, 2 * width))]

    h, a, q, kv = call(
        functools.partial(first_body, scale), "first",
        [(ha, half_spec), (hb, half_spec), (first_gain, gains), (first_weight, whole(width, 3 * width))],
        [(t_w, F32, full)] + qkv_out(),
        flops=dense * 3 * width, order=order,
    )
    kv_spec = whole(tokens, 2 * width)
    p_spec = whole(HEADS, tokens, 2 * tokens)

    def attend(q, kv, kv_other):
        return call(
            functools.partial(attend_body, block), "attend",
            [(info, scalars()), (q, full), (kv, kv_spec), (kv_other, kv_spec), (bias, whole(2 * tokens, LANES)), (hot, whole(tokens, LANES))],
            [((HEADS, tokens, 2 * tokens), BF, p_spec), (t_w, BF, full), (t_w, F32, full)],
            flops=4 * tokens * 2 * tokens * 256 * HEADS, transcendentals=HEADS * tokens * 2 * tokens, limit=20, order=order,
        )

    def feed_ins(layer, h, att):
        return [
            (h, full), (att, full), (out_weight, layer_of(layer, width, width)), (norm2_gain, gains),
            (fc_weight, layer_of(layer, width, inner)), (proj_weight, layer_of(layer, inner, width)),
        ]

    def swap_dp(x, step):
        return lax.ppermute(x, ALL, [(spot(d, s), spot(d ^ (1 << orders[d & 1][step]), s)) for d in range(dp) for s in range(seq)])

    def swap_seq(x, step):
        return lax.ppermute(x, ALL, [(spot(d, s), spot(d, s ^ (1 << z_orders[d & 1][step]))) for d in range(dp) for s in range(seq)])

    class Bucket:
        def __init__(self, keep, send):
            self.halves = None
            self.parts = None
            self.steps = self.run(keep, send)
            next(self.steps)

        def run(self, keep, send):
            got = pair(send)
            for step in range(len(dp_bits)):
                yield
                total = add(keep, order.after(got))
                half = total.shape[0] // 2
                keep, send = total[:half], total[half:]
                order.add(keep)
                got = swap_dp(send, step)
            self.parts = [(keep, got)]
            yield
            yield from self.rest()

        def rest(self):
            total = jnp.concatenate([add(keep, order.after(got)) for keep, got in self.parts], axis=1)
            order.add(total)
            for step in range(len(seq_bits)):
                got = swap_seq(total, step)
                yield
                total = add(total, order.after(got))
                order.add(total)
            for step in reversed(range(len(dp_bits))):
                got = swap_dp(total, step)
                yield
                total = jnp.concatenate([total, order.after(got)], axis=0)
                order.add(total)
            self.halves = (total, pair(total))
            yield

        def step(self):
            next(self.steps)

    def bucket_outs(rows):
        count = 2 ** len(dp_bits)
        size = rows // (2 * count)
        assert size * 2 * count == rows
        return [((count, size, width), BF, whole(count, size, width))] * 2, [VMEM((2 * count, size, width), BF)]

    gain_out = ((8, width), F32, whole(8, width))

    kv_other = pair(kv)
    ua, ub = spread(*[order.after(x) for x in grad_pieces])
    p, att, inv = attend(q, kv, kv_other)
    order.last += [ua, ub]
    mid, sec, act, gp, h_next, a_next, q_next, kv_next = call(
        functools.partial(middle_body, scale, 0), "middle",
        feed_ins(0, h, att) + [(norm1_gain, gains), (qkv_weight, layer_of(1, width, 3 * width))],
        [(t_w, F32, full), (t_w, BF, full), ((tokens, inner), BF, wide), ((tokens, inner), BF, wide), (t_w, F32, full)] + qkv_out(),
        flops=dense * (4 * width + 2 * inner), transcendentals=2 * tokens * inner, limit=18, order=order,
    )
    saved = (h, a, q, kv, kv_other, p, att, inv)
    h, a, q, kv = h_next, a_next, q_next, kv_next

    kv_other = pair(kv)
    p, att, inv = attend(q, kv, kv_other)
    outs, scratch = bucket_outs(2 * inner + width)
    oa, ob, keep, send, mg, ag, gain2_1 = call(
        functools.partial(turn_body, 1, bits), "turn",
        [(at, scalars())] + feed_ins(1, h, att) + [(ua, half_spec), (ub, half_spec)],
        [((span, width), BF, half_spec)] * 2 + outs + [(t_w, F32, full), (t_w, BF, full), gain_out],
        scratch=[VMEM(t_w, F32), VMEM(t_w, BF)] + [VMEM((tokens, inner), BF)] * 3 + scratch,
        flops=dense * (3 * width + 6 * inner), transcendentals=2 * tokens * inner, limit=24, order=order,
    )
    feed_1 = Bucket(keep, send)

    def back_attend(first, count, q, kv, kv_other, p, att, inv, ag):
        out = (tokens, count * LANES)
        dq, own, oth = call(
            functools.partial(back_attend_body, scale, first), "back_attend",
            [(q, full), (kv, kv_spec), (kv_other, kv_spec), (p, p_spec), (att, full), (inv, full), (ag, full)],
            [(out, BF, whole(*out)), ((2, *out), F32, whole(2, *out)), ((2, *out), BF, whole(2, *out))],
            flops=8 * tokens * 2 * tokens * 256 * 2 * count, limit=20, order=order,
        )
        return dq, own, pair(oth)

    def part_ins(parts):
        return [(x, whole(*x.shape)) for part in parts for x in part]

    layer_1 = (q, kv, kv_other, p, att, inv)
    h_1, a_1, mg_1, ag_1 = h, a, mg, ag
    h_0, a_0, *layer_0 = saved
    v = {}
    buckets = {"A": feed_1}

    def back_turn():
        outs, scratch = bucket_outs(3 * width + inner)
        keep, send, v["up"], v["gain1_1"], v["lift"] = call(
            functools.partial(back_turn_body, 1, bits), "back_turn",
            [(at, scalars())] + part_ins((v["1a"], v["1b"])) + [
                (a_1, full), (h_1, full), (norm1_gain, gains), (qkv_weight, layer_of(1, width, 3 * width)), (mg_1, full),
                (act, wide), (gp, wide), (proj_weight, layer_of(0, inner, width))],
            outs + [(t_w, F32, full), gain_out, ((tokens, inner), BF, wide)],
            scratch=scratch, flops=dense * (6 * width + 2 * inner), limit=18, order=order,
        )
        buckets["B"] = Bucket(keep, send)

    def back_fc_0():
        outs, scratch = bucket_outs(inner + width)
        keep, send, v["mg"], v["ag"], v["gain2_0"] = call(
            functools.partial(back_fc_body, 0, bits), "back_fc",
            [(at, scalars()), (v["up"], full), (v["lift"], wide), (sec, full), (mid, full), (layer_0[4], full),
             (fc_weight, layer_of(0, width, inner)), (out_weight, layer_of(0, width, width)), (norm2_gain, gains)],
            outs + [(t_w, F32, full), (t_w, BF, full), gain_out],
            scratch=scratch, flops=dense * (2 * width + 2 * inner), limit=16, order=order,
        )
        buckets["C"] = Bucket(keep, send)

    def back_both():
        outs, scratch = bucket_outs(4 * width + 2 * inner)
        keep, send, v["mg"], v["ag"], v["gain1_1"], v["gain2_0"] = call(
            functools.partial(back_both_body, 1, bits), "back_both",
            [(at, scalars())] + part_ins((v["1a"], v["1b"])) + [
                (a_1, full), (h_1, full), (norm1_gain, gains), (qkv_weight, layer_of(1, width, 3 * width)), (mg_1, full),
                (act, wide), (gp, wide), (proj_weight, layer_of(0, inner, width)), (sec, full), (mid, full), (layer_0[4], full),
                (fc_weight, layer_of(0, width, inner)), (out_weight, layer_of(0, width, width)), (norm2_gain, gains)],
            outs + [(t_w, F32, full), (t_w, BF, full), gain_out, gain_out],
            scratch=scratch + [VMEM(t_w, F32), VMEM((tokens, inner), BF)], flops=dense * (8 * width + 4 * inner), limit=24, order=order,
        )
        v["both"] = True
        buckets["B"] = Bucket(keep, send)

    def back_end():
        outs, scratch = bucket_outs(3 * width + GAIN_ROWS * blocks)
        keep, send, ga, gb = call(
            functools.partial(back_end_body, 0, bits), "back_end",
            [(at, scalars())] + part_ins((v["0a"], v["0b"])) + [
                (a_0, full), (h_0, full), (norm1_gain, gains), (qkv_weight, layer_of(0, width, 3 * width)), (v["mg"], full),
                (oa, half_spec), (ob, half_spec)]
            + [(g, whole(8, width)) for g in (v["gain1_1"], v["gain2_0"], gain2_1)],
            outs + [((2, span, width), BF, both_spec)] * 2,
            scratch=scratch, flops=2 * dense * 3 * width, limit=12, order=order,
        )
        buckets["D"] = Bucket(keep, send)
        v["ga"], v["gb"] = ga, gb

    def run_part(name, first, count, layer, ag):
        v[name] = back_attend(first, count, *layer, ag)

    parts_of = {
        "A": [(0, 1, (inner, width), "proj"), (inner, 1, (width, inner), "fc"), (2 * inner, 1, (width, width), "out")],
        "B": [(0, 1, (width, 3 * width), "qkv"), (3 * width, 0, (inner, width), "proj")],
        "C": [(0, 0, (width, inner), "fc"), (inner, 0, (width, width), "out")],
        "D": [(0, 0, (width, 3 * width), "qkv")],
    }

    def unpacked(names):
        last = "D" in names
        groups = [
            (buckets.pop(name).halves, [(row // blocks, layer, shape, v.get(key)) for row, layer, shape, key in parts_of[name]])
            for name in names
        ]
        gain_rows = [[3 * width // blocks + i for i in pair] for pair in ((0, 1), (2, 3))] if last else []
        got = unpack(bits, at, groups, layers, gain_rows, order)
        keys = [part[3] for name in names for part in parts_of[name]]
        v.update(zip(keys, got))
        if last:
            v["gains"] = got[len(keys) : len(keys) + 2]

    def bucket_step(name):
        if name not in buckets:
            return
        if buckets[name].halves is None:
            buckets[name].step()
        elif name == "D":
            while "C" in buckets and buckets["C"].halves is None:
                buckets["C"].step()
            unpacked([n for n in "CD" if n in buckets])
        elif name != "C":
            unpacked([name])

    kernels = {
        "BA1a": lambda: run_part("1a", 0, 1, layer_1, ag_1),
        "BA1b": lambda: run_part("1b", 1, pairs - 1, layer_1, ag_1),
        "BT": back_turn,
        "BF": back_fc_0,
        "BTF": back_both,
        "BA0a": lambda: run_part("0a", 0, 1, layer_0, v["ag"]),
        "BA0b": lambda: run_part("0b", 1, pairs - 1, layer_0, v["ag"]),
        "BE": back_end,
        "PG": lambda: v.update(home=v["home"].done(order)),
        "SG": lambda: v.update(home=Collect(order.after(v["ga"]), order.after(v["gb"]))),
    }
    for token in SCHEDULE.split():
        if token in kernels:
            kernels[token]()
        else:
            bucket_step(token)
    while buckets:
        for name in "ABCD":
            bucket_step(name)
    norm1_grad, norm2_grad = v["gains"]
    qkv_grad, out_grad, fc_grad, proj_grad = (
        v[name].reshape(layers, -1, v[name].shape[-1]) for name in ("qkv", "out", "fc", "proj")
    )
    return *v["home"], norm1_grad, qkv_grad, out_grad, norm2_grad, fc_grad, proj_grad


def solution(mesh):
    block = P("dp", "seq", None)
    return jax.shard_map(
        functools.partial(per_device, (mesh.shape["dp"], mesh.shape["seq"])),
        mesh=mesh,
        in_specs=(block, P(), P(), P(), P(), P(), P(), P("dp"), P(), block),
        out_specs=(block, block, P(), P(), P(), P(), P(), P()),
        check_vma=False,
    )
```

```python
import functools
import math

import jax
import jax.numpy as jnp
from jax import lax
from jax.experimental import pallas as pl
from jax.experimental.pallas import tpu as pltpu
from jax.sharding import PartitionSpec as P

HEADS = 6
EPSILON = 1e-05
NEGATIVE = -1e30
BF = jnp.bfloat16
F32 = jnp.float32
ALL = ("dp", "seq")
LANES = 128
GAIN_ROWS = 16
SCHEDULE = """
BA1a A BA1b BT A BF B A BA0a BA0b C A B BE C B D A C B D A C D B C D SG B C D A B C D A PG D B D
"""
MB = 1024 * 1024
VMEM = pltpu.VMEM
SMEM = pltpu.SMEM


def mm(a, b):
    return lax.dot_general(a, b, (((1,), (0,)), ((), ())), preferred_element_type=F32)


def mm_t(a, b):
    return lax.dot_general(a, b, (((1,), (1,)), ((), ())), preferred_element_type=F32)


def t_mm(a, b):
    return lax.dot_general(a, b, (((0,), (0,)), ((), ())), preferred_element_type=F32)


class Order:
    def __init__(self):
        self.last = []

    def after(self, x):
        x, *last = lax.optimization_barrier((x, *self.last))
        self.last = last[-1:]
        return x

    def add(self, result):
        self.last = [result, *self.last]


def call(body, name, ins, outs, scratch=(), limit=16, flops=0, transcendentals=0, grid=(1,), aliases=None, order=None):
    moved = sum(math.prod(o[0]) * jnp.dtype(o[1]).itemsize for o in outs)
    moved += sum(a.size * a.dtype.itemsize for a, _ in ins)
    kernel = body
    if order is not None:
        count, more = len(ins), len(order.last)
        ins = [*ins, *((x, pl.BlockSpec(memory_space=pl.ANY)) for x in order.last)]
        order.last = []
        results_at = count + more + len(outs)
        outs = [*outs, ((8, LANES), F32, whole(8, LANES))]

        def kernel(*refs):
            body(*refs[:count], *refs[count + more : results_at], *refs[results_at + 1 :])
            refs[results_at][...] = jnp.zeros((8, LANES), F32)

    results = pl.pallas_call(
        kernel,
        out_shape=[pltpu.HBM(o[0], o[1]) if len(o) > 3 else jax.ShapeDtypeStruct(o[0], o[1]) for o in outs],
        grid=grid,
        in_specs=[s for _, s in ins],
        out_specs=[o[2] for o in outs],
        scratch_shapes=list(scratch),
        input_output_aliases=aliases or {},
        compiler_params=pltpu.CompilerParams(vmem_limit_bytes=limit * MB),
        cost_estimate=pl.CostEstimate(flops=flops, bytes_accessed=moved, transcendentals=transcendentals),
        name=name,
    )(*[a for a, _ in ins])
    if order is not None:
        *results, token = results
        order.add(token)
    return results


def whole(*shape):
    return pl.BlockSpec(shape, lambda *_: (0,) * len(shape))


def layer_of(index, *shape):
    return pl.BlockSpec((None,) + shape, lambda *_: (index,) + (0,) * len(shape))


def in_hbm(x):
    return pltpu.with_memory_space_constraint(x, pltpu.HBM), pl.BlockSpec(memory_space=pltpu.HBM)


def scalars():
    return pl.BlockSpec(memory_space=SMEM)


def norm_parts(values):
    centre = jnp.mean(values, axis=-1, keepdims=True)
    centred = values - centre
    spread = jnp.mean(centred * centred, axis=-1, keepdims=True)
    inverse = lax.rsqrt(spread + EPSILON)
    return centred * inverse, inverse


def norm_back(grad, zhat, inverse, gain):
    e = grad * gain
    return inverse * (
        e
        - jnp.mean(e, axis=-1, keepdims=True)
        - zhat * jnp.mean(e * zhat, axis=-1, keepdims=True)
    )


def qkv_step(hidden, gain, weight, a_ref, q_ref, kv_ref, scale):
    zhat, _ = norm_parts(hidden)
    a = (zhat * gain).astype(BF)
    a_ref[...] = a
    packed = mm(a, weight).astype(BF)
    width = a.shape[1]
    q_ref[...] = packed[:, :width] * jnp.asarray(scale, BF)
    kv_ref[...] = packed[:, width:]


def first_body(scale, ha_ref, hb_ref, gain_ref, w_ref, h_ref, a_ref, q_ref, kv_ref):
    span = ha_ref.shape[0]
    h_ref[:span] = ha_ref[...].astype(F32)
    h_ref[span:] = hb_ref[...].astype(F32)
    qkv_step(h_ref[...], gain_ref[0:1], w_ref[...], a_ref, q_ref, kv_ref, scale)


def attend_body(block, info_ref, q_ref, kv_ref, kx_ref, bias_ref, hot_ref, p_ref, att_ref, inv_ref):
    tokens, width = q_ref.shape
    head = LANES // 2
    ones = jnp.ones((tokens, LANES), BF)

    def beside(a, b):
        return jnp.concatenate([a, b], axis=1)

    lower = lax.broadcasted_iota(jnp.int32, (tokens, LANES), 1) < head
    at_q = lax.broadcasted_iota(jnp.int32, (block, block), 0)
    at_k = lax.broadcasted_iota(jnp.int32, (block, block), 1)
    prefix = info_ref[0]

    @pl.loop(0, width // LANES)
    def _(pair):
        cols = pl.ds(pl.multiple_of(pair * LANES, LANES), LANES)
        vcols = pl.ds(pl.multiple_of(width + pair * LANES, LANES), LANES)
        keys = jnp.concatenate([beside(kv_ref[:, cols], bias_ref[:tokens]), beside(kx_ref[:, cols], bias_ref[tokens:])], axis=0)
        values = jnp.concatenate([beside(kv_ref[:, vcols], ones), beside(kx_ref[:, vcols], ones)], axis=0)
        q = q_ref[:, cols]
        scores = []
        for n in range(2):
            qn = jnp.where(lower if n == 0 else ~lower, q, jnp.zeros_like(q))
            scores.append(mm_t(beside(qn, hot_ref[...]), keys))
        chances = []
        for n in range(2):
            rows = []
            for t in range(tokens // block):
                s = scores[n][t * block : (t + 1) * block]
                seen = (at_k <= at_q) | (info_ref[1 + t] * block + at_k < prefix)
                pieces = [s[:, : t * block], jnp.where(seen, s[:, t * block : (t + 1) * block], NEGATIVE), s[:, (t + 1) * block :]]
                s = jnp.concatenate([piece for piece in pieces if piece.shape[1]], axis=1)
                rows.append(jnp.exp(s - jnp.max(s, axis=1, keepdims=True)).astype(BF))
            p = jnp.concatenate(rows, axis=0)
            p_ref[2 * pair + n] = p
            chances.append(p)
        even, odd = [mm(p, values) for p in chances]
        inverse = 1.0 / jnp.where(lower, even[:, LANES:], odd[:, LANES:])
        inv_ref[:, cols] = inverse
        att_ref[:, cols] = (jnp.where(lower, even[:, :LANES], odd[:, :LANES]) * inverse).astype(BF)


def feed(h_ref, att_ref, wout_ref, gain, wfc_ref, wproj_ref, mid_ref, sec_ref, act_ref, gp_ref):
    middle = h_ref[...] + mm(att_ref[...], wout_ref[...])
    mid_ref[...] = middle
    zhat, _ = norm_parts(middle)
    second = (zhat * gain).astype(BF)
    sec_ref[...] = second
    total = middle
    width = middle.shape[1]
    for j in range(wfc_ref.shape[1] // width):
        cols = slice(j * width, (j + 1) * width)
        lifted = mm(second, wfc_ref[:, cols])
        phi = 0.5 * (1.0 + lax.erf(lifted * (1.0 / math.sqrt(2.0))))
        slope = phi + lifted * jnp.exp(-0.5 * lifted * lifted) * (1.0 / math.sqrt(2.0 * math.pi))
        gp_ref[:, cols] = slope.astype(BF)
        act = (lifted * phi).astype(BF)
        act_ref[:, cols] = act
        total = total + mm(act, wproj_ref[cols, :])
    return total


def middle_body(scale, layer, h_ref, att_ref, wout_ref, g2_ref, wfc_ref, wproj_ref, g1_ref, wqkv_ref,
                mid_ref, sec_ref, act_ref, gp_ref, out_ref, a_ref, q_ref, kv_ref):
    out = feed(h_ref, att_ref, wout_ref, g2_ref[layer : layer + 1], wfc_ref, wproj_ref, mid_ref, sec_ref, act_ref, gp_ref)
    out_ref[...] = out
    qkv_step(out, g1_ref[layer + 1 : layer + 2], wqkv_ref[...], a_ref, q_ref, kv_ref, scale)


def relative(bits, index, core):
    place = 0
    for mine, others in bits:
        place = 2 * place + (jnp.where(core == 0, index >> mine, index >> others) & 1)
    return place


def hand_out(bits, at_ref, g_ref, keep_ref, send_ref):
    index = at_ref[0]
    core = index & 1
    count = keep_ref.shape[0]
    for ref, side in ((keep_ref, core), (send_ref, 1 - core)):
        place = relative(bits, index, side)
        for i in range(count):
            ref[i] = g_ref[side * count + (place ^ i)]


def put_rows(g_ref, at, values, first=0, total=None):
    share = (total or values.shape[0]) // g_ref.shape[0]
    done = 0
    while done < values.shape[0]:
        block, row = divmod(first + done, share)
        count = min(share - row, values.shape[0] - done)
        g_ref[block, at + row : at + row + count] = values[done : done + count]
        done += count


def back_proj(upstream, act_ref, gp_ref, wproj_ref, g_ref, at, lift_ref):
    down = upstream.astype(BF)
    width = down.shape[1]
    for j in range(act_ref.shape[1] // width):
        cols = slice(j * width, (j + 1) * width)
        put_rows(g_ref, at, t_mm(act_ref[:, cols], down).astype(BF), j * width, act_ref.shape[1])
        lift_ref[:, cols] = (mm_t(down, wproj_ref[cols, :]) * gp_ref[:, cols].astype(F32)).astype(BF)


def back_fc(upstream, lift_ref, sec_ref, mid_ref, att_ref, wfc_ref, wout_ref, gain, g_ref, at, mg_ref, ag_ref, gain_ref):
    second = sec_ref[...]
    width = second.shape[1]
    inner = lift_ref.shape[1]
    second_grad = None
    for j in range(inner // width):
        cols = slice(j * width, (j + 1) * width)
        lift = lift_ref[:, cols]
        put_rows(g_ref, at + j * width // g_ref.shape[0], t_mm(second, lift).astype(BF))
        term = mm_t(lift, wfc_ref[:, cols])
        second_grad = term if second_grad is None else second_grad + term
    zhat, inverse = norm_parts(mid_ref[...])
    gain_ref[...] = jnp.broadcast_to(jnp.sum(second_grad * zhat, axis=0, keepdims=True), gain_ref.shape)
    mg = upstream + norm_back(second_grad, zhat, inverse, gain)
    mg_ref[...] = mg
    branch = mg.astype(BF)
    put_rows(g_ref, at + inner // g_ref.shape[0], t_mm(att_ref[...], branch).astype(BF))
    ag_ref[...] = mm_t(branch, wout_ref[...]).astype(BF)


def turn_body(layer, bits, core_ref, h_ref, att_ref, wout_ref, g2_ref, wfc_ref, wproj_ref, ua_ref, ub_ref,
              oa_ref, ob_ref, keep_ref, send_ref, mg_ref, ag_ref, gain_ref,
              mid_ref, sec_ref, act_ref, gp_ref, lift_ref, g_ref):
    gain = g2_ref[layer : layer + 1]
    out = feed(h_ref, att_ref, wout_ref, gain, wfc_ref, wproj_ref, mid_ref, sec_ref, act_ref, gp_ref)
    span = oa_ref.shape[0]
    oa_ref[...] = out[:span].astype(BF)
    ob_ref[...] = out[span:].astype(BF)
    upstream = jnp.concatenate([ua_ref[...], ub_ref[...]], axis=0).astype(F32)
    back_proj(upstream, act_ref, gp_ref, wproj_ref, g_ref, 0, lift_ref)
    back_fc(upstream, lift_ref, sec_ref, mid_ref, att_ref, wfc_ref, wout_ref, gain, g_ref, act_ref.shape[1] // g_ref.shape[0],
            mg_ref, ag_ref, gain_ref)
    hand_out(bits, core_ref, g_ref, keep_ref, send_ref)


def back_fc_body(layer, bits, core_ref, u_ref, lift_ref, sec_ref, mid_ref, att_ref, wfc_ref, wout_ref, g2_ref,
                 keep_ref, send_ref, mg_ref, ag_ref, gain_ref, g_ref):
    back_fc(u_ref[...], lift_ref, sec_ref, mid_ref, att_ref, wfc_ref, wout_ref, g2_ref[layer : layer + 1], g_ref, 0,
            mg_ref, ag_ref, gain_ref)
    hand_out(bits, core_ref, g_ref, keep_ref, send_ref)


def back_attend_body(scale, first, q_ref, kv_ref, kx_ref, p_ref, att_ref, inv_ref, ag_ref, dq_ref, own_ref, oth_ref):
    tokens, width = q_ref.shape
    head = LANES // 2
    lower = lax.broadcasted_iota(jnp.int32, (tokens, LANES), 1) < head

    @pl.loop(0, dq_ref.shape[1] // LANES)
    def _(pair):
        out = pl.ds(pl.multiple_of(pair * LANES, LANES), LANES)
        cols = pl.ds(pl.multiple_of((first + pair) * LANES, LANES), LANES)
        vcols = pl.ds(pl.multiple_of(width + (first + pair) * LANES, LANES), LANES)
        q = q_ref[:, cols]
        scaled = ag_ref[:, cols].astype(F32) * inv_ref[:, cols]
        product = scaled * att_ref[:, cols].astype(F32)
        keys = jnp.concatenate([kv_ref[:, cols], kx_ref[:, cols]], axis=0)
        values = jnp.concatenate([kv_ref[:, vcols], kx_ref[:, vcols]], axis=0)
        dq = dk = dv = None
        for n in range(2):
            mine = lower if n == 0 else ~lower
            qn = jnp.where(mine, q, jnp.zeros_like(q))
            gn = jnp.where(mine, scaled, 0.0).astype(BF)
            delta = jnp.sum(jnp.where(mine, product, 0.0), axis=1, keepdims=True)
            p = p_ref[2 * (first + pair) + n]
            ds = (p.astype(F32) * (mm_t(gn, values) - delta)).astype(BF)
            dqn, dkn, dvn = mm(ds, keys), t_mm(qn, ds), t_mm(gn, p)
            if n == 0:
                dq, dk, dv = dqn, dkn, dvn
            else:
                dq, dk, dv = jnp.where(lower, dq, dqn), dk + dkn, dv + dvn
        dq_ref[:, out] = (dq * scale).astype(BF)
        for i, grad in enumerate((dk.T, dv.T)):
            own_ref[i, :, out] = grad[:tokens]
            oth_ref[i, :, out] = grad[tokens:].astype(BF)


def back_qkv(layer, parts, a_ref, h_ref, g1_ref, w_ref, mg_ref, g_ref):
    a = a_ref[...]
    width = a.shape[1]
    blocks = [jnp.concatenate([dq[...] for dq, _, _ in parts], axis=1)]
    for i in range(2):
        blocks.append(jnp.concatenate([(own[i] + got[i].astype(F32)).astype(BF) for _, own, got in parts], axis=1))
    grad = None
    for j, block in enumerate(blocks):
        put_rows(g_ref, j * width // g_ref.shape[0], t_mm(a, block).astype(BF))
        term = mm_t(block, w_ref[:, j * width : (j + 1) * width])
        grad = term if grad is None else grad + term
    zhat, inverse = norm_parts(h_ref[...])
    gain_grad = jnp.sum(grad * zhat, axis=0, keepdims=True)
    return mg_ref[...] + norm_back(grad, zhat, inverse, g1_ref[layer : layer + 1]), gain_grad


def back_turn_body(layer, bits, core_ref, *refs):
    parts, refs = (refs[:3], refs[3:6]), refs[6:]
    (a_ref, h_ref, g1_ref, w_ref, mg_ref, act_ref, gp_ref, wproj_ref,
     keep_ref, send_ref, up_ref, gain_ref, lift_ref, g_ref) = refs
    up, gain_grad = back_qkv(layer, parts, a_ref, h_ref, g1_ref, w_ref, mg_ref, g_ref)
    gain_ref[...] = jnp.broadcast_to(gain_grad, gain_ref.shape)
    up_ref[...] = up
    back_proj(up, act_ref, gp_ref, wproj_ref, g_ref, 3 * up.shape[1] // g_ref.shape[0], lift_ref)
    hand_out(bits, core_ref, g_ref, keep_ref, send_ref)


def back_end_body(layer, bits, core_ref, *refs):
    parts, refs = (refs[:3], refs[3:6]), refs[6:]
    (a_ref, h_ref, g1_ref, w_ref, mg_ref, oa_ref, ob_ref, *gain_refs, keep_ref, send_ref, to_a_ref, to_b_ref, g_ref) = refs
    up, gain_grad = back_qkv(layer, parts, a_ref, h_ref, g1_ref, w_ref, mg_ref, g_ref)
    span = oa_ref.shape[0]
    width = up.shape[1]
    to_a_ref[0] = oa_ref[...]
    to_b_ref[0] = ob_ref[...]
    to_a_ref[1] = up[:span].astype(BF)
    to_b_ref[1] = up[span:].astype(BF)
    at = 3 * width // g_ref.shape[0]
    for i, gain in enumerate([gain_grad] + [ref[0:1] for ref in gain_refs]):
        put_rows(g_ref, at + i, jnp.broadcast_to(gain, (g_ref.shape[0], width)).astype(BF))
    at += 1 + len(gain_refs)
    for block in range(g_ref.shape[0]):
        g_ref[block, at:] = jnp.zeros((g_ref.shape[1] - at, width), BF)
    hand_out(bits, core_ref, g_ref, keep_ref, send_ref)


def masks_body(per_span, block, ids_ref, order_ref, own_ref, other_ref, w_in, g_in, bias_ref, hot_ref, info_ref, w_ref, g_ref, sem):
    copies = [pltpu.make_async_copy(w_in.at[0], w_ref, sem.at[0]), pltpu.make_async_copy(g_in, g_ref, sem.at[1])]
    for copy in copies:
        copy.start()
    core, place = ids_ref[0] & 1, ids_ref[1]
    odd = place & 1
    prefix = jnp.where((place >> 1) == core, own_ref[odd], other_ref[odd])
    info_ref[0] = prefix
    ranks = []
    for c in (core, 1 - core):
        for span in (2 * c + odd, 2 * c + 1 - odd):
            ranks += [order_ref[span * per_span + i] for i in range(per_span)]
    tokens = hot_ref.shape[0]
    own = tokens // block
    lane = lax.broadcasted_iota(jnp.int32, (block, LANES), 1)
    within = lax.broadcasted_iota(jnp.int32, (block, LANES), 0)
    lane_rank = jnp.full((block, LANES), -1, jnp.int32)
    for b in range(own):
        info_ref[1 + b] = ranks[b]
        lane_rank = jnp.where(lane == b, ranks[b], lane_rank)
        hot_ref[b * block : (b + 1) * block] = jnp.where(lane == b, 1.0, 0.0).astype(BF)
    for k, rank in enumerate(ranks):
        unseen = (lane < own) & (rank >= lane_rank) & (lane != k) & (rank * block + within >= prefix)
        bias_ref[k * block : (k + 1) * block] = jnp.where(unseen, NEGATIVE, 0.0).astype(BF)
    for copy in copies:
        copy.wait()


def pick_body(at_ref, x_ref, a_ref, b_ref):
    odd = at_ref[1] & 1
    a_ref[...] = x_ref[odd]
    b_ref[...] = x_ref[1 - odd]


def place_body(odd_ref, a_ref, b_ref, *out_refs):
    odd = odd_ref[1] & 1
    for i, ref in enumerate(out_refs):
        ref[odd] = a_ref[i]
        ref[1 - odd] = b_ref[i]


def add(a, b):
    return (a.astype(F32) + b.astype(F32)).astype(BF)


def unpack_body(plan, gains, bits, groups, befores, at_ref, *refs):
    halves, refs = refs[: 2 * groups], refs[2 * groups + befores :]
    out_refs, refs = refs[: len(plan)], refs[len(plan) :]
    gain_refs, refs = refs[: len(gains)], refs[len(gains) :]
    *stage_refs, sem = refs
    index = at_ref[0]
    core = index & 1
    copies = []
    for group in range(groups):
        a_ref, b_ref = halves[2 * group : 2 * group + 2]
        count, _, width = a_ref.shape
        mine = [(at, layer, out, stage) for (g, at, layer), out, stage in zip(plan, out_refs, stage_refs) if g == group]
        for ref, side in ((a_ref, core), (b_ref, 1 - core)):
            place = relative(bits, index, side)
            for i in range(count):
                block = side * count + (place ^ i)
                for at, layer, out_ref, stage_ref in mine:
                    _, rows, cols = stage_ref.shape
                    for j in range(cols // width):
                        stage_ref[block, :, j * width : (j + 1) * width] = ref[i, at + j * rows : at + (j + 1) * rows].astype(F32)
                    copies.append(pltpu.make_async_copy(stage_ref.at[block], out_ref.at[layer, block], sem.at[len(copies)]))
                    copies[-1].start()
    for rows, ref in zip(gains, gain_refs):
        ref[...] = jnp.concatenate([halves[-2][0, row : row + 1] for row in rows], axis=0).astype(F32)
    for copy in copies:
        copy.wait()


def unpack(bits, at, groups, layers, gains, order):
    ins = [(at, scalars())] + [(x, whole(*x.shape)) for halves, _ in groups for x in halves]
    aliases = {}
    outs, plan = [], []
    count, _, width = groups[0][0][0].shape
    blocks = 2 * count
    scratch = []
    for group, (_, parts) in enumerate(groups):
        for row, layer, shape, before in parts:
            if before is not None:
                aliases[len(ins)] = len(outs)
                ins.append((before, pl.BlockSpec(memory_space=pltpu.HBM)))
            outs.append(((layers, blocks, shape[0] // blocks, shape[1]), F32, pl.BlockSpec(memory_space=pltpu.HBM), True))
            plan.append((group, row, layer))
            scratch.append(VMEM((blocks, shape[0] // blocks, shape[1]), F32))
    outs += [((len(rows), width), F32, whole(len(rows), width)) for rows in gains]
    return call(
        functools.partial(unpack_body, plan, gains, bits, len(groups), len(aliases)), "unpack", ins, outs,
        scratch=[*scratch, pltpu.SemaphoreType.DMA((blocks * len(plan),))], limit=24, aliases=aliases, order=order,
    )


def per_device(mesh_shape, hidden_in, norm1_gain, qkv_weight, out_weight, norm2_gain, fc_weight, proj_weight,
               prefix_len, block_order, grad_out):
    dp, seq = mesh_shape
    rows_here, span, width = hidden_in.shape
    layers = qkv_weight.shape[0]
    inner = fc_weight.shape[2]
    scale = 1.0 / math.sqrt(width // HEADS)
    row_length = span * seq
    block_count = block_order.shape[0]
    block = row_length // block_count
    per_span = span // block
    tokens = 2 * span
    pairs = width // LANES
    assert rows_here == 2 and seq == 4 and dp % 2 == 0 and layers == 2
    di, si = lax.axis_index("dp"), lax.axis_index("seq")
    at = jnp.stack([di, si]).astype(jnp.int32)
    order = Order()

    def spot(d, s):
        return d * seq + s

    perm_a = [(spot(d, s), spot((d & ~1) | (s >> 1), 2 * (d & 1) + (s & 1))) for d in range(dp) for s in range(seq)]
    perm_b = [(spot(d, s), spot((d & ~1) | (s >> 1), 2 * (d & 1) + 1 - (s & 1))) for d in range(dp) for s in range(seq)]
    back_a = [(b, a) for a, b in perm_a]
    back_b = [(b, a) for a, b in perm_b]
    pair_perm = [(spot(d, s), spot(d ^ 1, s)) for d in range(dp) for s in range(seq)]
    t_w = (tokens, width)
    full = whole(*t_w)
    half_spec = whole(span, width)
    both_spec = whole(2, span, width)

    def pair(x):
        return lax.ppermute(x, ALL, pair_perm)

    def pick(x):
        return call(
            pick_body, "pick", [(at, scalars()), (x, both_spec)], [((span, width), BF, half_spec)] * 2, limit=4, order=order
        )

    def spread(first, other):
        return lax.ppermute(first, ALL, perm_a), lax.ppermute(other, ALL, perm_b)

    class Collect:
        def __init__(self, a, b):
            self.a, self.b = lax.ppermute(a, ALL, back_a), lax.ppermute(b, ALL, back_b)

        def done(self, order):
            return call(
                place_body, "place", [(at, scalars()), (self.a, both_spec), (self.b, both_spec)],
                [((2, span, width), BF, both_spec, True)] * 2, limit=8, order=order,
            )

    dp_bits = [i for i in range(1, dp.bit_length() - 1)]
    seq_bits = [i for i in range(seq.bit_length() - 1)]
    orders = (dp_bits, dp_bits[::-1])
    z_orders = (seq_bits, seq_bits[::-1])
    bits = list(zip(*orders))
    blocks = 2 ** (len(dp_bits) + 1)

    own_blocks = tokens // block
    ha, hb = spread(*pick(hidden_in))
    grad_pieces = pick(grad_out)
    prefix_other = pair(prefix_len)
    bias, hot, info, first_weight, first_gain = call(
        functools.partial(masks_body, per_span, block), "masks",
        [(at, scalars()), (block_order, scalars()), (prefix_len, scalars()), (prefix_other, scalars()),
         in_hbm(qkv_weight), in_hbm(norm1_gain)],
        [((2 * tokens, LANES), BF, whole(2 * tokens, LANES)), ((tokens, LANES), BF, whole(tokens, LANES)),
         ((1 + own_blocks,), jnp.int32, scalars()),
         ((width, 3 * width), BF, whole(width, 3 * width)), ((layers, width), F32, whole(layers, width))],
        scratch=[pltpu.SemaphoreType.DMA((2,))], order=order,
    )

    wide = whole(tokens, inner)
    gains = whole(layers, width)
    dense = 2 * tokens * width

    def qkv_out():
        return [(t_w, BF, full), (t_w, BF, full), ((tokens, 2 * width), BF, whole(tokens, 2 * width))]

    h, a, q, kv = call(
        functools.partial(first_body, scale), "first",
        [(ha, half_spec), (hb, half_spec), (first_gain, gains), (first_weight, whole(width, 3 * width))],
        [(t_w, F32, full)] + qkv_out(),
        flops=dense * 3 * width, order=order,
    )
    kv_spec = whole(tokens, 2 * width)
    p_spec = whole(HEADS, tokens, 2 * tokens)

    def attend(q, kv, kv_other):
        return call(
            functools.partial(attend_body, block), "attend",
            [(info, scalars()), (q, full), (kv, kv_spec), (kv_other, kv_spec), (bias, whole(2 * tokens, LANES)), (hot, whole(tokens, LANES))],
            [((HEADS, tokens, 2 * tokens), BF, p_spec), (t_w, BF, full), (t_w, F32, full)],
            flops=4 * tokens * 2 * tokens * 256 * HEADS, transcendentals=HEADS * tokens * 2 * tokens, limit=20, order=order,
        )

    def feed_ins(layer, h, att):
        return [
            (h, full), (att, full), (out_weight, layer_of(layer, width, width)), (norm2_gain, gains),
            (fc_weight, layer_of(layer, width, inner)), (proj_weight, layer_of(layer, inner, width)),
        ]

    def swap_dp(x, step):
        return lax.ppermute(x, ALL, [(spot(d, s), spot(d ^ (1 << orders[d & 1][step]), s)) for d in range(dp) for s in range(seq)])

    def swap_seq(x, step):
        return lax.ppermute(x, ALL, [(spot(d, s), spot(d, s ^ (1 << z_orders[d & 1][step]))) for d in range(dp) for s in range(seq)])

    class Bucket:
        def __init__(self, keep, send):
            self.halves = None
            self.parts = None
            self.steps = self.run(keep, send)
            next(self.steps)

        def run(self, keep, send):
            got = pair(send)
            for step in range(len(dp_bits)):
                yield
                total = add(keep, order.after(got))
                half = total.shape[0] // 2
                keep, send = total[:half], total[half:]
                order.add(keep)
                got = swap_dp(send, step)
            self.parts = [(keep, got)]
            yield
            yield from self.rest()

        def rest(self):
            total = jnp.concatenate([add(keep, order.after(got)) for keep, got in self.parts], axis=1)
            order.add(total)
            for step in range(len(seq_bits)):
                got = swap_seq(total, step)
                yield
                total = add(total, order.after(got))
                order.add(total)
            for step in reversed(range(len(dp_bits))):
                got = swap_dp(total, step)
                yield
                total = jnp.concatenate([total, order.after(got)], axis=0)
                order.add(total)
            self.halves = (total, pair(total))
            yield

        def step(self):
            next(self.steps)

    def bucket_outs(rows):
        count = 2 ** len(dp_bits)
        size = rows // (2 * count)
        assert size * 2 * count == rows
        return [((count, size, width), BF, whole(count, size, width))] * 2, [VMEM((2 * count, size, width), BF)]

    gain_out = ((8, width), F32, whole(8, width))

    kv_other = pair(kv)
    ua, ub = spread(*[order.after(x) for x in grad_pieces])
    p, att, inv = attend(q, kv, kv_other)
    order.last += [ua, ub]
    mid, sec, act, gp, h_next, a_next, q_next, kv_next = call(
        functools.partial(middle_body, scale, 0), "middle",
        feed_ins(0, h, att) + [(norm1_gain, gains), (qkv_weight, layer_of(1, width, 3 * width))],
        [(t_w, F32, full), (t_w, BF, full), ((tokens, inner), BF, wide), ((tokens, inner), BF, wide), (t_w, F32, full)] + qkv_out(),
        flops=dense * (4 * width + 2 * inner), transcendentals=2 * tokens * inner, limit=18, order=order,
    )
    saved = (h, a, q, kv, kv_other, p, att, inv)
    h, a, q, kv = h_next, a_next, q_next, kv_next

    kv_other = pair(kv)
    p, att, inv = attend(q, kv, kv_other)
    outs, scratch = bucket_outs(2 * inner + width)
    oa, ob, keep, send, mg, ag, gain2_1 = call(
        functools.partial(turn_body, 1, bits), "turn",
        [(at, scalars())] + feed_ins(1, h, att) + [(ua, half_spec), (ub, half_spec)],
        [((span, width), BF, half_spec)] * 2 + outs + [(t_w, F32, full), (t_w, BF, full), gain_out],
        scratch=[VMEM(t_w, F32), VMEM(t_w, BF)] + [VMEM((tokens, inner), BF)] * 3 + scratch,
        flops=dense * (3 * width + 6 * inner), transcendentals=2 * tokens * inner, limit=24, order=order,
    )
    feed_1 = Bucket(keep, send)

    def back_attend(first, count, q, kv, kv_other, p, att, inv, ag):
        out = (tokens, count * LANES)
        dq, own, oth = call(
            functools.partial(back_attend_body, scale, first), "back_attend",
            [(q, full), (kv, kv_spec), (kv_other, kv_spec), (p, p_spec), (att, full), (inv, full), (ag, full)],
            [(out, BF, whole(*out)), ((2, *out), F32, whole(2, *out)), ((2, *out), BF, whole(2, *out))],
            flops=8 * tokens * 2 * tokens * 256 * 2 * count, limit=20, order=order,
        )
        return dq, own, pair(oth)

    def part_ins(parts):
        return [(x, whole(*x.shape)) for part in parts for x in part]

    layer_1 = (q, kv, kv_other, p, att, inv)
    h_1, a_1, mg_1, ag_1 = h, a, mg, ag
    h_0, a_0, *layer_0 = saved
    v = {}
    buckets = {"A": feed_1}

    def back_turn():
        outs, scratch = bucket_outs(3 * width + inner)
        keep, send, v["up"], v["gain1_1"], v["lift"] = call(
            functools.partial(back_turn_body, 1, bits), "back_turn",
            [(at, scalars())] + part_ins((v["1a"], v["1b"])) + [
                (a_1, full), (h_1, full), (norm1_gain, gains), (qkv_weight, layer_of(1, width, 3 * width)), (mg_1, full),
                (act, wide), (gp, wide), (proj_weight, layer_of(0, inner, width))],
            outs + [(t_w, F32, full), gain_out, ((tokens, inner), BF, wide)],
            scratch=scratch, flops=dense * (6 * width + 2 * inner), limit=18, order=order,
        )
        buckets["B"] = Bucket(keep, send)

    def back_fc_0():
        outs, scratch = bucket_outs(inner + width)
        keep, send, v["mg"], v["ag"], v["gain2_0"] = call(
            functools.partial(back_fc_body, 0, bits), "back_fc",
            [(at, scalars()), (v["up"], full), (v["lift"], wide), (sec, full), (mid, full), (layer_0[4], full),
             (fc_weight, layer_of(0, width, inner)), (out_weight, layer_of(0, width, width)), (norm2_gain, gains)],
            outs + [(t_w, F32, full), (t_w, BF, full), gain_out],
            scratch=scratch, flops=dense * (2 * width + 2 * inner), limit=16, order=order,
        )
        buckets["C"] = Bucket(keep, send)

    def back_end():
        outs, scratch = bucket_outs(3 * width + GAIN_ROWS * blocks)
        keep, send, ga, gb = call(
            functools.partial(back_end_body, 0, bits), "back_end",
            [(at, scalars())] + part_ins((v["0a"], v["0b"])) + [
                (a_0, full), (h_0, full), (norm1_gain, gains), (qkv_weight, layer_of(0, width, 3 * width)), (v["mg"], full),
                (oa, half_spec), (ob, half_spec)]
            + [(g, whole(8, width)) for g in (v["gain1_1"], v["gain2_0"], gain2_1)],
            outs + [((2, span, width), BF, both_spec)] * 2,
            scratch=scratch, flops=2 * dense * 3 * width, limit=12, order=order,
        )
        buckets["D"] = Bucket(keep, send)
        v["ga"], v["gb"] = ga, gb

    def run_part(name, first, count, layer, ag):
        v[name] = back_attend(first, count, *layer, ag)

    parts_of = {
        "A": [(0, 1, (inner, width), "proj"), (inner, 1, (width, inner), "fc"), (2 * inner, 1, (width, width), "out")],
        "B": [(0, 1, (width, 3 * width), "qkv"), (3 * width, 0, (inner, width), "proj")],
        "C": [(0, 0, (width, inner), "fc"), (inner, 0, (width, width), "out")],
        "D": [(0, 0, (width, 3 * width), "qkv")],
    }

    def unpacked(names):
        last = "D" in names
        groups = [
            (buckets.pop(name).halves, [(row // blocks, layer, shape, v.get(key)) for row, layer, shape, key in parts_of[name]])
            for name in names
        ]
        gain_rows = [[3 * width // blocks + i for i in pair] for pair in ((0, 1), (2, 3))] if last else []
        got = unpack(bits, at, groups, layers, gain_rows, order)
        keys = [part[3] for name in names for part in parts_of[name]]
        v.update(zip(keys, got))
        if last:
            v["gains"] = got[len(keys) : len(keys) + 2]

    def bucket_step(name):
        if name not in buckets:
            return
        if buckets[name].halves is None:
            buckets[name].step()
        elif name == "D":
            while "C" in buckets and buckets["C"].halves is None:
                buckets["C"].step()
            unpacked([n for n in "CD" if n in buckets])
        elif name != "C":
            unpacked([name])

    kernels = {
        "BA1a": lambda: run_part("1a", 0, 1, layer_1, ag_1),
        "BA1b": lambda: run_part("1b", 1, pairs - 1, layer_1, ag_1),
        "BT": back_turn,
        "BF": back_fc_0,
        "BA0a": lambda: run_part("0a", 0, 1, layer_0, v["ag"]),
        "BA0b": lambda: run_part("0b", 1, pairs - 1, layer_0, v["ag"]),
        "BE": back_end,
        "PG": lambda: v.update(home=v["home"].done(order)),
        "SG": lambda: v.update(home=Collect(order.after(v["ga"]), order.after(v["gb"]))),
    }
    for token in SCHEDULE.split():
        if token in kernels:
            kernels[token]()
        else:
            bucket_step(token)
    while buckets:
        for name in "ABCD":
            bucket_step(name)
    norm1_grad, norm2_grad = v["gains"]
    qkv_grad, out_grad, fc_grad, proj_grad = (
        v[name].reshape(layers, -1, v[name].shape[-1]) for name in ("qkv", "out", "fc", "proj")
    )
    return *v["home"], norm1_grad, qkv_grad, out_grad, norm2_grad, fc_grad, proj_grad


def solution(mesh):
    block = P("dp", "seq", None)
    return jax.shard_map(
        functools.partial(per_device, (mesh.shape["dp"], mesh.shape["seq"])),
        mesh=mesh,
        in_specs=(block, P(), P(), P(), P(), P(), P(), P("dp"), P(), block),
        out_specs=(block, block, P(), P(), P(), P(), P(), P()),
        check_vma=False,
    )
```

```python
import functools
import math

import jax
import jax.numpy as jnp
from jax import lax
from jax.experimental import pallas as pl
from jax.experimental.pallas import tpu as pltpu
from jax.sharding import PartitionSpec as P

HEADS = 6
EPSILON = 1e-05
NEGATIVE = -1e30
BF = jnp.bfloat16
F32 = jnp.float32
ALL = ("dp", "seq")
LANES = 128
GAIN_ROWS = 16
SCHEDULE = (
    "BA1a", "A", "BA1b", "BT", "A", "BF", "B", "A", "BA0a", "BA0b", "C", "A", "B", "BE", "C", "B", "D", "A", "C",
    "B", "D", "A", "C", "D", "B", "C", "D", "SG", "B", "C", "D", "A", "B", "C", "D", "A", "PG", "D", "B", "D",
)
MB = 1024 * 1024
VMEM = pltpu.VMEM
SMEM = pltpu.SMEM


def mm(a, b):
    return lax.dot_general(a, b, (((1,), (0,)), ((), ())), preferred_element_type=F32)


def mm_t(a, b):
    return lax.dot_general(a, b, (((1,), (1,)), ((), ())), preferred_element_type=F32)


def t_mm(a, b):
    return lax.dot_general(a, b, (((0,), (0,)), ((), ())), preferred_element_type=F32)


class Order:
    def __init__(self):
        self.last = []

    def after(self, x):
        x, *last = lax.optimization_barrier((x, *self.last))
        self.last = last[-1:]
        return x

    def add(self, result):
        self.last = [result, *self.last]


def call(body, name, ins, outs, scratch=(), limit=16, flops=0, transcendentals=0, grid=(1,), aliases=None, order=None):
    moved = sum(math.prod(o[0]) * jnp.dtype(o[1]).itemsize for o in outs)
    moved += sum(a.size * a.dtype.itemsize for a, _ in ins)
    kernel = body
    if order is not None:
        count, more = len(ins), len(order.last)
        ins = [*ins, *((x, pl.BlockSpec(memory_space=pl.ANY)) for x in order.last)]
        order.last = []
        results_at = count + more + len(outs)
        outs = [*outs, ((8, LANES), F32, whole(8, LANES))]

        def kernel(*refs):
            body(*refs[:count], *refs[count + more : results_at], *refs[results_at + 1 :])
            refs[results_at][...] = jnp.zeros((8, LANES), F32)

    results = pl.pallas_call(
        kernel,
        out_shape=[pltpu.HBM(o[0], o[1]) if len(o) > 3 else jax.ShapeDtypeStruct(o[0], o[1]) for o in outs],
        grid=grid,
        in_specs=[s for _, s in ins],
        out_specs=[o[2] for o in outs],
        scratch_shapes=list(scratch),
        input_output_aliases=aliases or {},
        compiler_params=pltpu.CompilerParams(vmem_limit_bytes=limit * MB),
        cost_estimate=pl.CostEstimate(flops=flops, bytes_accessed=moved, transcendentals=transcendentals),
        name=name,
    )(*[a for a, _ in ins])
    if order is not None:
        *results, token = results
        order.add(token)
    return results


def whole(*shape):
    return pl.BlockSpec(shape, lambda *_: (0,) * len(shape))


def layer_of(index, *shape):
    return pl.BlockSpec((None,) + shape, lambda *_: (index,) + (0,) * len(shape))


def in_hbm(x):
    return pltpu.with_memory_space_constraint(x, pltpu.HBM), pl.BlockSpec(memory_space=pltpu.HBM)


def scalars():
    return pl.BlockSpec(memory_space=SMEM)


def norm_parts(values):
    centre = jnp.mean(values, axis=-1, keepdims=True)
    centred = values - centre
    spread = jnp.mean(centred * centred, axis=-1, keepdims=True)
    inverse = lax.rsqrt(spread + EPSILON)
    return centred * inverse, inverse


def norm_back(grad, zhat, inverse, gain):
    e = grad * gain
    return inverse * (
        e
        - jnp.mean(e, axis=-1, keepdims=True)
        - zhat * jnp.mean(e * zhat, axis=-1, keepdims=True)
    )


def qkv_step(hidden, gain, weight, a_ref, q_ref, kv_ref, scale):
    zhat, _ = norm_parts(hidden)
    a = (zhat * gain).astype(BF)
    a_ref[...] = a
    packed = mm(a, weight).astype(BF)
    width = a.shape[1]
    q_ref[...] = packed[:, :width] * jnp.asarray(scale, BF)
    kv_ref[...] = packed[:, width:]


def first_body(scale, ha_ref, hb_ref, gain_ref, w_ref, h_ref, a_ref, q_ref, kv_ref):
    span = ha_ref.shape[0]
    h_ref[:span] = ha_ref[...].astype(F32)
    h_ref[span:] = hb_ref[...].astype(F32)
    qkv_step(h_ref[...], gain_ref[0:1], w_ref[...], a_ref, q_ref, kv_ref, scale)


def attend_body(block, info_ref, q_ref, kv_ref, kx_ref, bias_ref, hot_ref, p_ref, att_ref, inv_ref):
    tokens, width = q_ref.shape
    head = LANES // 2
    ones = jnp.ones((tokens, LANES), BF)

    def beside(a, b):
        return jnp.concatenate([a, b], axis=1)

    lower = lax.broadcasted_iota(jnp.int32, (tokens, LANES), 1) < head
    at_q = lax.broadcasted_iota(jnp.int32, (block, block), 0)
    at_k = lax.broadcasted_iota(jnp.int32, (block, block), 1)
    prefix = info_ref[0]

    @pl.loop(0, width // LANES)
    def _(pair):
        cols = pl.ds(pl.multiple_of(pair * LANES, LANES), LANES)
        vcols = pl.ds(pl.multiple_of(width + pair * LANES, LANES), LANES)
        keys = jnp.concatenate([beside(kv_ref[:, cols], bias_ref[:tokens]), beside(kx_ref[:, cols], bias_ref[tokens:])], axis=0)
        values = jnp.concatenate([beside(kv_ref[:, vcols], ones), beside(kx_ref[:, vcols], ones)], axis=0)
        q = q_ref[:, cols]
        scores = []
        for n in range(2):
            qn = jnp.where(lower if n == 0 else ~lower, q, jnp.zeros_like(q))
            scores.append(mm_t(beside(qn, hot_ref[...]), keys))
        chances = []
        for n in range(2):
            rows = []
            for t in range(tokens // block):
                s = scores[n][t * block : (t + 1) * block]
                seen = (at_k <= at_q) | (info_ref[1 + t] * block + at_k < prefix)
                pieces = [s[:, : t * block], jnp.where(seen, s[:, t * block : (t + 1) * block], NEGATIVE), s[:, (t + 1) * block :]]
                s = jnp.concatenate([piece for piece in pieces if piece.shape[1]], axis=1)
                rows.append(jnp.exp(s - jnp.max(s, axis=1, keepdims=True)).astype(BF))
            p = jnp.concatenate(rows, axis=0)
            p_ref[2 * pair + n] = p
            chances.append(p)
        even, odd = [mm(p, values) for p in chances]
        inverse = 1.0 / jnp.where(lower, even[:, LANES:], odd[:, LANES:])
        inv_ref[:, cols] = inverse
        att_ref[:, cols] = (jnp.where(lower, even[:, :LANES], odd[:, :LANES]) * inverse).astype(BF)


def feed(h_ref, att_ref, wout_ref, gain, wfc_ref, wproj_ref, mid_ref, sec_ref, act_ref, gp_ref):
    middle = h_ref[...] + mm(att_ref[...], wout_ref[...])
    mid_ref[...] = middle
    zhat, _ = norm_parts(middle)
    second = (zhat * gain).astype(BF)
    sec_ref[...] = second
    total = middle
    width = middle.shape[1]
    for j in range(wfc_ref.shape[1] // width):
        cols = slice(j * width, (j + 1) * width)
        lifted = mm(second, wfc_ref[:, cols])
        phi = 0.5 * (1.0 + lax.erf(lifted * (1.0 / math.sqrt(2.0))))
        slope = phi + lifted * jnp.exp(-0.5 * lifted * lifted) * (1.0 / math.sqrt(2.0 * math.pi))
        gp_ref[:, cols] = slope.astype(BF)
        act = (lifted * phi).astype(BF)
        act_ref[:, cols] = act
        total = total + mm(act, wproj_ref[cols, :])
    return total


def middle_body(scale, layer, h_ref, att_ref, wout_ref, g2_ref, wfc_ref, wproj_ref, g1_ref, wqkv_ref,
                mid_ref, sec_ref, act_ref, gp_ref, out_ref, a_ref, q_ref, kv_ref):
    out = feed(h_ref, att_ref, wout_ref, g2_ref[layer : layer + 1], wfc_ref, wproj_ref, mid_ref, sec_ref, act_ref, gp_ref)
    out_ref[...] = out
    qkv_step(out, g1_ref[layer + 1 : layer + 2], wqkv_ref[...], a_ref, q_ref, kv_ref, scale)


def relative(bits, index, core):
    place = 0
    for mine, others in bits:
        place = 2 * place + (jnp.where(core == 0, index >> mine, index >> others) & 1)
    return place


def hand_out(bits, at_ref, g_ref, keep_ref, send_ref):
    index = at_ref[0]
    core = index & 1
    count = keep_ref.shape[0]
    for ref, side in ((keep_ref, core), (send_ref, 1 - core)):
        place = relative(bits, index, side)
        for i in range(count):
            ref[i] = g_ref[side * count + (place ^ i)]


def put_rows(g_ref, at, values, first=0, total=None):
    share = (total or values.shape[0]) // g_ref.shape[0]
    done = 0
    while done < values.shape[0]:
        block, row = divmod(first + done, share)
        count = min(share - row, values.shape[0] - done)
        g_ref[block, at + row : at + row + count] = values[done : done + count]
        done += count


def back_proj(upstream, act_ref, gp_ref, wproj_ref, g_ref, at, lift_ref):
    down = upstream.astype(BF)
    width = down.shape[1]
    for j in range(act_ref.shape[1] // width):
        cols = slice(j * width, (j + 1) * width)
        put_rows(g_ref, at, t_mm(act_ref[:, cols], down).astype(BF), j * width, act_ref.shape[1])
        lift_ref[:, cols] = (mm_t(down, wproj_ref[cols, :]) * gp_ref[:, cols].astype(F32)).astype(BF)


def back_fc(upstream, lift_ref, sec_ref, mid_ref, att_ref, wfc_ref, wout_ref, gain, g_ref, at, mg_ref, ag_ref, gain_ref):
    second = sec_ref[...]
    width = second.shape[1]
    inner = lift_ref.shape[1]
    second_grad = None
    for j in range(inner // width):
        cols = slice(j * width, (j + 1) * width)
        lift = lift_ref[:, cols]
        put_rows(g_ref, at + j * width // g_ref.shape[0], t_mm(second, lift).astype(BF))
        term = mm_t(lift, wfc_ref[:, cols])
        second_grad = term if second_grad is None else second_grad + term
    zhat, inverse = norm_parts(mid_ref[...])
    gain_ref[...] = jnp.broadcast_to(jnp.sum(second_grad * zhat, axis=0, keepdims=True), gain_ref.shape)
    mg = upstream + norm_back(second_grad, zhat, inverse, gain)
    mg_ref[...] = mg
    branch = mg.astype(BF)
    put_rows(g_ref, at + inner // g_ref.shape[0], t_mm(att_ref[...], branch).astype(BF))
    ag_ref[...] = mm_t(branch, wout_ref[...]).astype(BF)


def turn_body(layer, bits, core_ref, h_ref, att_ref, wout_ref, g2_ref, wfc_ref, wproj_ref, ua_ref, ub_ref,
              oa_ref, ob_ref, keep_ref, send_ref, mg_ref, ag_ref, gain_ref,
              mid_ref, sec_ref, act_ref, gp_ref, lift_ref, g_ref):
    gain = g2_ref[layer : layer + 1]
    out = feed(h_ref, att_ref, wout_ref, gain, wfc_ref, wproj_ref, mid_ref, sec_ref, act_ref, gp_ref)
    span = oa_ref.shape[0]
    oa_ref[...] = out[:span].astype(BF)
    ob_ref[...] = out[span:].astype(BF)
    upstream = jnp.concatenate([ua_ref[...], ub_ref[...]], axis=0).astype(F32)
    back_proj(upstream, act_ref, gp_ref, wproj_ref, g_ref, 0, lift_ref)
    back_fc(upstream, lift_ref, sec_ref, mid_ref, att_ref, wfc_ref, wout_ref, gain, g_ref, act_ref.shape[1] // g_ref.shape[0],
            mg_ref, ag_ref, gain_ref)
    hand_out(bits, core_ref, g_ref, keep_ref, send_ref)


def back_fc_body(layer, bits, core_ref, u_ref, lift_ref, sec_ref, mid_ref, att_ref, wfc_ref, wout_ref, g2_ref,
                 keep_ref, send_ref, mg_ref, ag_ref, gain_ref, g_ref):
    back_fc(u_ref[...], lift_ref, sec_ref, mid_ref, att_ref, wfc_ref, wout_ref, g2_ref[layer : layer + 1], g_ref, 0,
            mg_ref, ag_ref, gain_ref)
    hand_out(bits, core_ref, g_ref, keep_ref, send_ref)


def back_attend_body(scale, first, q_ref, kv_ref, kx_ref, p_ref, att_ref, inv_ref, ag_ref, dq_ref, own_ref, oth_ref):
    tokens, width = q_ref.shape
    head = LANES // 2
    lower = lax.broadcasted_iota(jnp.int32, (tokens, LANES), 1) < head

    @pl.loop(0, dq_ref.shape[1] // LANES)
    def _(pair):
        out = pl.ds(pl.multiple_of(pair * LANES, LANES), LANES)
        cols = pl.ds(pl.multiple_of((first + pair) * LANES, LANES), LANES)
        vcols = pl.ds(pl.multiple_of(width + (first + pair) * LANES, LANES), LANES)
        q = q_ref[:, cols]
        scaled = ag_ref[:, cols].astype(F32) * inv_ref[:, cols]
        product = scaled * att_ref[:, cols].astype(F32)
        keys = jnp.concatenate([kv_ref[:, cols], kx_ref[:, cols]], axis=0)
        values = jnp.concatenate([kv_ref[:, vcols], kx_ref[:, vcols]], axis=0)
        dq = dk = dv = None
        for n in range(2):
            mine = lower if n == 0 else ~lower
            qn = jnp.where(mine, q, jnp.zeros_like(q))
            gn = jnp.where(mine, scaled, 0.0).astype(BF)
            delta = jnp.sum(jnp.where(mine, product, 0.0), axis=1, keepdims=True)
            p = p_ref[2 * (first + pair) + n]
            ds = (p.astype(F32) * (mm_t(gn, values) - delta)).astype(BF)
            dqn, dkn, dvn = mm(ds, keys), t_mm(qn, ds), t_mm(gn, p)
            if n == 0:
                dq, dk, dv = dqn, dkn, dvn
            else:
                dq, dk, dv = jnp.where(lower, dq, dqn), dk + dkn, dv + dvn
        dq_ref[:, out] = (dq * scale).astype(BF)
        for i, grad in enumerate((dk.T, dv.T)):
            own_ref[i, :, out] = grad[:tokens]
            oth_ref[i, :, out] = grad[tokens:].astype(BF)


def back_qkv(layer, parts, a_ref, h_ref, g1_ref, w_ref, mg_ref, g_ref):
    a = a_ref[...]
    width = a.shape[1]
    blocks = [jnp.concatenate([dq[...] for dq, _, _ in parts], axis=1)]
    for i in range(2):
        blocks.append(jnp.concatenate([(own[i] + got[i].astype(F32)).astype(BF) for _, own, got in parts], axis=1))
    grad = None
    for j, block in enumerate(blocks):
        put_rows(g_ref, j * width // g_ref.shape[0], t_mm(a, block).astype(BF))
        term = mm_t(block, w_ref[:, j * width : (j + 1) * width])
        grad = term if grad is None else grad + term
    zhat, inverse = norm_parts(h_ref[...])
    gain_grad = jnp.sum(grad * zhat, axis=0, keepdims=True)
    return mg_ref[...] + norm_back(grad, zhat, inverse, g1_ref[layer : layer + 1]), gain_grad


def back_turn_body(layer, bits, core_ref, *refs):
    parts, refs = (refs[:3], refs[3:6]), refs[6:]
    (a_ref, h_ref, g1_ref, w_ref, mg_ref, act_ref, gp_ref, wproj_ref,
     keep_ref, send_ref, up_ref, gain_ref, lift_ref, g_ref) = refs
    up, gain_grad = back_qkv(layer, parts, a_ref, h_ref, g1_ref, w_ref, mg_ref, g_ref)
    gain_ref[...] = jnp.broadcast_to(gain_grad, gain_ref.shape)
    up_ref[...] = up
    back_proj(up, act_ref, gp_ref, wproj_ref, g_ref, 3 * up.shape[1] // g_ref.shape[0], lift_ref)
    hand_out(bits, core_ref, g_ref, keep_ref, send_ref)


def back_end_body(layer, bits, core_ref, *refs):
    parts, refs = (refs[:3], refs[3:6]), refs[6:]
    (a_ref, h_ref, g1_ref, w_ref, mg_ref, oa_ref, ob_ref, *gain_refs, keep_ref, send_ref, to_a_ref, to_b_ref, g_ref) = refs
    up, gain_grad = back_qkv(layer, parts, a_ref, h_ref, g1_ref, w_ref, mg_ref, g_ref)
    span = oa_ref.shape[0]
    width = up.shape[1]
    to_a_ref[0] = oa_ref[...]
    to_b_ref[0] = ob_ref[...]
    to_a_ref[1] = up[:span].astype(BF)
    to_b_ref[1] = up[span:].astype(BF)
    at = 3 * width // g_ref.shape[0]
    for i, gain in enumerate([gain_grad] + [ref[0:1] for ref in gain_refs]):
        put_rows(g_ref, at + i, jnp.broadcast_to(gain, (g_ref.shape[0], width)).astype(BF))
    at += 1 + len(gain_refs)
    for block in range(g_ref.shape[0]):
        g_ref[block, at:] = jnp.zeros((g_ref.shape[1] - at, width), BF)
    hand_out(bits, core_ref, g_ref, keep_ref, send_ref)


def masks_body(per_span, block, ids_ref, order_ref, own_ref, other_ref, w_in, g_in, bias_ref, hot_ref, info_ref, w_ref, g_ref, sem):
    copies = [pltpu.make_async_copy(w_in.at[0], w_ref, sem.at[0]), pltpu.make_async_copy(g_in, g_ref, sem.at[1])]
    for copy in copies:
        copy.start()
    core, place = ids_ref[0] & 1, ids_ref[1]
    odd = place & 1
    prefix = jnp.where((place >> 1) == core, own_ref[odd], other_ref[odd])
    info_ref[0] = prefix
    ranks = []
    for c in (core, 1 - core):
        for span in (2 * c + odd, 2 * c + 1 - odd):
            ranks += [order_ref[span * per_span + i] for i in range(per_span)]
    tokens = hot_ref.shape[0]
    own = tokens // block
    lane = lax.broadcasted_iota(jnp.int32, (block, LANES), 1)
    within = lax.broadcasted_iota(jnp.int32, (block, LANES), 0)
    lane_rank = jnp.full((block, LANES), -1, jnp.int32)
    for b in range(own):
        info_ref[1 + b] = ranks[b]
        lane_rank = jnp.where(lane == b, ranks[b], lane_rank)
        hot_ref[b * block : (b + 1) * block] = jnp.where(lane == b, 1.0, 0.0).astype(BF)
    for k, rank in enumerate(ranks):
        unseen = (lane < own) & (rank >= lane_rank) & (lane != k) & (rank * block + within >= prefix)
        bias_ref[k * block : (k + 1) * block] = jnp.where(unseen, NEGATIVE, 0.0).astype(BF)
    for copy in copies:
        copy.wait()


def pick_body(at_ref, x_ref, a_ref, b_ref):
    odd = at_ref[1] & 1
    a_ref[...] = x_ref[odd]
    b_ref[...] = x_ref[1 - odd]


def place_body(odd_ref, a_ref, b_ref, *out_refs):
    odd = odd_ref[1] & 1
    for i, ref in enumerate(out_refs):
        ref[odd] = a_ref[i]
        ref[1 - odd] = b_ref[i]


def add(a, b):
    return (a.astype(F32) + b.astype(F32)).astype(BF)


def unpack_body(plan, gains, bits, groups, befores, at_ref, *refs):
    halves, refs = refs[: 2 * groups], refs[2 * groups + befores :]
    out_refs, refs = refs[: len(plan)], refs[len(plan) :]
    gain_refs, refs = refs[: len(gains)], refs[len(gains) :]
    *stage_refs, sem = refs
    index = at_ref[0]
    core = index & 1
    copies = []
    for group in range(groups):
        a_ref, b_ref = halves[2 * group : 2 * group + 2]
        count, _, width = a_ref.shape
        mine = [(at, layer, out, stage) for (g, at, layer), out, stage in zip(plan, out_refs, stage_refs) if g == group]
        for ref, side in ((a_ref, core), (b_ref, 1 - core)):
            place = relative(bits, index, side)
            for i in range(count):
                block = side * count + (place ^ i)
                for at, layer, out_ref, stage_ref in mine:
                    _, rows, cols = stage_ref.shape
                    for j in range(cols // width):
                        stage_ref[block, :, j * width : (j + 1) * width] = ref[i, at + j * rows : at + (j + 1) * rows].astype(F32)
                    copies.append(pltpu.make_async_copy(stage_ref.at[block], out_ref.at[layer, block], sem.at[len(copies)]))
                    copies[-1].start()
    for rows, ref in zip(gains, gain_refs):
        ref[...] = jnp.concatenate([halves[-2][0, row : row + 1] for row in rows], axis=0).astype(F32)
    for copy in copies:
        copy.wait()


def unpack(bits, at, groups, layers, gains, order):
    ins = [(at, scalars())] + [(x, whole(*x.shape)) for halves, _ in groups for x in halves]
    aliases = {}
    outs, plan = [], []
    count, _, width = groups[0][0][0].shape
    blocks = 2 * count
    scratch = []
    for group, (_, parts) in enumerate(groups):
        for row, layer, shape, before in parts:
            if before is not None:
                aliases[len(ins)] = len(outs)
                ins.append((before, pl.BlockSpec(memory_space=pltpu.HBM)))
            outs.append(((layers, blocks, shape[0] // blocks, shape[1]), F32, pl.BlockSpec(memory_space=pltpu.HBM), True))
            plan.append((group, row, layer))
            scratch.append(VMEM((blocks, shape[0] // blocks, shape[1]), F32))
    outs += [((len(rows), width), F32, whole(len(rows), width)) for rows in gains]
    return call(
        functools.partial(unpack_body, plan, gains, bits, len(groups), len(aliases)), "unpack", ins, outs,
        scratch=[*scratch, pltpu.SemaphoreType.DMA((blocks * len(plan),))], limit=24, aliases=aliases, order=order,
    )


def per_device(mesh_shape, hidden_in, norm1_gain, qkv_weight, out_weight, norm2_gain, fc_weight, proj_weight,
               prefix_len, block_order, grad_out):
    dp, seq = mesh_shape
    rows_here, span, width = hidden_in.shape
    layers = qkv_weight.shape[0]
    inner = fc_weight.shape[2]
    scale = 1.0 / math.sqrt(width // HEADS)
    row_length = span * seq
    block_count = block_order.shape[0]
    block = row_length // block_count
    per_span = span // block
    tokens = 2 * span
    pairs = width // LANES
    assert rows_here == 2 and seq == 4 and dp % 2 == 0 and layers == 2
    di, si = lax.axis_index("dp"), lax.axis_index("seq")
    at = jnp.stack([di, si]).astype(jnp.int32)
    order = Order()

    def spot(d, s):
        return d * seq + s

    perm_a = [(spot(d, s), spot((d & ~1) | (s >> 1), 2 * (d & 1) + (s & 1))) for d in range(dp) for s in range(seq)]
    perm_b = [(spot(d, s), spot((d & ~1) | (s >> 1), 2 * (d & 1) + 1 - (s & 1))) for d in range(dp) for s in range(seq)]
    back_a = [(b, a) for a, b in perm_a]
    back_b = [(b, a) for a, b in perm_b]
    pair_perm = [(spot(d, s), spot(d ^ 1, s)) for d in range(dp) for s in range(seq)]
    t_w = (tokens, width)
    full = whole(*t_w)
    half_spec = whole(span, width)
    both_spec = whole(2, span, width)

    def pair(x):
        return lax.ppermute(x, ALL, pair_perm)

    def pick(x):
        return call(
            pick_body, "pick", [(at, scalars()), (x, both_spec)], [((span, width), BF, half_spec)] * 2, limit=4, order=order
        )

    def spread(first, other):
        return lax.ppermute(first, ALL, perm_a), lax.ppermute(other, ALL, perm_b)

    class Collect:
        def __init__(self, a, b):
            self.a, self.b = lax.ppermute(a, ALL, back_a), lax.ppermute(b, ALL, back_b)

        def done(self, order):
            return call(
                place_body, "place", [(at, scalars()), (self.a, both_spec), (self.b, both_spec)],
                [((2, span, width), BF, both_spec, True)] * 2, limit=8, order=order,
            )

    dp_bits = [i for i in range(1, dp.bit_length() - 1)]
    seq_bits = [i for i in range(seq.bit_length() - 1)]
    orders = (dp_bits, dp_bits[::-1])
    z_orders = (seq_bits, seq_bits[::-1])
    bits = list(zip(*orders))
    blocks = 2 ** (len(dp_bits) + 1)

    own_blocks = tokens // block
    ha, hb = spread(*pick(hidden_in))
    grad_pieces = pick(grad_out)
    prefix_other = pair(prefix_len)
    bias, hot, info, first_weight, first_gain = call(
        functools.partial(masks_body, per_span, block), "masks",
        [(at, scalars()), (block_order, scalars()), (prefix_len, scalars()), (prefix_other, scalars()),
         in_hbm(qkv_weight), in_hbm(norm1_gain)],
        [((2 * tokens, LANES), BF, whole(2 * tokens, LANES)), ((tokens, LANES), BF, whole(tokens, LANES)),
         ((1 + own_blocks,), jnp.int32, scalars()),
         ((width, 3 * width), BF, whole(width, 3 * width)), ((layers, width), F32, whole(layers, width))],
        scratch=[pltpu.SemaphoreType.DMA((2,))], order=order,
    )

    wide = whole(tokens, inner)
    gains = whole(layers, width)
    dense = 2 * tokens * width

    def qkv_out():
        return [(t_w, BF, full), (t_w, BF, full), ((tokens, 2 * width), BF, whole(tokens, 2 * width))]

    h, a, q, kv = call(
        functools.partial(first_body, scale), "first",
        [(ha, half_spec), (hb, half_spec), (first_gain, gains), (first_weight, whole(width, 3 * width))],
        [(t_w, F32, full)] + qkv_out(),
        flops=dense * 3 * width, order=order,
    )
    kv_spec = whole(tokens, 2 * width)
    p_spec = whole(HEADS, tokens, 2 * tokens)

    def attend(q, kv, kv_other):
        return call(
            functools.partial(attend_body, block), "attend",
            [(info, scalars()), (q, full), (kv, kv_spec), (kv_other, kv_spec), (bias, whole(2 * tokens, LANES)), (hot, whole(tokens, LANES))],
            [((HEADS, tokens, 2 * tokens), BF, p_spec), (t_w, BF, full), (t_w, F32, full)],
            flops=4 * tokens * 2 * tokens * 256 * HEADS, transcendentals=HEADS * tokens * 2 * tokens, limit=20, order=order,
        )

    def feed_ins(layer, h, att):
        return [
            (h, full), (att, full), (out_weight, layer_of(layer, width, width)), (norm2_gain, gains),
            (fc_weight, layer_of(layer, width, inner)), (proj_weight, layer_of(layer, inner, width)),
        ]

    def swap_dp(x, step):
        return lax.ppermute(x, ALL, [(spot(d, s), spot(d ^ (1 << orders[d & 1][step]), s)) for d in range(dp) for s in range(seq)])

    def swap_seq(x, step):
        return lax.ppermute(x, ALL, [(spot(d, s), spot(d, s ^ (1 << z_orders[d & 1][step]))) for d in range(dp) for s in range(seq)])

    class Bucket:
        def __init__(self, keep, send):
            self.halves = None
            self.parts = None
            self.steps = self.run(keep, send)
            next(self.steps)

        def run(self, keep, send):
            got = pair(send)
            for step in range(len(dp_bits)):
                yield
                total = add(keep, order.after(got))
                half = total.shape[0] // 2
                keep, send = total[:half], total[half:]
                order.add(keep)
                got = swap_dp(send, step)
            self.parts = [(keep, got)]
            yield
            yield from self.rest()

        def rest(self):
            total = jnp.concatenate([add(keep, order.after(got)) for keep, got in self.parts], axis=1)
            order.add(total)
            for step in range(len(seq_bits)):
                got = swap_seq(total, step)
                yield
                total = add(total, order.after(got))
                order.add(total)
            for step in reversed(range(len(dp_bits))):
                got = swap_dp(total, step)
                yield
                total = jnp.concatenate([total, order.after(got)], axis=0)
                order.add(total)
            self.halves = (total, pair(total))
            yield

        def step(self):
            next(self.steps)

    def bucket_outs(rows):
        count = 2 ** len(dp_bits)
        size = rows // (2 * count)
        assert size * 2 * count == rows
        return [((count, size, width), BF, whole(count, size, width))] * 2, [VMEM((2 * count, size, width), BF)]

    gain_out = ((8, width), F32, whole(8, width))

    kv_other = pair(kv)
    ua, ub = spread(*[order.after(x) for x in grad_pieces])
    p, att, inv = attend(q, kv, kv_other)
    order.last += [ua, ub]
    mid, sec, act, gp, h_next, a_next, q_next, kv_next = call(
        functools.partial(middle_body, scale, 0), "middle",
        feed_ins(0, h, att) + [(norm1_gain, gains), (qkv_weight, layer_of(1, width, 3 * width))],
        [(t_w, F32, full), (t_w, BF, full), ((tokens, inner), BF, wide), ((tokens, inner), BF, wide), (t_w, F32, full)] + qkv_out(),
        flops=dense * (4 * width + 2 * inner), transcendentals=2 * tokens * inner, limit=18, order=order,
    )
    saved = (h, a, q, kv, kv_other, p, att, inv)
    h, a, q, kv = h_next, a_next, q_next, kv_next

    kv_other = pair(kv)
    p, att, inv = attend(q, kv, kv_other)
    outs, scratch = bucket_outs(2 * inner + width)
    oa, ob, keep, send, mg, ag, gain2_1 = call(
        functools.partial(turn_body, 1, bits), "turn",
        [(at, scalars())] + feed_ins(1, h, att) + [(ua, half_spec), (ub, half_spec)],
        [((span, width), BF, half_spec)] * 2 + outs + [(t_w, F32, full), (t_w, BF, full), gain_out],
        scratch=[VMEM(t_w, F32), VMEM(t_w, BF)] + [VMEM((tokens, inner), BF)] * 3 + scratch,
        flops=dense * (3 * width + 6 * inner), transcendentals=2 * tokens * inner, limit=24, order=order,
    )
    feed_1 = Bucket(keep, send)

    def back_attend(first, count, q, kv, kv_other, p, att, inv, ag):
        out = (tokens, count * LANES)
        dq, own, oth = call(
            functools.partial(back_attend_body, scale, first), "back_attend",
            [(q, full), (kv, kv_spec), (kv_other, kv_spec), (p, p_spec), (att, full), (inv, full), (ag, full)],
            [(out, BF, whole(*out)), ((2, *out), F32, whole(2, *out)), ((2, *out), BF, whole(2, *out))],
            flops=8 * tokens * 2 * tokens * 256 * 2 * count, limit=20, order=order,
        )
        return dq, own, pair(oth)

    def part_ins(parts):
        return [(x, whole(*x.shape)) for part in parts for x in part]

    layer_1 = (q, kv, kv_other, p, att, inv)
    h_1, a_1, mg_1, ag_1 = h, a, mg, ag
    h_0, a_0, *layer_0 = saved
    v = {}
    buckets = {"A": feed_1}

    def back_turn():
        outs, scratch = bucket_outs(3 * width + inner)
        keep, send, v["up"], v["gain1_1"], v["lift"] = call(
            functools.partial(back_turn_body, 1, bits), "back_turn",
            [(at, scalars())] + part_ins((v["1a"], v["1b"])) + [
                (a_1, full), (h_1, full), (norm1_gain, gains), (qkv_weight, layer_of(1, width, 3 * width)), (mg_1, full),
                (act, wide), (gp, wide), (proj_weight, layer_of(0, inner, width))],
            outs + [(t_w, F32, full), gain_out, ((tokens, inner), BF, wide)],
            scratch=scratch, flops=dense * (6 * width + 2 * inner), limit=18, order=order,
        )
        buckets["B"] = Bucket(keep, send)

    def back_fc_0():
        outs, scratch = bucket_outs(inner + width)
        keep, send, v["mg"], v["ag"], v["gain2_0"] = call(
            functools.partial(back_fc_body, 0, bits), "back_fc",
            [(at, scalars()), (v["up"], full), (v["lift"], wide), (sec, full), (mid, full), (layer_0[4], full),
             (fc_weight, layer_of(0, width, inner)), (out_weight, layer_of(0, width, width)), (norm2_gain, gains)],
            outs + [(t_w, F32, full), (t_w, BF, full), gain_out],
            scratch=scratch, flops=dense * (2 * width + 2 * inner), limit=16, order=order,
        )
        buckets["C"] = Bucket(keep, send)

    def back_end():
        outs, scratch = bucket_outs(3 * width + GAIN_ROWS * blocks)
        keep, send, ga, gb = call(
            functools.partial(back_end_body, 0, bits), "back_end",
            [(at, scalars())] + part_ins((v["0a"], v["0b"])) + [
                (a_0, full), (h_0, full), (norm1_gain, gains), (qkv_weight, layer_of(0, width, 3 * width)), (v["mg"], full),
                (oa, half_spec), (ob, half_spec)]
            + [(g, whole(8, width)) for g in (v["gain1_1"], v["gain2_0"], gain2_1)],
            outs + [((2, span, width), BF, both_spec)] * 2,
            scratch=scratch, flops=2 * dense * 3 * width, limit=12, order=order,
        )
        buckets["D"] = Bucket(keep, send)
        v["ga"], v["gb"] = ga, gb

    def run_part(name, first, count, layer, ag):
        v[name] = back_attend(first, count, *layer, ag)

    parts_of = {
        "A": [(0, 1, (inner, width), "proj"), (inner, 1, (width, inner), "fc"), (2 * inner, 1, (width, width), "out")],
        "B": [(0, 1, (width, 3 * width), "qkv"), (3 * width, 0, (inner, width), "proj")],
        "C": [(0, 0, (width, inner), "fc"), (inner, 0, (width, width), "out")],
        "D": [(0, 0, (width, 3 * width), "qkv")],
    }

    def unpacked(names):
        last = "D" in names
        groups = [
            (buckets.pop(name).halves, [(row // blocks, layer, shape, v.get(key)) for row, layer, shape, key in parts_of[name]])
            for name in names
        ]
        gain_rows = [[3 * width // blocks + i for i in pair] for pair in ((0, 1), (2, 3))] if last else []
        got = unpack(bits, at, groups, layers, gain_rows, order)
        keys = [part[3] for name in names for part in parts_of[name]]
        v.update(zip(keys, got))
        if last:
            v["gains"] = got[len(keys) : len(keys) + 2]

    def bucket_step(name):
        if name not in buckets:
            return
        if buckets[name].halves is None:
            buckets[name].step()
        elif name == "D":
            while "C" in buckets and buckets["C"].halves is None:
                buckets["C"].step()
            unpacked([n for n in "CD" if n in buckets])
        elif name != "C":
            unpacked([name])

    kernels = {
        "BA1a": lambda: run_part("1a", 0, 1, layer_1, ag_1),
        "BA1b": lambda: run_part("1b", 1, pairs - 1, layer_1, ag_1),
        "BT": back_turn,
        "BF": back_fc_0,
        "BA0a": lambda: run_part("0a", 0, 1, layer_0, v["ag"]),
        "BA0b": lambda: run_part("0b", 1, pairs - 1, layer_0, v["ag"]),
        "BE": back_end,
        "PG": lambda: v.update(home=v["home"].done(order)),
        "SG": lambda: v.update(home=Collect(order.after(v["ga"]), order.after(v["gb"]))),
    }
    for token in SCHEDULE:
        if token in kernels:
            kernels[token]()
        else:
            bucket_step(token)
    while buckets:
        for name in "ABCD":
            bucket_step(name)
    norm1_grad, norm2_grad = v["gains"]
    qkv_grad, out_grad, fc_grad, proj_grad = (
        v[name].reshape(layers, -1, v[name].shape[-1]) for name in ("qkv", "out", "fc", "proj")
    )
    return *v["home"], norm1_grad, qkv_grad, out_grad, norm2_grad, fc_grad, proj_grad


def solution(mesh):
    block = P("dp", "seq", None)
    return jax.shard_map(
        functools.partial(per_device, (mesh.shape["dp"], mesh.shape["seq"])),
        mesh=mesh,
        in_specs=(block, P(), P(), P(), P(), P(), P(), P("dp"), P(), block),
        out_specs=(block, block, P(), P(), P(), P(), P(), P()),
        check_vma=False,
    )
```

```python
import functools
import math

import jax
import jax.numpy as jnp
from jax import lax
from jax.experimental import pallas as pl
from jax.experimental.pallas import tpu as pltpu
from jax.sharding import PartitionSpec as P

HEADS = 6
EPSILON = 1e-05
NEGATIVE = -1e30
BF = jnp.bfloat16
F32 = jnp.float32
ALL = ("dp", "seq")
LANES = 128
GAIN_ROWS = 16
SCHEDULE = (
    "A", "BA1a", "BA1b", "BT", "A", "BF", "B", "A", "BA0a", "BA0b", "C", "A", "B", "BE", "C", "B", "A", "D", "C",
    "B", "D", "A", "C", "D", "B", "A", "C", "D", "SG", "B", "D", "B", "C", "D", "A", "PG", "D", "C", "B", "D",
)
MB = 1024 * 1024
VMEM = pltpu.VMEM
SMEM = pltpu.SMEM


def mm(a, b):
    return lax.dot_general(a, b, (((1,), (0,)), ((), ())), preferred_element_type=F32)


def mm_t(a, b):
    return lax.dot_general(a, b, (((1,), (1,)), ((), ())), preferred_element_type=F32)


def t_mm(a, b):
    return lax.dot_general(a, b, (((0,), (0,)), ((), ())), preferred_element_type=F32)


class Order:
    def __init__(self):
        self.last = []

    def after(self, x):
        x, *last = lax.optimization_barrier((x, *self.last))
        self.last = last[-1:]
        return x

    def add(self, result):
        self.last = [result, *self.last]


def call(body, name, ins, outs, scratch=(), limit=16, flops=0, transcendentals=0, grid=(1,), aliases=None, order=None):
    moved = sum(math.prod(o[0]) * jnp.dtype(o[1]).itemsize for o in outs)
    moved += sum(a.size * a.dtype.itemsize for a, _ in ins)
    kernel = body
    if order is not None:
        count, more = len(ins), len(order.last)
        ins = [*ins, *((x, pl.BlockSpec(memory_space=pl.ANY)) for x in order.last)]
        order.last = []
        results_at = count + more + len(outs)
        outs = [*outs, ((8, LANES), F32, whole(8, LANES))]

        def kernel(*refs):
            body(*refs[:count], *refs[count + more : results_at], *refs[results_at + 1 :])
            refs[results_at][...] = jnp.zeros((8, LANES), F32)

    results = pl.pallas_call(
        kernel,
        out_shape=[pltpu.HBM(o[0], o[1]) if len(o) > 3 else jax.ShapeDtypeStruct(o[0], o[1]) for o in outs],
        grid=grid,
        in_specs=[s for _, s in ins],
        out_specs=[o[2] for o in outs],
        scratch_shapes=list(scratch),
        input_output_aliases=aliases or {},
        compiler_params=pltpu.CompilerParams(vmem_limit_bytes=limit * MB),
        cost_estimate=pl.CostEstimate(flops=flops, bytes_accessed=moved, transcendentals=transcendentals),
        name=name,
    )(*[a for a, _ in ins])
    if order is not None:
        *results, token = results
        order.add(token)
    return results


def whole(*shape):
    return pl.BlockSpec(shape, lambda *_: (0,) * len(shape))


def layer_of(index, *shape):
    return pl.BlockSpec((None,) + shape, lambda *_: (index,) + (0,) * len(shape))


def in_hbm(x):
    return pltpu.with_memory_space_constraint(x, pltpu.HBM), pl.BlockSpec(memory_space=pltpu.HBM)


def scalars():
    return pl.BlockSpec(memory_space=SMEM)


def norm_parts(values):
    centre = jnp.mean(values, axis=-1, keepdims=True)
    centred = values - centre
    spread = jnp.mean(centred * centred, axis=-1, keepdims=True)
    inverse = lax.rsqrt(spread + EPSILON)
    return centred * inverse, inverse


def norm_back(grad, zhat, inverse, gain):
    e = grad * gain
    return inverse * (
        e
        - jnp.mean(e, axis=-1, keepdims=True)
        - zhat * jnp.mean(e * zhat, axis=-1, keepdims=True)
    )


def qkv_step(hidden, gain, weight, a_ref, q_ref, kv_ref, scale):
    zhat, _ = norm_parts(hidden)
    a = (zhat * gain).astype(BF)
    a_ref[...] = a
    packed = mm(a, weight).astype(BF)
    width = a.shape[1]
    q_ref[...] = packed[:, :width] * jnp.asarray(scale, BF)
    kv_ref[...] = packed[:, width:]


def first_body(scale, ha_ref, hb_ref, gain_ref, w_ref, h_ref, a_ref, q_ref, kv_ref):
    span = ha_ref.shape[0]
    h_ref[:span] = ha_ref[...].astype(F32)
    h_ref[span:] = hb_ref[...].astype(F32)
    qkv_step(h_ref[...], gain_ref[0:1], w_ref[...], a_ref, q_ref, kv_ref, scale)


def attend_body(block, info_ref, q_ref, kv_ref, kx_ref, bias_ref, hot_ref, p_ref, att_ref, inv_ref):
    tokens, width = q_ref.shape
    head = LANES // 2
    ones = jnp.ones((tokens, LANES), BF)

    def beside(a, b):
        return jnp.concatenate([a, b], axis=1)

    lower = lax.broadcasted_iota(jnp.int32, (tokens, LANES), 1) < head
    at_q = lax.broadcasted_iota(jnp.int32, (block, block), 0)
    at_k = lax.broadcasted_iota(jnp.int32, (block, block), 1)
    prefix = info_ref[0]

    @pl.loop(0, width // LANES)
    def _(pair):
        cols = pl.ds(pl.multiple_of(pair * LANES, LANES), LANES)
        vcols = pl.ds(pl.multiple_of(width + pair * LANES, LANES), LANES)
        keys = jnp.concatenate([beside(kv_ref[:, cols], bias_ref[:tokens]), beside(kx_ref[:, cols], bias_ref[tokens:])], axis=0)
        values = jnp.concatenate([beside(kv_ref[:, vcols], ones), beside(kx_ref[:, vcols], ones)], axis=0)
        q = q_ref[:, cols]
        scores = []
        for n in range(2):
            qn = jnp.where(lower if n == 0 else ~lower, q, jnp.zeros_like(q))
            scores.append(mm_t(beside(qn, hot_ref[...]), keys))
        chances = []
        for n in range(2):
            rows = []
            for t in range(tokens // block):
                s = scores[n][t * block : (t + 1) * block]
                seen = (at_k <= at_q) | (info_ref[1 + t] * block + at_k < prefix)
                pieces = [s[:, : t * block], jnp.where(seen, s[:, t * block : (t + 1) * block], NEGATIVE), s[:, (t + 1) * block :]]
                s = jnp.concatenate([piece for piece in pieces if piece.shape[1]], axis=1)
                rows.append(jnp.exp(s - jnp.max(s, axis=1, keepdims=True)).astype(BF))
            p = jnp.concatenate(rows, axis=0)
            p_ref[2 * pair + n] = p
            chances.append(p)
        even, odd = [mm(p, values) for p in chances]
        inverse = 1.0 / jnp.where(lower, even[:, LANES:], odd[:, LANES:])
        inv_ref[:, cols] = inverse
        att_ref[:, cols] = (jnp.where(lower, even[:, :LANES], odd[:, :LANES]) * inverse).astype(BF)


def feed(h_ref, att_ref, wout_ref, gain, wfc_ref, wproj_ref, mid_ref, sec_ref, act_ref, gp_ref):
    middle = h_ref[...] + mm(att_ref[...], wout_ref[...])
    mid_ref[...] = middle
    zhat, _ = norm_parts(middle)
    second = (zhat * gain).astype(BF)
    sec_ref[...] = second
    total = middle
    width = middle.shape[1]
    for j in range(wfc_ref.shape[1] // width):
        cols = slice(j * width, (j + 1) * width)
        lifted = mm(second, wfc_ref[:, cols])
        phi = 0.5 * (1.0 + lax.erf(lifted * (1.0 / math.sqrt(2.0))))
        slope = phi + lifted * jnp.exp(-0.5 * lifted * lifted) * (1.0 / math.sqrt(2.0 * math.pi))
        gp_ref[:, cols] = slope.astype(BF)
        act = (lifted * phi).astype(BF)
        act_ref[:, cols] = act
        total = total + mm(act, wproj_ref[cols, :])
    return total


def middle_body(scale, layer, h_ref, att_ref, wout_ref, g2_ref, wfc_ref, wproj_ref, g1_ref, wqkv_ref,
                mid_ref, sec_ref, act_ref, gp_ref, out_ref, a_ref, q_ref, kv_ref):
    out = feed(h_ref, att_ref, wout_ref, g2_ref[layer : layer + 1], wfc_ref, wproj_ref, mid_ref, sec_ref, act_ref, gp_ref)
    out_ref[...] = out
    qkv_step(out, g1_ref[layer + 1 : layer + 2], wqkv_ref[...], a_ref, q_ref, kv_ref, scale)


def relative(bits, index, core):
    place = 0
    for mine, others in bits:
        place = 2 * place + (jnp.where(core == 0, index >> mine, index >> others) & 1)
    return place


def hand_out(bits, at_ref, g_ref, keep_ref, send_ref):
    index = at_ref[0]
    core = index & 1
    count = keep_ref.shape[0]
    for ref, side in ((keep_ref, core), (send_ref, 1 - core)):
        place = relative(bits, index, side)
        for i in range(count):
            ref[i] = g_ref[side * count + (place ^ i)]


def put_rows(g_ref, at, values, first=0, total=None):
    share = (total or values.shape[0]) // g_ref.shape[0]
    done = 0
    while done < values.shape[0]:
        block, row = divmod(first + done, share)
        count = min(share - row, values.shape[0] - done)
        g_ref[block, at + row : at + row + count] = values[done : done + count]
        done += count


def back_proj(upstream, act_ref, gp_ref, wproj_ref, g_ref, at, lift_ref):
    down = upstream.astype(BF)
    width = down.shape[1]
    for j in range(act_ref.shape[1] // width):
        cols = slice(j * width, (j + 1) * width)
        put_rows(g_ref, at, t_mm(act_ref[:, cols], down).astype(BF), j * width, act_ref.shape[1])
        lift_ref[:, cols] = (mm_t(down, wproj_ref[cols, :]) * gp_ref[:, cols].astype(F32)).astype(BF)


def back_fc(upstream, lift_ref, sec_ref, mid_ref, att_ref, wfc_ref, wout_ref, gain, g_ref, at, mg_ref, ag_ref, gain_ref):
    second = sec_ref[...]
    width = second.shape[1]
    inner = lift_ref.shape[1]
    second_grad = None
    for j in range(inner // width):
        cols = slice(j * width, (j + 1) * width)
        lift = lift_ref[:, cols]
        put_rows(g_ref, at + j * width // g_ref.shape[0], t_mm(second, lift).astype(BF))
        term = mm_t(lift, wfc_ref[:, cols])
        second_grad = term if second_grad is None else second_grad + term
    zhat, inverse = norm_parts(mid_ref[...])
    gain_ref[...] = jnp.broadcast_to(jnp.sum(second_grad * zhat, axis=0, keepdims=True), gain_ref.shape)
    mg = upstream + norm_back(second_grad, zhat, inverse, gain)
    mg_ref[...] = mg
    branch = mg.astype(BF)
    put_rows(g_ref, at + inner // g_ref.shape[0], t_mm(att_ref[...], branch).astype(BF))
    ag_ref[...] = mm_t(branch, wout_ref[...]).astype(BF)


def turn_body(layer, bits, core_ref, h_ref, att_ref, wout_ref, g2_ref, wfc_ref, wproj_ref, ua_ref, ub_ref,
              oa_ref, ob_ref, keep_ref, send_ref, mg_ref, ag_ref, gain_ref,
              mid_ref, sec_ref, act_ref, gp_ref, lift_ref, g_ref):
    gain = g2_ref[layer : layer + 1]
    out = feed(h_ref, att_ref, wout_ref, gain, wfc_ref, wproj_ref, mid_ref, sec_ref, act_ref, gp_ref)
    span = oa_ref.shape[0]
    oa_ref[...] = out[:span].astype(BF)
    ob_ref[...] = out[span:].astype(BF)
    upstream = jnp.concatenate([ua_ref[...], ub_ref[...]], axis=0).astype(F32)
    back_proj(upstream, act_ref, gp_ref, wproj_ref, g_ref, 0, lift_ref)
    back_fc(upstream, lift_ref, sec_ref, mid_ref, att_ref, wfc_ref, wout_ref, gain, g_ref, act_ref.shape[1] // g_ref.shape[0],
            mg_ref, ag_ref, gain_ref)
    hand_out(bits, core_ref, g_ref, keep_ref, send_ref)


def back_fc_body(layer, bits, core_ref, u_ref, lift_ref, sec_ref, mid_ref, att_ref, wfc_ref, wout_ref, g2_ref,
                 keep_ref, send_ref, mg_ref, ag_ref, gain_ref, g_ref):
    back_fc(u_ref[...], lift_ref, sec_ref, mid_ref, att_ref, wfc_ref, wout_ref, g2_ref[layer : layer + 1], g_ref, 0,
            mg_ref, ag_ref, gain_ref)
    hand_out(bits, core_ref, g_ref, keep_ref, send_ref)


def back_attend_body(scale, first, q_ref, kv_ref, kx_ref, p_ref, att_ref, inv_ref, ag_ref, dq_ref, own_ref, oth_ref):
    tokens, width = q_ref.shape
    head = LANES // 2
    lower = lax.broadcasted_iota(jnp.int32, (tokens, LANES), 1) < head

    @pl.loop(0, dq_ref.shape[1] // LANES)
    def _(pair):
        out = pl.ds(pl.multiple_of(pair * LANES, LANES), LANES)
        cols = pl.ds(pl.multiple_of((first + pair) * LANES, LANES), LANES)
        vcols = pl.ds(pl.multiple_of(width + (first + pair) * LANES, LANES), LANES)
        q = q_ref[:, cols]
        scaled = ag_ref[:, cols].astype(F32) * inv_ref[:, cols]
        product = scaled * att_ref[:, cols].astype(F32)
        keys = jnp.concatenate([kv_ref[:, cols], kx_ref[:, cols]], axis=0)
        values = jnp.concatenate([kv_ref[:, vcols], kx_ref[:, vcols]], axis=0)
        dq = dk = dv = None
        for n in range(2):
            mine = lower if n == 0 else ~lower
            qn = jnp.where(mine, q, jnp.zeros_like(q))
            gn = jnp.where(mine, scaled, 0.0).astype(BF)
            delta = jnp.sum(jnp.where(mine, product, 0.0), axis=1, keepdims=True)
            p = p_ref[2 * (first + pair) + n]
            ds = (p.astype(F32) * (mm_t(gn, values) - delta)).astype(BF)
            dqn, dkn, dvn = mm(ds, keys), t_mm(qn, ds), t_mm(gn, p)
            if n == 0:
                dq, dk, dv = dqn, dkn, dvn
            else:
                dq, dk, dv = jnp.where(lower, dq, dqn), dk + dkn, dv + dvn
        dq_ref[:, out] = (dq * scale).astype(BF)
        for i, grad in enumerate((dk.T, dv.T)):
            own_ref[i, :, out] = grad[:tokens]
            oth_ref[i, :, out] = grad[tokens:].astype(BF)


def back_qkv(layer, parts, a_ref, h_ref, g1_ref, w_ref, mg_ref, g_ref):
    a = a_ref[...]
    width = a.shape[1]
    blocks = [jnp.concatenate([dq[...] for dq, _, _ in parts], axis=1)]
    for i in range(2):
        blocks.append(jnp.concatenate([(own[i] + got[i].astype(F32)).astype(BF) for _, own, got in parts], axis=1))
    grad = None
    for j, block in enumerate(blocks):
        put_rows(g_ref, j * width // g_ref.shape[0], t_mm(a, block).astype(BF))
        term = mm_t(block, w_ref[:, j * width : (j + 1) * width])
        grad = term if grad is None else grad + term
    zhat, inverse = norm_parts(h_ref[...])
    gain_grad = jnp.sum(grad * zhat, axis=0, keepdims=True)
    return mg_ref[...] + norm_back(grad, zhat, inverse, g1_ref[layer : layer + 1]), gain_grad


def back_turn_body(layer, bits, core_ref, *refs):
    parts, refs = (refs[:3], refs[3:6]), refs[6:]
    (a_ref, h_ref, g1_ref, w_ref, mg_ref, act_ref, gp_ref, wproj_ref,
     keep_ref, send_ref, up_ref, gain_ref, lift_ref, g_ref) = refs
    up, gain_grad = back_qkv(layer, parts, a_ref, h_ref, g1_ref, w_ref, mg_ref, g_ref)
    gain_ref[...] = jnp.broadcast_to(gain_grad, gain_ref.shape)
    up_ref[...] = up
    back_proj(up, act_ref, gp_ref, wproj_ref, g_ref, 3 * up.shape[1] // g_ref.shape[0], lift_ref)
    hand_out(bits, core_ref, g_ref, keep_ref, send_ref)


def back_end_body(layer, bits, core_ref, *refs):
    parts, refs = (refs[:3], refs[3:6]), refs[6:]
    (a_ref, h_ref, g1_ref, w_ref, mg_ref, oa_ref, ob_ref, *gain_refs, keep_ref, send_ref, to_a_ref, to_b_ref, g_ref) = refs
    up, gain_grad = back_qkv(layer, parts, a_ref, h_ref, g1_ref, w_ref, mg_ref, g_ref)
    span = oa_ref.shape[0]
    width = up.shape[1]
    to_a_ref[0] = oa_ref[...]
    to_b_ref[0] = ob_ref[...]
    to_a_ref[1] = up[:span].astype(BF)
    to_b_ref[1] = up[span:].astype(BF)
    at = 3 * width // g_ref.shape[0]
    for i, gain in enumerate([gain_grad] + [ref[0:1] for ref in gain_refs]):
        put_rows(g_ref, at + i, jnp.broadcast_to(gain, (g_ref.shape[0], width)).astype(BF))
    at += 1 + len(gain_refs)
    for block in range(g_ref.shape[0]):
        g_ref[block, at:] = jnp.zeros((g_ref.shape[1] - at, width), BF)
    hand_out(bits, core_ref, g_ref, keep_ref, send_ref)


def masks_body(per_span, block, ids_ref, order_ref, own_ref, other_ref, w_in, g_in, bias_ref, hot_ref, info_ref, w_ref, g_ref, sem):
    copies = [pltpu.make_async_copy(w_in.at[0], w_ref, sem.at[0]), pltpu.make_async_copy(g_in, g_ref, sem.at[1])]
    for copy in copies:
        copy.start()
    core, place = ids_ref[0] & 1, ids_ref[1]
    odd = place & 1
    prefix = jnp.where((place >> 1) == core, own_ref[odd], other_ref[odd])
    info_ref[0] = prefix
    ranks = []
    for c in (core, 1 - core):
        for span in (2 * c + odd, 2 * c + 1 - odd):
            ranks += [order_ref[span * per_span + i] for i in range(per_span)]
    tokens = hot_ref.shape[0]
    own = tokens // block
    lane = lax.broadcasted_iota(jnp.int32, (block, LANES), 1)
    within = lax.broadcasted_iota(jnp.int32, (block, LANES), 0)
    lane_rank = jnp.full((block, LANES), -1, jnp.int32)
    for b in range(own):
        info_ref[1 + b] = ranks[b]
        lane_rank = jnp.where(lane == b, ranks[b], lane_rank)
        hot_ref[b * block : (b + 1) * block] = jnp.where(lane == b, 1.0, 0.0).astype(BF)
    for k, rank in enumerate(ranks):
        unseen = (lane < own) & (rank >= lane_rank) & (lane != k) & (rank * block + within >= prefix)
        bias_ref[k * block : (k + 1) * block] = jnp.where(unseen, NEGATIVE, 0.0).astype(BF)
    for copy in copies:
        copy.wait()


def pick_body(at_ref, x_ref, a_ref, b_ref):
    odd = at_ref[1] & 1
    a_ref[...] = x_ref[odd]
    b_ref[...] = x_ref[1 - odd]


def place_body(odd_ref, a_ref, b_ref, *out_refs):
    odd = odd_ref[1] & 1
    for i, ref in enumerate(out_refs):
        ref[odd] = a_ref[i]
        ref[1 - odd] = b_ref[i]


def add(a, b):
    return (a.astype(F32) + b.astype(F32)).astype(BF)


def unpack_body(plan, gains, bits, groups, befores, at_ref, *refs):
    halves, refs = refs[: 2 * groups], refs[2 * groups + befores :]
    out_refs, refs = refs[: len(plan)], refs[len(plan) :]
    gain_refs, refs = refs[: len(gains)], refs[len(gains) :]
    *stage_refs, sem = refs
    index = at_ref[0]
    core = index & 1
    copies = []
    for group in range(groups):
        a_ref, b_ref = halves[2 * group : 2 * group + 2]
        count, _, width = a_ref.shape
        mine = [(at, layer, out, stage) for (g, at, layer), out, stage in zip(plan, out_refs, stage_refs) if g == group]
        for ref, side in ((a_ref, core), (b_ref, 1 - core)):
            place = relative(bits, index, side)
            for i in range(count):
                block = side * count + (place ^ i)
                for at, layer, out_ref, stage_ref in mine:
                    _, rows, cols = stage_ref.shape
                    for j in range(cols // width):
                        stage_ref[block, :, j * width : (j + 1) * width] = ref[i, at + j * rows : at + (j + 1) * rows].astype(F32)
                    copies.append(pltpu.make_async_copy(stage_ref.at[block], out_ref.at[layer, block], sem.at[len(copies)]))
                    copies[-1].start()
    for rows, ref in zip(gains, gain_refs):
        ref[...] = jnp.concatenate([halves[-2][0, row : row + 1] for row in rows], axis=0).astype(F32)
    for copy in copies:
        copy.wait()


def unpack(bits, at, groups, layers, gains, order):
    ins = [(at, scalars())] + [(x, whole(*x.shape)) for halves, _ in groups for x in halves]
    aliases = {}
    outs, plan = [], []
    count, _, width = groups[0][0][0].shape
    blocks = 2 * count
    scratch = []
    for group, (_, parts) in enumerate(groups):
        for row, layer, shape, before in parts:
            if before is not None:
                aliases[len(ins)] = len(outs)
                ins.append((before, pl.BlockSpec(memory_space=pltpu.HBM)))
            outs.append(((layers, blocks, shape[0] // blocks, shape[1]), F32, pl.BlockSpec(memory_space=pltpu.HBM), True))
            plan.append((group, row, layer))
            scratch.append(VMEM((blocks, shape[0] // blocks, shape[1]), F32))
    outs += [((len(rows), width), F32, whole(len(rows), width)) for rows in gains]
    return call(
        functools.partial(unpack_body, plan, gains, bits, len(groups), len(aliases)), "unpack", ins, outs,
        scratch=[*scratch, pltpu.SemaphoreType.DMA((blocks * len(plan),))], limit=24, aliases=aliases, order=order,
    )


def per_device(mesh_shape, hidden_in, norm1_gain, qkv_weight, out_weight, norm2_gain, fc_weight, proj_weight,
               prefix_len, block_order, grad_out):
    dp, seq = mesh_shape
    rows_here, span, width = hidden_in.shape
    layers = qkv_weight.shape[0]
    inner = fc_weight.shape[2]
    scale = 1.0 / math.sqrt(width // HEADS)
    row_length = span * seq
    block_count = block_order.shape[0]
    block = row_length // block_count
    per_span = span // block
    tokens = 2 * span
    pairs = width // LANES
    assert rows_here == 2 and seq == 4 and dp % 2 == 0 and layers == 2
    di, si = lax.axis_index("dp"), lax.axis_index("seq")
    at = jnp.stack([di, si]).astype(jnp.int32)
    order = Order()

    def spot(d, s):
        return d * seq + s

    perm_a = [(spot(d, s), spot((d & ~1) | (s >> 1), 2 * (d & 1) + (s & 1))) for d in range(dp) for s in range(seq)]
    perm_b = [(spot(d, s), spot((d & ~1) | (s >> 1), 2 * (d & 1) + 1 - (s & 1))) for d in range(dp) for s in range(seq)]
    back_a = [(b, a) for a, b in perm_a]
    back_b = [(b, a) for a, b in perm_b]
    pair_perm = [(spot(d, s), spot(d ^ 1, s)) for d in range(dp) for s in range(seq)]
    t_w = (tokens, width)
    full = whole(*t_w)
    half_spec = whole(span, width)
    both_spec = whole(2, span, width)

    def pair(x):
        return lax.ppermute(x, ALL, pair_perm)

    def pick(x):
        return call(
            pick_body, "pick", [(at, scalars()), (x, both_spec)], [((span, width), BF, half_spec)] * 2, limit=4, order=order
        )

    def spread(first, other):
        return lax.ppermute(first, ALL, perm_a), lax.ppermute(other, ALL, perm_b)

    class Collect:
        def __init__(self, a, b):
            self.a, self.b = lax.ppermute(a, ALL, back_a), lax.ppermute(b, ALL, back_b)

        def done(self, order):
            return call(
                place_body, "place", [(at, scalars()), (self.a, both_spec), (self.b, both_spec)],
                [((2, span, width), BF, both_spec, True)] * 2, limit=8, order=order,
            )

    dp_bits = [i for i in range(1, dp.bit_length() - 1)]
    seq_bits = [i for i in range(seq.bit_length() - 1)]
    orders = (dp_bits, dp_bits[::-1])
    z_orders = (seq_bits, seq_bits[::-1])
    bits = list(zip(*orders))
    blocks = 2 ** (len(dp_bits) + 1)

    own_blocks = tokens // block
    ha, hb = spread(*pick(hidden_in))
    grad_pieces = pick(grad_out)
    prefix_other = pair(prefix_len)
    bias, hot, info, first_weight, first_gain = call(
        functools.partial(masks_body, per_span, block), "masks",
        [(at, scalars()), (block_order, scalars()), (prefix_len, scalars()), (prefix_other, scalars()),
         in_hbm(qkv_weight), in_hbm(norm1_gain)],
        [((2 * tokens, LANES), BF, whole(2 * tokens, LANES)), ((tokens, LANES), BF, whole(tokens, LANES)),
         ((1 + own_blocks,), jnp.int32, scalars()),
         ((width, 3 * width), BF, whole(width, 3 * width)), ((layers, width), F32, whole(layers, width))],
        scratch=[pltpu.SemaphoreType.DMA((2,))], order=order,
    )

    wide = whole(tokens, inner)
    gains = whole(layers, width)
    dense = 2 * tokens * width

    def qkv_out():
        return [(t_w, BF, full), (t_w, BF, full), ((tokens, 2 * width), BF, whole(tokens, 2 * width))]

    h, a, q, kv = call(
        functools.partial(first_body, scale), "first",
        [(ha, half_spec), (hb, half_spec), (first_gain, gains), (first_weight, whole(width, 3 * width))],
        [(t_w, F32, full)] + qkv_out(),
        flops=dense * 3 * width, order=order,
    )
    kv_spec = whole(tokens, 2 * width)
    p_spec = whole(HEADS, tokens, 2 * tokens)

    def attend(q, kv, kv_other):
        return call(
            functools.partial(attend_body, block), "attend",
            [(info, scalars()), (q, full), (kv, kv_spec), (kv_other, kv_spec), (bias, whole(2 * tokens, LANES)), (hot, whole(tokens, LANES))],
            [((HEADS, tokens, 2 * tokens), BF, p_spec), (t_w, BF, full), (t_w, F32, full)],
            flops=4 * tokens * 2 * tokens * 256 * HEADS, transcendentals=HEADS * tokens * 2 * tokens, limit=20, order=order,
        )

    def feed_ins(layer, h, att):
        return [
            (h, full), (att, full), (out_weight, layer_of(layer, width, width)), (norm2_gain, gains),
            (fc_weight, layer_of(layer, width, inner)), (proj_weight, layer_of(layer, inner, width)),
        ]

    def swap_dp(x, step):
        return lax.ppermute(x, ALL, [(spot(d, s), spot(d ^ (1 << orders[d & 1][step]), s)) for d in range(dp) for s in range(seq)])

    def swap_seq(x, step):
        return lax.ppermute(x, ALL, [(spot(d, s), spot(d, s ^ (1 << z_orders[d & 1][step]))) for d in range(dp) for s in range(seq)])

    class Bucket:
        def __init__(self, keep, send):
            self.halves = None
            self.parts = None
            self.steps = self.run(keep, send)
            next(self.steps)

        def run(self, keep, send):
            got = pair(send)
            for step in range(len(dp_bits)):
                yield
                total = add(keep, order.after(got))
                half = total.shape[0] // 2
                keep, send = total[:half], total[half:]
                order.add(keep)
                got = swap_dp(send, step)
            self.parts = [(keep, got)]
            yield
            yield from self.rest()

        def rest(self):
            total = jnp.concatenate([add(keep, order.after(got)) for keep, got in self.parts], axis=1)
            order.add(total)
            for step in range(len(seq_bits)):
                got = swap_seq(total, step)
                yield
                total = add(total, order.after(got))
                order.add(total)
            for step in reversed(range(len(dp_bits))):
                got = swap_dp(total, step)
                yield
                total = jnp.concatenate([total, order.after(got)], axis=0)
                order.add(total)
            self.halves = (total, pair(total))
            yield

        def step(self):
            next(self.steps)

    def bucket_outs(rows):
        count = 2 ** len(dp_bits)
        size = rows // (2 * count)
        assert size * 2 * count == rows
        return [((count, size, width), BF, whole(count, size, width))] * 2, [VMEM((2 * count, size, width), BF)]

    gain_out = ((8, width), F32, whole(8, width))

    kv_other = pair(kv)
    ua, ub = spread(*[order.after(x) for x in grad_pieces])
    p, att, inv = attend(q, kv, kv_other)
    order.last += [ua, ub]
    mid, sec, act, gp, h_next, a_next, q_next, kv_next = call(
        functools.partial(middle_body, scale, 0), "middle",
        feed_ins(0, h, att) + [(norm1_gain, gains), (qkv_weight, layer_of(1, width, 3 * width))],
        [(t_w, F32, full), (t_w, BF, full), ((tokens, inner), BF, wide), ((tokens, inner), BF, wide), (t_w, F32, full)] + qkv_out(),
        flops=dense * (4 * width + 2 * inner), transcendentals=2 * tokens * inner, limit=18, order=order,
    )
    saved = (h, a, q, kv, kv_other, p, att, inv)
    h, a, q, kv = h_next, a_next, q_next, kv_next

    kv_other = pair(kv)
    p, att, inv = attend(q, kv, kv_other)
    outs, scratch = bucket_outs(2 * inner + width)
    oa, ob, keep, send, mg, ag, gain2_1 = call(
        functools.partial(turn_body, 1, bits), "turn",
        [(at, scalars())] + feed_ins(1, h, att) + [(ua, half_spec), (ub, half_spec)],
        [((span, width), BF, half_spec)] * 2 + outs + [(t_w, F32, full), (t_w, BF, full), gain_out],
        scratch=[VMEM(t_w, F32), VMEM(t_w, BF)] + [VMEM((tokens, inner), BF)] * 3 + scratch,
        flops=dense * (3 * width + 6 * inner), transcendentals=2 * tokens * inner, limit=24, order=order,
    )
    feed_1 = Bucket(keep, send)

    def back_attend(first, count, q, kv, kv_other, p, att, inv, ag):
        out = (tokens, count * LANES)
        dq, own, oth = call(
            functools.partial(back_attend_body, scale, first), "back_attend",
            [(q, full), (kv, kv_spec), (kv_other, kv_spec), (p, p_spec), (att, full), (inv, full), (ag, full)],
            [(out, BF, whole(*out)), ((2, *out), F32, whole(2, *out)), ((2, *out), BF, whole(2, *out))],
            flops=8 * tokens * 2 * tokens * 256 * 2 * count, limit=20, order=order,
        )
        return dq, own, pair(oth)

    def part_ins(parts):
        return [(x, whole(*x.shape)) for part in parts for x in part]

    layer_1 = (q, kv, kv_other, p, att, inv)
    h_1, a_1, mg_1, ag_1 = h, a, mg, ag
    h_0, a_0, *layer_0 = saved
    v = {}
    buckets = {"A": feed_1}

    def back_turn():
        outs, scratch = bucket_outs(3 * width + inner)
        keep, send, v["up"], v["gain1_1"], v["lift"] = call(
            functools.partial(back_turn_body, 1, bits), "back_turn",
            [(at, scalars())] + part_ins((v["1a"], v["1b"])) + [
                (a_1, full), (h_1, full), (norm1_gain, gains), (qkv_weight, layer_of(1, width, 3 * width)), (mg_1, full),
                (act, wide), (gp, wide), (proj_weight, layer_of(0, inner, width))],
            outs + [(t_w, F32, full), gain_out, ((tokens, inner), BF, wide)],
            scratch=scratch, flops=dense * (6 * width + 2 * inner), limit=18, order=order,
        )
        buckets["B"] = Bucket(keep, send)

    def back_fc_0():
        outs, scratch = bucket_outs(inner + width)
        keep, send, v["mg"], v["ag"], v["gain2_0"] = call(
            functools.partial(back_fc_body, 0, bits), "back_fc",
            [(at, scalars()), (v["up"], full), (v["lift"], wide), (sec, full), (mid, full), (layer_0[4], full),
             (fc_weight, layer_of(0, width, inner)), (out_weight, layer_of(0, width, width)), (norm2_gain, gains)],
            outs + [(t_w, F32, full), (t_w, BF, full), gain_out],
            scratch=scratch, flops=dense * (2 * width + 2 * inner), limit=16, order=order,
        )
        buckets["C"] = Bucket(keep, send)

    def back_end():
        outs, scratch = bucket_outs(3 * width + GAIN_ROWS * blocks)
        keep, send, ga, gb = call(
            functools.partial(back_end_body, 0, bits), "back_end",
            [(at, scalars())] + part_ins((v["0a"], v["0b"])) + [
                (a_0, full), (h_0, full), (norm1_gain, gains), (qkv_weight, layer_of(0, width, 3 * width)), (v["mg"], full),
                (oa, half_spec), (ob, half_spec)]
            + [(g, whole(8, width)) for g in (v["gain1_1"], v["gain2_0"], gain2_1)],
            outs + [((2, span, width), BF, both_spec)] * 2,
            scratch=scratch, flops=2 * dense * 3 * width, limit=12, order=order,
        )
        buckets["D"] = Bucket(keep, send)
        v["ga"], v["gb"] = ga, gb

    def run_part(name, first, count, layer, ag):
        v[name] = back_attend(first, count, *layer, ag)

    parts_of = {
        "A": [(0, 1, (inner, width), "proj"), (inner, 1, (width, inner), "fc"), (2 * inner, 1, (width, width), "out")],
        "B": [(0, 1, (width, 3 * width), "qkv"), (3 * width, 0, (inner, width), "proj")],
        "C": [(0, 0, (width, inner), "fc"), (inner, 0, (width, width), "out")],
        "D": [(0, 0, (width, 3 * width), "qkv")],
    }

    def unpacked(names):
        last = "D" in names
        groups = [
            (buckets.pop(name).halves, [(row // blocks, layer, shape, v.get(key)) for row, layer, shape, key in parts_of[name]])
            for name in names
        ]
        gain_rows = [[3 * width // blocks + i for i in pair] for pair in ((0, 1), (2, 3))] if last else []
        got = unpack(bits, at, groups, layers, gain_rows, order)
        keys = [part[3] for name in names for part in parts_of[name]]
        v.update(zip(keys, got))
        if last:
            v["gains"] = got[len(keys) : len(keys) + 2]

    def bucket_step(name):
        if name not in buckets:
            return
        if buckets[name].halves is None:
            buckets[name].step()
        elif name == "D":
            while "C" in buckets and buckets["C"].halves is None:
                buckets["C"].step()
            unpacked([n for n in "CD" if n in buckets])
        elif name != "C":
            unpacked([name])

    kernels = {
        "BA1a": lambda: run_part("1a", 0, 1, layer_1, ag_1),
        "BA1b": lambda: run_part("1b", 1, pairs - 1, layer_1, ag_1),
        "BT": back_turn,
        "BF": back_fc_0,
        "BA0a": lambda: run_part("0a", 0, 1, layer_0, v["ag"]),
        "BA0b": lambda: run_part("0b", 1, pairs - 1, layer_0, v["ag"]),
        "BE": back_end,
        "PG": lambda: v.update(home=v["home"].done(order)),
        "SG": lambda: v.update(home=Collect(order.after(v["ga"]), order.after(v["gb"]))),
    }
    for token in SCHEDULE:
        if token in kernels:
            kernels[token]()
        else:
            bucket_step(token)
    while buckets:
        for name in "ABCD":
            bucket_step(name)
    norm1_grad, norm2_grad = v["gains"]
    qkv_grad, out_grad, fc_grad, proj_grad = (
        v[name].reshape(layers, -1, v[name].shape[-1]) for name in ("qkv", "out", "fc", "proj")
    )
    return *v["home"], norm1_grad, qkv_grad, out_grad, norm2_grad, fc_grad, proj_grad


def solution(mesh):
    block = P("dp", "seq", None)
    return jax.shard_map(
        functools.partial(per_device, (mesh.shape["dp"], mesh.shape["seq"])),
        mesh=mesh,
        in_specs=(block, P(), P(), P(), P(), P(), P(), P("dp"), P(), block),
        out_specs=(block, block, P(), P(), P(), P(), P(), P()),
        check_vma=False,
    )
```
